32 devices in a mesh: mesh: 16 (over z, y, x), col: 2 (over core).
Axes of the slice: x: 2, y: 2, z: 4, core: 2. Of those that a mesh axis runs over, the one named last changes fastest.
Arguments:
- basis: bfloat16 [49152, 512], P(('mesh', 'col')), may hold values from -6 to 6
- jac_blocks: bfloat16 [768, 8, 64, 64], P(('mesh', 'col')), may hold values from -0.25 to 0.25
- block_cols: int32 [768, 8], P(('mesh', 'col')), may hold values from 0 to 767, as said below
- live_slots: int32 [768], P(('mesh', 'col')), may hold values from 1 to 8
- accumulation: float32 [49152], P(('mesh', 'col')), may hold values from 0.5 to 4
Outputs:
- image: bfloat16 [49152, 512], P(('mesh', 'col'))
- projected: float32 [512, 512], P('mesh', 'col')
The draws below stay inside these ranges and needn't reach their ends.
Inputs may be any that keep to these rules, and one draw needn't show every extreme that they name: `block_cols`: each block row's column blocks lie within 2 block rows of it, and some lie exactly 2 away on either side.
All inputs are finite; a program needn't handle non-finite values.
Results may differ from the reference program's by a relative error of at most 0.003.
Values may be sent and summed in bfloat16 or wider, within the bound.
No kernel may reach another device: no remote copies, remote signals or barrier semaphores. Data moves between devices by JAX's collectives and lax.ppermute only.
A program may use at most 64 MiB of HBM per device.

```python
import math
import jax
import jax.numpy as jnp
from jax import lax

BS = 64
K = 512
SLOTS = 8
REACH = 2
RD = 24
NBLOCKS = 768
NROWS = 49152


def draw_block_cols(key, part):
    offsets = jax.random.randint(key, (NBLOCKS, SLOTS), -REACH, REACH + 1)
    rowids = jnp.arange(NBLOCKS, dtype=jnp.int32)[:, None]
    return jnp.clip(rowids + offsets, 0, NBLOCKS - 1).astype(jnp.int32)


def touch_ends(array, own_key, smallest, largest):
    place = [jax.random.randint(jax.random.fold_in(own_key, axis), (), 0, length) for axis, length in enumerate(array.shape)]
    main_axis = array.shape.index(max(array.shape))
    neighbour = place[:main_axis] + [(place[main_axis] + 1) % array.shape[main_axis]] + place[main_axis + 1:]
    return array.at[tuple(place)].set(smallest).at[tuple(neighbour)].set(largest)


def raised(values, own_key, source, target, blocks, factor):
    def block_of(dim):
        return (jnp.arange(values.shape[dim]) // (values.shape[dim] // blocks)).reshape((-1,) + (1,) * (values.ndim - 1 - dim))

    first = jax.random.permutation(own_key, blocks)[block_of(target)]
    far = (block_of(target) + blocks // 2) % blocks
    return jnp.where((block_of(source) == first) | (block_of(source) == far), factor * values, values)


def shard_levels(key, extent, shards, least, high):
    loudness, own = 1.0, jax.random.fold_in(key, 6)
    for axis_at, shards_of in shards:
        heights = jnp.exp(jax.random.uniform(jax.random.fold_in(own, axis_at), (shards_of,), jnp.float32, least / len(shards), high / len(shards)))
        loudness = loudness * jnp.repeat(heights, extent[axis_at] // shards_of).reshape([-1 if axis == axis_at else 1 for axis in range(len(extent))])
    return loudness


def normal_values(rng, dims, scale, limit, shards=(), kind=jnp.bfloat16):
    gain = shard_levels(rng, dims, shards, -0.22, 0.18) if shards else 1.0
    values = jax.random.normal(rng, dims, jnp.float32) * scale * gain
    return jnp.minimum(jnp.maximum(values, -limit), limit).astype(kind)


def heavy_noise(key, shape, scale, bound, cuts, heavy, kind=jnp.bfloat16):
    result = scale * jax.random.normal(key, shape, jnp.float32)
    if cuts:
        result = result * shard_levels(key, shape, cuts, -0.22, 0.18)
    return jnp.clip(raised(result, jax.random.fold_in(key, 3), *heavy), -bound, bound).astype(kind)


def setup_inputs(seed: int = 0) -> dict:
    key_list = jax.random.split(jax.random.key(seed), 6)
    return {
        "basis": heavy_noise(key_list[0], (NROWS, K), 1.0, 6.0, ((0, 32),), (0, 1, 32, 2.75)),
        "jac_blocks": normal_values(key_list[1], (NBLOCKS, SLOTS, BS, BS), (BS * SLOTS) ** -0.5, 0.25, ((0, 32),)),
        "block_cols": draw_block_cols(jax.random.fold_in(key_list[5], 71), 0),
        "live_slots": touch_ends(jax.random.randint(key_list[3], (NBLOCKS,), 1, SLOTS + 1), jax.random.fold_in(key_list[3], 1), 1, SLOTS).astype(jnp.int32),
        "accumulation": jnp.clip(jnp.exp(math.log(4.0) - 2.0794415 * jax.random.uniform(key_list[4], (NROWS,), jnp.float32) ** shard_levels(key_list[4], (NROWS,), ((0, 32),), -0.2, 0.2)), 0.5, 4.0),
    }


def reference(basis, jac_blocks, block_cols, live_slots, accumulation):
    nblk = jac_blocks.shape[0]
    width = basis.shape[1]
    vblocks = basis.reshape(nblk, BS, width)
    groups = nblk // RD

    def one_group(args):
        jac, cols, live = args
        picked = vblocks[cols].astype(jnp.float32)
        keep = (jnp.arange(SLOTS, dtype=jnp.int32)[None, :] < live[:, None]).astype(jnp.float32)
        masked = jac.astype(jnp.float32) * keep[:, :, None, None]
        return jnp.einsum('rsab,rsbk->rak', masked, picked)

    coupled = lax.map(one_group, (jac_blocks.reshape(groups, RD, SLOTS, BS, BS), block_cols.reshape(groups, RD, SLOTS), live_slots.reshape(groups, RD)))
    coupled = coupled.reshape(nblk * BS, width)
    image = (coupled + accumulation[:, None] * basis.astype(jnp.float32)).astype(jnp.bfloat16)
    projected = jnp.dot(basis.T, image, preferred_element_type=jnp.float32) * (1.0 / NROWS)
    return image, projected
```

```python
import jax
import jax.numpy as jnp
from jax import lax
from jax.sharding import PartitionSpec as P

REACH = 2
AXES = ("mesh", "col")


def with_halo(block, sides, width):
    for axis, dim in sides:
        count = lax.axis_size(axis)
        forward = [(i, i + 1) for i in range(count - 1)]
        backward = [(target, source) for source, target in forward]
        low = lax.ppermute(
            lax.slice_in_dim(block, block.shape[dim] - width, None, axis=dim), axis, forward
        )
        high = lax.ppermute(lax.slice_in_dim(block, 0, width, axis=dim), axis, backward)
        block = jnp.concatenate([low, block, high], axis=dim)
    return block


def local(basis, jac_blocks, block_cols, live_slots, accumulation):
    nrows, width = basis.shape
    nblk, slots, bsize, _ = jac_blocks.shape
    padded = with_halo(basis, ((AXES, 0),), REACH * bsize)
    first = lax.axis_index(AXES) * nblk
    local_cols = block_cols - first + REACH
    pblocks = padded.reshape(nblk + 2 * REACH, bsize, width)
    picked = pblocks[local_cols]
    keep = lax.broadcasted_iota(jnp.int32, (nblk, slots), 1) < live_slots[:, None]
    masked = jnp.where(keep[:, :, None, None], jac_blocks, jnp.zeros_like(jac_blocks))
    coupled = jnp.einsum("rsab,rsbk->rak", masked, picked, preferred_element_type=jnp.float32)
    coupled = coupled.reshape(nrows, width)
    image = (coupled + accumulation[:, None] * basis.astype(jnp.float32)).astype(jnp.bfloat16)
    mesh_count = lax.axis_size("mesh")
    col_count = lax.axis_size("col")
    total_rows = nrows * mesh_count * col_count
    dims = (((0,), (0,)), ((), ()))
    part = lax.dot_general(basis, image, dims, preferred_element_type=jnp.float32)
    part = part.astype(jnp.bfloat16)
    part = part.reshape(mesh_count, width // mesh_count, col_count, width // col_count)
    part = part.transpose(0, 2, 1, 3).reshape(
        mesh_count * col_count, width // mesh_count, width // col_count
    )
    got = lax.all_to_all(part, AXES, 0, 0, tiled=True)
    projected = jnp.sum(got.astype(jnp.float32), axis=0) * (1.0 / total_rows)
    return (image, projected)


def solution(mesh):
    return jax.shard_map(
        local,
        mesh=mesh,
        in_specs=(
            P(AXES, None),
            P(AXES, None, None, None),
            P(AXES, None),
            P(AXES),
            P(AXES),
        ),
        out_specs=(P(AXES, None), P("mesh", "col")),
        check_vma=False,
    )
```

```python
import jax
import jax.numpy as jnp
from jax import lax
from jax.sharding import PartitionSpec as P

REACH = 2
AXES = ("outer", "inner", "col")


def with_halo(block, sides, width):
    for axis, dim in sides:
        count = lax.axis_size(axis)
        forward = [(i, i + 1) for i in range(count - 1)]
        backward = [(target, source) for source, target in forward]
        low = lax.ppermute(
            lax.slice_in_dim(block, block.shape[dim] - width, None, axis=dim), axis, forward
        )
        high = lax.ppermute(lax.slice_in_dim(block, 0, width, axis=dim), axis, backward)
        block = jnp.concatenate([low, block, high], axis=dim)
    return block


def local(basis, jac_blocks, block_cols, live_slots, accumulation):
    nrows, width = basis.shape
    nblk, slots, bsize, _ = jac_blocks.shape
    padded = with_halo(basis, ((AXES, 0),), REACH * bsize)
    first = lax.axis_index(AXES) * nblk
    local_cols = block_cols - first + REACH
    pblocks = padded.reshape(nblk + 2 * REACH, bsize, width)
    picked = pblocks[local_cols]
    keep = lax.broadcasted_iota(jnp.int32, (nblk, slots), 1) < live_slots[:, None]
    masked = jnp.where(keep[:, :, None, None], jac_blocks, jnp.zeros_like(jac_blocks))
    coupled = jnp.einsum("rsab,rsbk->rak", masked, picked, preferred_element_type=jnp.float32)
    coupled = coupled.reshape(nrows, width)
    image = (coupled + accumulation[:, None] * basis.astype(jnp.float32)).astype(jnp.bfloat16)
    outer, inner, cols = (lax.axis_size(axis) for axis in AXES)
    total_rows = nrows * outer * inner * cols
    dims = (((0,), (0,)), ((), ()))
    part = lax.dot_general(basis, image, dims, preferred_element_type=jnp.float32)
    part = part.astype(jnp.bfloat16)
    part = part.reshape(outer, inner, width // (outer * inner), cols, width // cols)
    part = part.transpose(1, 3, 0, 2, 4).reshape(
        inner * cols, width // inner, width // cols
    )
    got = lax.all_to_all(part, AXES[1:], 0, 0, tiled=True)
    near = jnp.sum(got.astype(jnp.float32), axis=0).astype(jnp.bfloat16)
    near = near.reshape(outer, width // (outer * inner), width // cols)
    got = lax.all_to_all(near, AXES[0], 0, 0, tiled=True)
    projected = jnp.sum(got.astype(jnp.float32), axis=0) * (1.0 / total_rows)
    return (image, projected)


def solution(mesh):
    rows, cols = mesh.devices.shape
    outer = 4 if rows % 4 == 0 else 1
    split = jax.sharding.Mesh(mesh.devices.reshape(outer, rows // outer, cols), AXES)
    return jax.shard_map(
        local,
        mesh=split,
        in_specs=(
            P(AXES, None),
            P(AXES, None, None, None),
            P(AXES, None),
            P(AXES),
            P(AXES),
        ),
        out_specs=(P(AXES, None), P(AXES[:2], "col")),
        check_vma=False,
    )
```

```python
import functools

import jax
import jax.numpy as jnp
from jax import lax
from jax.experimental import pallas as pl
from jax.experimental.pallas import tpu as pltpu
from jax.sharding import PartitionSpec as P

REACH = 2
AXES = ("mesh", "col")
ROWS_DOT = (((0,), (0,)), ((), ()))


def strip_of(cols_ref, live_ref, jac_ref, acc_ref, first, pair):
    _, slots, bsize, _ = jac_ref.shape
    tile = 2 * bsize
    half = lax.broadcasted_iota(jnp.int32, (1, tile), 1) // bsize
    halves = []
    for g in (2 * pair, 2 * pair + 1):
        tiles = [None, None, None]
        for s in range(slots):
            place = cols_ref[s, g] - (first + 2 * pair) + REACH
            place = jnp.where(s < live_ref[g], place, -1)
            block = jac_ref[g, s].astype(jnp.float32)
            wide = jnp.concatenate([block, block], axis=1)
            for t in range(3):
                here = jnp.where(half + 2 * t == place, 1.0, 0.0)
                term = wide * here
                tiles[t] = term if tiles[t] is None else tiles[t] + term
        halves.append(jnp.concatenate(tiles, axis=1))
    strip = jnp.concatenate(halves, axis=0)
    row = lax.broadcasted_iota(jnp.int32, strip.shape, 0)
    lane = lax.broadcasted_iota(jnp.int32, strip.shape, 1)
    weight = acc_ref[pl.ds(pair, 1), :]
    weight = jnp.concatenate([weight, weight, weight], axis=1)
    strip = strip + jnp.where(lane == row + tile, weight, 0.0)
    high = strip.astype(jnp.bfloat16)
    low = (strip - high.astype(jnp.float32)).astype(jnp.bfloat16)
    return jnp.concatenate([high, low], axis=0)


def apply_strip(strip, rows):
    both = jnp.dot(strip, rows, preferred_element_type=jnp.float32)
    half = strip.shape[0] // 2
    return both[:half] + both[half:]


def inner_kernel(
    cols_ref, live_ref, jac_ref, basis_ref, acc_ref,
    image_ref, edge_ref, arm_ref, part_ref, staged, sems,
):
    nblk, _, bsize, _ = jac_ref.shape
    nrows = basis_ref.shape[0]
    tile = 2 * bsize
    pairs = nblk // 2
    first = lax.axis_index(AXES) * nblk
    copies = []
    for pair in range(pairs):
        strip = strip_of(cols_ref, live_ref, jac_ref, acc_ref, first, pair)
        start = pair * tile
        if pair == 0:
            edge_ref[0] = apply_strip(strip[:, tile:], basis_ref[: 2 * tile, :])
            arm_ref[0] = strip[:, :tile]
        elif pair == pairs - 1:
            edge_ref[1] = apply_strip(strip[:, : 2 * tile], basis_ref[nrows - 2 * tile :, :])
            arm_ref[1] = strip[:, 2 * tile :]
        else:
            rows = basis_ref[start - tile : start + 2 * tile, :]
            staged[start : start + tile, :] = apply_strip(strip, rows).astype(jnp.bfloat16)
            where = pl.ds(start, tile)
            copy = pltpu.make_async_copy(staged.at[where], image_ref.at[where], sems.at[pair])
            copy.start()
            copies.append(copy)
    part_ref[...] = lax.dot_general(
        basis_ref[tile : nrows - tile, :], staged[tile : nrows - tile, :], ROWS_DOT,
        preferred_element_type=jnp.float32,
    )
    for copy in copies:
        copy.wait()


def edge_kernel(
    chunks, near_ref, far_ref, edge_ref, arm_ref, top_ref, bottom_ref, part_ref, _,
    image_ref, total_ref, staged, sems,
):
    tile, width = top_ref.shape
    nrows = image_ref.shape[0]
    odd = lax.rem(lax.axis_index(AXES), 2) == 1
    near, far = near_ref[...], far_ref[...]
    halos = (jnp.where(odd, near, far), jnp.where(odd, far, near))
    total = part_ref[...]
    copies = []
    for side, own_ref in enumerate((top_ref, bottom_ref)):
        rows = edge_ref[side] + apply_strip(arm_ref[side], halos[side])
        rows = rows.astype(jnp.bfloat16)
        staged[side] = rows
        where = pl.ds(0 if side == 0 else nrows - tile, tile)
        copy = pltpu.make_async_copy(staged.at[side], image_ref.at[where], sems.at[side])
        copy.start()
        copies.append(copy)
        total = total + lax.dot_general(
            own_ref[...], rows, ROWS_DOT, preferred_element_type=jnp.float32
        )
    total = total.astype(jnp.bfloat16)
    if chunks is None:
        total_ref[...] = total
    else:
        down, across = chunks
        high, wide = width // down, width // across
        for i in range(down):
            for j in range(across):
                total_ref[i * across + j] = total[
                    i * high : (i + 1) * high, j * wide : (j + 1) * wide
                ]
    for copy in copies:
        copy.wait()


def whole(memory_space=pltpu.VMEM):
    return pl.BlockSpec(memory_space=memory_space)


def local(basis, jac_blocks, block_cols, live_slots, accumulation):
    nrows, width = basis.shape
    nblk, slots, bsize, _ = jac_blocks.shape
    tile = 2 * bsize
    down, across = (lax.axis_size(axis) for axis in AXES)
    count = down * across
    odd = lax.rem(lax.axis_index(AXES), 2)

    last = nrows - tile
    far_send = lax.dynamic_slice_in_dim(basis, odd * last, tile, axis=0)
    near_send = lax.dynamic_slice_in_dim(basis, (1 - odd) * last, tile, axis=0)
    swaps = [(i, i + 1) for i in range(1, count - 1, 2)]
    far = lax.ppermute(far_send, AXES, swaps + [(j, i) for i, j in swaps])
    swaps = [(i, i + 1) for i in range(0, count, 2)]
    near = lax.ppermute(near_send, AXES, swaps + [(j, i) for i, j in swaps])

    f32, bf16 = jnp.float32, jnp.bfloat16
    image, edge, arm, part = pl.pallas_call(
        inner_kernel,
        out_shape=(
            jax.ShapeDtypeStruct((nrows, width), bf16),
            jax.ShapeDtypeStruct((2, tile, width), f32),
            jax.ShapeDtypeStruct((2, 2 * tile, tile), bf16),
            jax.ShapeDtypeStruct((width, width), f32),
        ),
        in_specs=[whole(pltpu.SMEM), whole(pltpu.SMEM), whole(), whole(), whole()],
        out_specs=(whole(pl.ANY), whole(), whole(), whole()),
        scratch_shapes=[
            pltpu.VMEM((nrows, width), bf16),
            pltpu.SemaphoreType.DMA((nblk // 2,)),
        ],
        compiler_params=pltpu.CompilerParams(vmem_limit_bytes=32 * 2**20),
        cost_estimate=pl.CostEstimate(
            flops=2 * nrows * width * (width + 12 * bsize),
            bytes_accessed=8 * 2**20,
            transcendentals=0,
        ),
        name="inner",
    )(
        block_cols.T,
        live_slots,
        jac_blocks,
        basis,
        accumulation.reshape(nblk // 2, tile),
    )

    in_kernel = (width // down) % 16 == 0 and (width // across) % 128 == 0
    chunk = (count, width // down, width // across)
    image, total = pl.pallas_call(
        functools.partial(edge_kernel, (down, across) if in_kernel else None),
        out_shape=(
            jax.ShapeDtypeStruct((nrows, width), bf16),
            jax.ShapeDtypeStruct(chunk if in_kernel else (width, width), bf16),
        ),
        grid=(1,),
        in_specs=[
            whole(), whole(), whole(), whole(),
            pl.BlockSpec((tile, width), lambda i: (0, 0)),
            pl.BlockSpec((tile, width), lambda i: (nrows // tile - 1, 0)),
            whole(), whole(pl.ANY),
        ],
        out_specs=(whole(pl.ANY), whole()),
        scratch_shapes=[
            pltpu.VMEM((2, tile, width), bf16),
            pltpu.SemaphoreType.DMA((2,)),
        ],
        input_output_aliases={7: 0},
        compiler_params=pltpu.CompilerParams(vmem_limit_bytes=32 * 2**20),
        name="edges",
    )(near, far, edge, arm, basis, basis, part, image)
    if not in_kernel:
        total = total.reshape(down, width // down, across, width // across)
        total = total.transpose(0, 2, 1, 3).reshape(chunk)
    got = lax.all_to_all(total, AXES, 0, 0, tiled=True)
    projected = jnp.sum(got.astype(f32), axis=0) * (1.0 / (nrows * count))
    return (image, projected)


def solution(mesh):
    return jax.shard_map(
        local,
        mesh=mesh,
        in_specs=(
            P(AXES, None),
            P(AXES, None, None, None),
            P(AXES, None),
            P(AXES),
            P(AXES),
        ),
        out_specs=(P(AXES, None), P("mesh", "col")),
        check_vma=False,
    )
```

```python
import functools

import jax
import jax.numpy as jnp
from jax import lax
from jax.experimental import pallas as pl
from jax.experimental.pallas import tpu as pltpu
from jax.sharding import PartitionSpec as P

REACH = 2
AXES = ("mesh", "col")
ROWS_DOT = (((0,), (0,)), ((), ()))


def strip_of(cols_ref, live_ref, jac_ref, acc_ref, first, pair):
    _, slots, bsize, _ = jac_ref.shape
    tile = 2 * bsize
    half = lax.broadcasted_iota(jnp.int32, (1, tile), 1) // bsize
    row = lax.broadcasted_iota(jnp.int32, (bsize, tile), 0)
    lane = lax.broadcasted_iota(jnp.int32, (bsize, tile), 1)
    weight = acc_ref[pair : pair + 1, :]
    halves = []
    for side in range(2):
        g = 2 * pair + side
        tiles = [None, jnp.where(lane == row + side * bsize, weight, 0.0), None]
        for s in range(slots):
            place = cols_ref[s, g] - (first + 2 * pair) + REACH
            place = jnp.where(s < live_ref[g], place, -1)
            block = jac_ref[g, s]
            wide = jnp.concatenate([block, block], axis=1).astype(jnp.float32)
            for t in range(3):
                here = jnp.where(half + 2 * t == place, 1.0, 0.0)
                term = wide * here
                tiles[t] = term if tiles[t] is None else tiles[t] + term
        halves.append(jnp.concatenate(tiles, axis=1))
    strip = jnp.concatenate(halves, axis=0)
    high = strip.astype(jnp.bfloat16)
    low = (strip - high.astype(jnp.float32)).astype(jnp.bfloat16)
    return jnp.concatenate([high, low], axis=0)


def apply_strip(strip, rows):
    both = jnp.dot(strip, rows, preferred_element_type=jnp.float32)
    half = strip.shape[0] // 2
    return both[:half] + both[half:]


def inner_kernel(
    cols_hbm, live_hbm, jac_hbm, basis_hbm, acc_hbm,
    image_ref, edge_ref, arm_ref, part_ref,
    cols_ref, live_ref, jac_ref, basis_ref, acc_ref, strips, staged, load_sems, store_sems,
):
    nblk, _, bsize, _ = jac_ref.shape
    nrows = basis_ref.shape[0]
    tile = 2 * bsize
    pairs = nblk // 2
    groups = 3 if pairs % 3 == 0 else 1
    size = pairs // groups
    first = lax.axis_index(AXES) * nblk

    def load(source, target, at):
        copy = pltpu.make_async_copy(source, target, load_sems.at[at])
        copy.start()
        return copy

    small = [
        load(cols_hbm, cols_ref, 0),
        load(live_hbm, live_ref, 1),
        load(acc_hbm, acc_ref, 2),
    ]
    blocks = []
    for i in range(groups):
        where = pl.ds(2 * size * i, 2 * size)
        blocks.append(load(jac_hbm.at[where], jac_ref.at[where], 4 + i))
        if i == 0:
            rows = load(basis_hbm, basis_ref, 3)

    def build(pair):
        if pair % size == 0:
            blocks[pair // size].wait()
        strips[pair % 2] = strip_of(cols_ref, live_ref, jac_ref, acc_ref, first, pair)

    def project(start, stop):
        return lax.dot_general(
            basis_ref[start:stop, :], staged[start:stop, :], ROWS_DOT,
            preferred_element_type=jnp.float32,
        )

    def store(start, stop, at):
        where = pl.ds(start, stop - start)
        copy = pltpu.make_async_copy(staged.at[where], image_ref.at[where], store_sems.at[at])
        copy.start()
        return copy

    for copy in small:
        copy.wait()
    build(0)
    rows.wait()
    middle = (pairs // 2) * tile
    for pair in range(pairs):
        if pair + 1 < pairs:
            build(pair + 1)
        strip = strips[pair % 2]
        start = pair * tile
        if pair == 0:
            edge_ref[0] = apply_strip(strip[:, tile:], basis_ref[: 2 * tile, :])
            arm_ref[0] = strip[:, :tile]
        elif pair == pairs - 1:
            edge_ref[1] = apply_strip(strip[:, : 2 * tile], basis_ref[nrows - 2 * tile :, :])
            arm_ref[1] = strip[:, 2 * tile :]
        else:
            block = basis_ref[start - tile : start + 2 * tile, :]
            staged[start : start + tile, :] = apply_strip(strip, block).astype(jnp.bfloat16)
        if start + tile == middle:
            early = store(tile, middle, 0)
            part_ref[...] = project(tile, middle)
    late = store(middle, nrows - tile, 1)
    part_ref[...] += project(middle, nrows - tile)
    early.wait()
    late.wait()


def edge_kernel(
    chunks, near_ref, far_ref, edge_ref, arm_ref, top_ref, bottom_ref, part_ref, _,
    image_ref, total_ref, staged, sems,
):
    tile, width = top_ref.shape
    nrows = image_ref.shape[0]
    odd = lax.rem(lax.axis_index(AXES), 2) == 1
    near, far = near_ref[...], far_ref[...]
    halos = (jnp.where(odd, near, far), jnp.where(odd, far, near))
    total = part_ref[...]
    copies = []
    for side, own_ref in enumerate((top_ref, bottom_ref)):
        rows = edge_ref[side] + apply_strip(arm_ref[side], halos[side])
        rows = rows.astype(jnp.bfloat16)
        staged[side] = rows
        where = pl.ds(0 if side == 0 else nrows - tile, tile)
        copy = pltpu.make_async_copy(staged.at[side], image_ref.at[where], sems.at[side])
        copy.start()
        copies.append(copy)
        total = total + lax.dot_general(
            own_ref[...], rows, ROWS_DOT, preferred_element_type=jnp.float32
        )
    total = total.astype(jnp.bfloat16)
    if chunks is None:
        total_ref[...] = total
    else:
        down, across = chunks
        high, wide = width // down, width // across
        for i in range(down):
            for j in range(across):
                total_ref[i * across + j] = total[
                    i * high : (i + 1) * high, j * wide : (j + 1) * wide
                ]
    for copy in copies:
        copy.wait()


def whole(memory_space=pltpu.VMEM):
    return pl.BlockSpec(memory_space=memory_space)


def local(basis, jac_blocks, block_cols, live_slots, accumulation):
    nrows, width = basis.shape
    nblk, slots, bsize, _ = jac_blocks.shape
    tile = 2 * bsize
    down, across = (lax.axis_size(axis) for axis in AXES)
    count = down * across
    odd = lax.rem(lax.axis_index(AXES), 2)

    last = nrows - tile
    far_send = lax.dynamic_slice_in_dim(basis, odd * last, tile, axis=0)
    near_send = lax.dynamic_slice_in_dim(basis, (1 - odd) * last, tile, axis=0)
    swaps = [(i, i + 1) for i in range(1, count - 1, 2)]
    far = lax.ppermute(far_send, AXES, swaps + [(j, i) for i, j in swaps])
    swaps = [(i, i + 1) for i in range(0, count, 2)]
    near = lax.ppermute(near_send, AXES, swaps + [(j, i) for i, j in swaps])

    f32, bf16 = jnp.float32, jnp.bfloat16
    image, edge, arm, part = pl.pallas_call(
        inner_kernel,
        out_shape=(
            jax.ShapeDtypeStruct((nrows, width), bf16),
            jax.ShapeDtypeStruct((2, tile, width), f32),
            jax.ShapeDtypeStruct((2, 2 * tile, tile), bf16),
            jax.ShapeDtypeStruct((width, width), f32),
        ),
        in_specs=[whole(pltpu.HBM)] * 5,
        out_specs=(whole(pltpu.HBM), whole(), whole(), whole()),
        scratch_shapes=[
            pltpu.SMEM((slots, nblk), jnp.int32),
            pltpu.SMEM((nblk,), jnp.int32),
            pltpu.VMEM(jac_blocks.shape, bf16),
            pltpu.VMEM((nrows, width), bf16),
            pltpu.VMEM((nblk // 2, tile), f32),
            pltpu.VMEM((2, 2 * tile, 3 * tile), bf16),
            pltpu.VMEM((nrows, width), bf16),
            pltpu.SemaphoreType.DMA((7,)),
            pltpu.SemaphoreType.DMA((2,)),
        ],
        compiler_params=pltpu.CompilerParams(vmem_limit_bytes=32 * 2**20),
        cost_estimate=pl.CostEstimate(
            flops=2 * nrows * width * (width + 12 * bsize),
            bytes_accessed=8 * 2**20,
            transcendentals=0,
        ),
        name="inner",
    )(
        *(
            pltpu.with_memory_space_constraint(array, pltpu.HBM)
            for array in (
                block_cols.T,
                live_slots,
                jac_blocks,
                basis,
                accumulation.reshape(nblk // 2, tile),
            )
        )
    )

    in_kernel = (width // down) % 16 == 0 and (width // across) % 128 == 0
    chunk = (count, width // down, width // across)
    image, total = pl.pallas_call(
        functools.partial(edge_kernel, (down, across) if in_kernel else None),
        out_shape=(
            jax.ShapeDtypeStruct((nrows, width), bf16),
            jax.ShapeDtypeStruct(chunk if in_kernel else (width, width), bf16),
        ),
        grid=(1,),
        in_specs=[
            whole(), whole(), whole(), whole(),
            pl.BlockSpec((tile, width), lambda i: (0, 0)),
            pl.BlockSpec((tile, width), lambda i: (nrows // tile - 1, 0)),
            whole(), whole(pl.ANY),
        ],
        out_specs=(whole(pl.ANY), whole()),
        scratch_shapes=[
            pltpu.VMEM((2, tile, width), bf16),
            pltpu.SemaphoreType.DMA((2,)),
        ],
        input_output_aliases={7: 0},
        compiler_params=pltpu.CompilerParams(vmem_limit_bytes=32 * 2**20),
        name="edges",
    )(near, far, edge, arm, basis, basis, part, image)
    if not in_kernel:
        total = total.reshape(down, width // down, across, width // across)
        total = total.transpose(0, 2, 1, 3).reshape(chunk)
    got = lax.all_to_all(total, AXES, 0, 0, tiled=True)
    projected = jnp.sum(got.astype(f32), axis=0) * (1.0 / (nrows * count))
    return (image, projected)


def solution(mesh):
    return jax.shard_map(
        local,
        mesh=mesh,
        in_specs=(
            P(AXES, None),
            P(AXES, None, None, None),
            P(AXES, None),
            P(AXES),
            P(AXES),
        ),
        out_specs=(P(AXES, None), P("mesh", "col")),
        check_vma=False,
    )
```

```python
import jax
import jax.numpy as jnp
from jax import lax
from jax.experimental import pallas as pl
from jax.experimental.pallas import tpu as pltpu
from jax.sharding import PartitionSpec as P

REACH = 2
AXES = ("mesh", "col")
ROWS_DOT = (((0,), (0,)), ((), ()))


def strip_of(cols_ref, live_ref, jac_ref, acc_ref, first, pair):
    _, slots, bsize, _ = jac_ref.shape
    tile = 2 * bsize
    half = lax.broadcasted_iota(jnp.int32, (1, tile), 1) // bsize
    row = lax.broadcasted_iota(jnp.int32, (bsize, tile), 0)
    lane = lax.broadcasted_iota(jnp.int32, (bsize, tile), 1)
    weight = acc_ref[pair : pair + 1, :]
    halves = []
    for side in range(2):
        g = 2 * pair + side
        tiles = [None, jnp.where(lane == row + side * bsize, weight, 0.0), None]
        for s in range(slots):
            place = cols_ref[s, g] - (first + 2 * pair) + REACH
            place = jnp.where(s < live_ref[g], place, -1)
            block = jac_ref[g, s]
            wide = jnp.concatenate([block, block], axis=1).astype(jnp.float32)
            for t in range(3):
                here = jnp.where(half + 2 * t == place, 1.0, 0.0)
                term = wide * here
                tiles[t] = term if tiles[t] is None else tiles[t] + term
        halves.append(jnp.concatenate(tiles, axis=1))
    strip = jnp.concatenate(halves, axis=0)
    high = strip.astype(jnp.bfloat16)
    low = (strip - high.astype(jnp.float32)).astype(jnp.bfloat16)
    return jnp.concatenate([high, low], axis=0)


def apply_strip(strip, rows):
    both = jnp.dot(strip, rows, preferred_element_type=jnp.float32)
    half = strip.shape[0] // 2
    return both[:half] + both[half:]


def inner_kernel(
    cols_hbm, live_hbm, jac_hbm, basis_hbm, acc_hbm,
    image_ref, edge_ref, arm_ref, part_ref,
    cols_ref, live_ref, jac_ref, basis_ref, acc_ref, strips, staged, load_sems, store_sems,
):
    nblk, _, bsize, _ = jac_ref.shape
    nrows = basis_ref.shape[0]
    tile = 2 * bsize
    pairs = nblk // 2
    groups = 3 if pairs % 3 == 0 else 1
    size = pairs // groups
    first = lax.axis_index(AXES) * nblk

    def load(source, target, at):
        copy = pltpu.make_async_copy(source, target, load_sems.at[at])
        copy.start()
        return copy

    small = [
        load(cols_hbm, cols_ref, 0),
        load(live_hbm, live_ref, 1),
        load(acc_hbm, acc_ref, 2),
    ]
    blocks = []
    for i in range(groups):
        where = pl.ds(2 * size * i, 2 * size)
        blocks.append(load(jac_hbm.at[where], jac_ref.at[where], 4 + i))
        if i == 0:
            rows = load(basis_hbm, basis_ref, 3)

    def build(pair):
        if pair % size == 0:
            blocks[pair // size].wait()
        strips[pair % 2] = strip_of(cols_ref, live_ref, jac_ref, acc_ref, first, pair)

    def project(start, stop):
        return lax.dot_general(
            basis_ref[start:stop, :], staged[start:stop, :], ROWS_DOT,
            preferred_element_type=jnp.float32,
        )

    def store(start, stop, at):
        where = pl.ds(start, stop - start)
        copy = pltpu.make_async_copy(staged.at[where], image_ref.at[where], store_sems.at[at])
        copy.start()
        return copy

    for copy in small:
        copy.wait()
    build(0)
    rows.wait()
    middle = (pairs // 2) * tile
    for pair in range(pairs):
        if pair + 1 < pairs:
            build(pair + 1)
        strip = strips[pair % 2]
        start = pair * tile
        if pair == 0:
            edge_ref[0] = apply_strip(strip[:, tile:], basis_ref[: 2 * tile, :])
            arm_ref[0] = strip[:, :tile]
        elif pair == pairs - 1:
            edge_ref[1] = apply_strip(strip[:, : 2 * tile], basis_ref[nrows - 2 * tile :, :])
            arm_ref[1] = strip[:, 2 * tile :]
        else:
            block = basis_ref[start - tile : start + 2 * tile, :]
            staged[start : start + tile, :] = apply_strip(strip, block).astype(jnp.bfloat16)
        if start + tile == middle:
            early = store(tile, middle, 0)
            part_ref[...] = project(tile, middle)
    late = store(middle, nrows - tile, 1)
    part_ref[...] += project(middle, nrows - tile)
    early.wait()
    late.wait()


def edge_kernel(
    near_ref, far_ref, edge_ref, arm_ref, top_ref, bottom_ref, part_ref, _, image_ref, *rest,
):
    *total_refs, staged, sems = rest
    tile, width = top_ref.shape
    nrows = image_ref.shape[0]
    odd = lax.rem(lax.axis_index(AXES), 2) == 1
    near, far = near_ref[...], far_ref[...]
    halos = (jnp.where(odd, near, far), jnp.where(odd, far, near))
    total = part_ref[...]
    copies = []
    for side, own_ref in enumerate((top_ref, bottom_ref)):
        rows = edge_ref[side] + apply_strip(arm_ref[side], halos[side])
        rows = rows.astype(jnp.bfloat16)
        staged[side] = rows
        where = pl.ds(0 if side == 0 else nrows - tile, tile)
        copy = pltpu.make_async_copy(staged.at[side], image_ref.at[where], sems.at[side])
        copy.start()
        copies.append(copy)
        total = total + lax.dot_general(
            own_ref[...], rows, ROWS_DOT, preferred_element_type=jnp.float32
        )
    if len(total_refs) == 1:
        total_refs[0][...] = total.astype(jnp.bfloat16)
    else:
        keep_ref, send_ref = total_refs
        left, right = total[:, : width // 2], total[:, width // 2 :]
        second = lax.axis_index("col") == 1
        keep_ref[...] = jnp.where(second, right, left)
        send_ref[...] = jnp.where(second, left, right).astype(jnp.bfloat16)
    for copy in copies:
        copy.wait()


def whole(memory_space=pltpu.VMEM):
    return pl.BlockSpec(memory_space=memory_space)


def local(basis, jac_blocks, block_cols, live_slots, accumulation):
    nrows, width = basis.shape
    nblk, slots, bsize, _ = jac_blocks.shape
    tile = 2 * bsize
    down, across = (lax.axis_size(axis) for axis in AXES)
    count = down * across
    odd = lax.rem(lax.axis_index(AXES), 2)

    last = nrows - tile
    far_send = lax.dynamic_slice_in_dim(basis, odd * last, tile, axis=0)
    near_send = lax.dynamic_slice_in_dim(basis, (1 - odd) * last, tile, axis=0)
    swaps = [(i, i + 1) for i in range(1, count - 1, 2)]
    far = lax.ppermute(far_send, AXES, swaps + [(j, i) for i, j in swaps])
    swaps = [(i, i + 1) for i in range(0, count, 2)]
    near = lax.ppermute(near_send, AXES, swaps + [(j, i) for i, j in swaps])

    f32, bf16 = jnp.float32, jnp.bfloat16
    image, edge, arm, part = pl.pallas_call(
        inner_kernel,
        out_shape=(
            jax.ShapeDtypeStruct((nrows, width), bf16),
            jax.ShapeDtypeStruct((2, tile, width), f32),
            jax.ShapeDtypeStruct((2, 2 * tile, tile), bf16),
            jax.ShapeDtypeStruct((width, width), f32),
        ),
        in_specs=[whole(pltpu.HBM)] * 5,
        out_specs=(whole(pltpu.HBM), whole(), whole(), whole()),
        scratch_shapes=[
            pltpu.SMEM((slots, nblk), jnp.int32),
            pltpu.SMEM((nblk,), jnp.int32),
            pltpu.VMEM(jac_blocks.shape, bf16),
            pltpu.VMEM((nrows, width), bf16),
            pltpu.VMEM((nblk // 2, tile), f32),
            pltpu.VMEM((2, 2 * tile, 3 * tile), bf16),
            pltpu.VMEM((nrows, width), bf16),
            pltpu.SemaphoreType.DMA((7,)),
            pltpu.SemaphoreType.DMA((2,)),
        ],
        compiler_params=pltpu.CompilerParams(vmem_limit_bytes=32 * 2**20),
        cost_estimate=pl.CostEstimate(
            flops=2 * nrows * width * (width + 12 * bsize),
            bytes_accessed=8 * 2**20,
            transcendentals=0,
        ),
        name="inner",
    )(
        *(
            pltpu.with_memory_space_constraint(array, pltpu.HBM)
            for array in (
                block_cols.T,
                live_slots,
                jac_blocks,
                basis,
                accumulation.reshape(nblk // 2, tile),
            )
        )
    )

    halved = across == 2
    image, *totals = pl.pallas_call(
        edge_kernel,
        out_shape=(
            jax.ShapeDtypeStruct((nrows, width), bf16),
            *(
                jax.ShapeDtypeStruct((width, width // 2 if halved else width), kind)
                for kind in ((f32, bf16) if halved else (bf16,))
            ),
        ),
        grid=(1,),
        in_specs=[
            whole(), whole(), whole(), whole(),
            pl.BlockSpec((tile, width), lambda i: (0, 0)),
            pl.BlockSpec((tile, width), lambda i: (nrows // tile - 1, 0)),
            whole(), whole(pl.ANY),
        ],
        out_specs=(whole(pl.ANY), *([whole()] * (1 + halved))),
        scratch_shapes=[
            pltpu.VMEM((2, tile, width), bf16),
            pltpu.SemaphoreType.DMA((2,)),
        ],
        input_output_aliases={7: 0},
        compiler_params=pltpu.CompilerParams(vmem_limit_bytes=32 * 2**20),
        name="edges",
    )(near, far, edge, arm, basis, basis, part, image)
    if halved:
        keep, send = totals
        got = lax.ppermute(send, "col", [(0, 1), (1, 0)])
        total = (keep + got.astype(f32)).astype(bf16)
        total = total.reshape(down, width // down, width // across)
        got = lax.all_to_all(total, "mesh", 0, 0, tiled=True)
    else:
        total = totals[0].reshape(down, width // down, across, width // across)
        total = total.transpose(0, 2, 1, 3)
        total = total.reshape(count, width // down, width // across)
        got = lax.all_to_all(total, AXES, 0, 0, tiled=True)
    projected = jnp.sum(got.astype(f32), axis=0) * (1.0 / (nrows * count))
    return (image, projected)


def solution(mesh):
    return jax.shard_map(
        local,
        mesh=mesh,
        in_specs=(
            P(AXES, None),
            P(AXES, None, None, None),
            P(AXES, None),
            P(AXES),
            P(AXES),
        ),
        out_specs=(P(AXES, None), P("mesh", "col")),
        check_vma=False,
    )
```

```python
import jax
import jax.numpy as jnp
from jax import lax
from jax.experimental import pallas as pl
from jax.experimental.pallas import tpu as pltpu
from jax.sharding import PartitionSpec as P

REACH = 2
AXES = ("mesh", "col")
ROWS_DOT = (((0,), (0,)), ((), ()))


def strip_of(cols_ref, live_ref, jac_ref, acc_ref, first, pair):
    _, slots, bsize, _ = jac_ref.shape
    tile = 2 * bsize
    half = lax.broadcasted_iota(jnp.int32, (1, tile), 1) // bsize
    row = lax.broadcasted_iota(jnp.int32, (bsize, tile), 0)
    lane = lax.broadcasted_iota(jnp.int32, (bsize, tile), 1)
    weight = acc_ref[pair : pair + 1, :]
    halves = []
    for side in range(2):
        g = 2 * pair + side
        tiles = [None, jnp.where(lane == row + side * bsize, weight, 0.0), None]
        for s in range(slots):
            place = cols_ref[s, g] - (first + 2 * pair) + REACH
            place = jnp.where(s < live_ref[g], place, -1)
            block = jac_ref[g, s]
            wide = jnp.concatenate([block, block], axis=1).astype(jnp.float32)
            for t in range(3):
                here = jnp.where(half + 2 * t == place, 1.0, 0.0)
                term = wide * here
                tiles[t] = term if tiles[t] is None else tiles[t] + term
        halves.append(jnp.concatenate(tiles, axis=1))
    strip = jnp.concatenate(halves, axis=0)
    high = strip.astype(jnp.bfloat16)
    low = (strip - high.astype(jnp.float32)).astype(jnp.bfloat16)
    return jnp.concatenate([high, low], axis=0)


def gathered_rows(cols_ref, live_ref, jac_ref, basis_ref, first, g):
    nblk, slots, bsize, _ = jac_ref.shape
    lane = lax.broadcasted_iota(jnp.int32, (1, slots * bsize), 1)
    keep = jnp.where(lane < live_ref[g] * bsize, 1.0, 0.0).astype(jnp.bfloat16)
    blocks = jnp.concatenate([jac_ref[g, s] for s in range(slots)], axis=1) * keep
    rows = []
    for s in range(slots):
        at = jnp.clip(cols_ref[s, g] - first, 0, nblk - 1) * bsize
        rows.append(basis_ref[pl.ds(pl.multiple_of(at, bsize), bsize), :])
    rows = jnp.concatenate(rows, axis=0)
    return jnp.dot(blocks, rows, preferred_element_type=jnp.float32)


def apply_strip(strip, rows):
    both = jnp.dot(strip, rows, preferred_element_type=jnp.float32)
    half = strip.shape[0] // 2
    return both[:half] + both[half:]


def inner_kernel(
    cols_hbm, live_hbm, jac_hbm, basis_hbm, acc_hbm,
    image_ref, edge_ref, arm_ref, part_ref,
    cols_ref, live_ref, jac_ref, basis_ref, acc_ref, staged, load_sems, store_sems,
):
    nblk, _, bsize, _ = jac_ref.shape
    nrows = basis_ref.shape[0]
    tile = 2 * bsize
    pairs = nblk // 2
    groups = 3 if pairs % 3 == 0 else 1
    size = pairs // groups
    first = lax.axis_index(AXES) * nblk

    def load(source, target, at):
        copy = pltpu.make_async_copy(source, target, load_sems.at[at])
        copy.start()
        return copy

    small = [
        load(cols_hbm, cols_ref, 0),
        load(live_hbm, live_ref, 1),
        load(acc_hbm, acc_ref, 2),
    ]
    blocks = []
    for i in range(groups):
        where = pl.ds(2 * size * i, 2 * size)
        blocks.append(load(jac_hbm.at[where], jac_ref.at[where], 4 + i))
        if i == 0:
            rows = load(basis_hbm, basis_ref, 3)

    def edge_strip(pair):
        return strip_of(cols_ref, live_ref, jac_ref, acc_ref, first, pair)

    row = lax.broadcasted_iota(jnp.int32, (tile, tile), 0)
    lane = lax.broadcasted_iota(jnp.int32, (tile, tile), 1)

    def project(start, stop):
        return lax.dot_general(
            basis_ref[start:stop, :], staged[start:stop, :], ROWS_DOT,
            preferred_element_type=jnp.float32,
        )

    def store(start, stop, at):
        where = pl.ds(start, stop - start)
        copy = pltpu.make_async_copy(staged.at[where], image_ref.at[where], store_sems.at[at])
        copy.start()
        return copy

    for copy in small:
        copy.wait()
    rows.wait()
    middle = (pairs // 2) * tile
    for pair in range(pairs):
        if pair % size == 0:
            blocks[pair // size].wait()
        start = pair * tile
        if pair == 0:
            strip = edge_strip(pair)
            edge_ref[0] = apply_strip(strip[:, tile:], basis_ref[: 2 * tile, :])
            arm_ref[0] = strip[:, :tile]
        elif pair == pairs - 1:
            strip = edge_strip(pair)
            edge_ref[1] = apply_strip(strip[:, : 2 * tile], basis_ref[nrows - 2 * tile :, :])
            arm_ref[1] = strip[:, 2 * tile :]
        else:
            weight = jnp.where(lane == row, acc_ref[pair : pair + 1, :], 0.0)
            weight = jnp.sum(weight, axis=1, keepdims=True)
            coupled = [
                gathered_rows(cols_ref, live_ref, jac_ref, basis_ref, first, 2 * pair + side)
                for side in range(2)
            ]
            own = basis_ref[start : start + tile, :].astype(jnp.float32)
            total = jnp.concatenate(coupled, axis=0) + weight * own
            staged[start : start + tile, :] = total.astype(jnp.bfloat16)
        if start + tile == middle:
            early = store(tile, middle, 0)
            part_ref[...] = project(tile, middle)
    late = store(middle, nrows - tile, 1)
    part_ref[...] += project(middle, nrows - tile)
    early.wait()
    late.wait()


def edge_kernel(
    near_ref, far_ref, edge_ref, arm_ref, top_ref, bottom_ref, part_ref, _, image_ref, *rest,
):
    *total_refs, staged, sems = rest
    tile, width = top_ref.shape
    nrows = image_ref.shape[0]
    odd = lax.rem(lax.axis_index(AXES), 2) == 1
    near, far = near_ref[...], far_ref[...]
    halos = (jnp.where(odd, near, far), jnp.where(odd, far, near))
    total = part_ref[...]
    copies = []
    for side, own_ref in enumerate((top_ref, bottom_ref)):
        rows = edge_ref[side] + apply_strip(arm_ref[side], halos[side])
        rows = rows.astype(jnp.bfloat16)
        staged[side] = rows
        where = pl.ds(0 if side == 0 else nrows - tile, tile)
        copy = pltpu.make_async_copy(staged.at[side], image_ref.at[where], sems.at[side])
        copy.start()
        copies.append(copy)
        total = total + lax.dot_general(
            own_ref[...], rows, ROWS_DOT, preferred_element_type=jnp.float32
        )
    if len(total_refs) == 1:
        total_refs[0][...] = total.astype(jnp.bfloat16)
    else:
        keep_ref, send_ref = total_refs
        left, right = total[:, : width // 2], total[:, width // 2 :]
        second = lax.axis_index("col") == 1
        keep_ref[...] = jnp.where(second, right, left)
        send_ref[...] = jnp.where(second, left, right).astype(jnp.bfloat16)
    for copy in copies:
        copy.wait()


def whole(memory_space=pltpu.VMEM):
    return pl.BlockSpec(memory_space=memory_space)


def local(basis, jac_blocks, block_cols, live_slots, accumulation):
    nrows, width = basis.shape
    nblk, slots, bsize, _ = jac_blocks.shape
    tile = 2 * bsize
    down, across = (lax.axis_size(axis) for axis in AXES)
    count = down * across
    odd = lax.rem(lax.axis_index(AXES), 2)

    last = nrows - tile
    far_send = lax.dynamic_slice_in_dim(basis, odd * last, tile, axis=0)
    near_send = lax.dynamic_slice_in_dim(basis, (1 - odd) * last, tile, axis=0)
    swaps = [(i, i + 1) for i in range(1, count - 1, 2)]
    far = lax.ppermute(far_send, AXES, swaps + [(j, i) for i, j in swaps])
    swaps = [(i, i + 1) for i in range(0, count, 2)]
    near = lax.ppermute(near_send, AXES, swaps + [(j, i) for i, j in swaps])

    f32, bf16 = jnp.float32, jnp.bfloat16
    image, edge, arm, part = pl.pallas_call(
        inner_kernel,
        out_shape=(
            jax.ShapeDtypeStruct((nrows, width), bf16),
            jax.ShapeDtypeStruct((2, tile, width), f32),
            jax.ShapeDtypeStruct((2, 2 * tile, tile), bf16),
            jax.ShapeDtypeStruct((width, width), f32),
        ),
        in_specs=[whole(pltpu.HBM)] * 5,
        out_specs=(whole(pltpu.HBM), whole(), whole(), whole()),
        scratch_shapes=[
            pltpu.SMEM((slots, nblk), jnp.int32),
            pltpu.SMEM((nblk,), jnp.int32),
            pltpu.VMEM(jac_blocks.shape, bf16),
            pltpu.VMEM((nrows, width), bf16),
            pltpu.VMEM((nblk // 2, tile), f32),
            pltpu.VMEM((nrows, width), bf16),
            pltpu.SemaphoreType.DMA((7,)),
            pltpu.SemaphoreType.DMA((2,)),
        ],
        compiler_params=pltpu.CompilerParams(vmem_limit_bytes=32 * 2**20),
        cost_estimate=pl.CostEstimate(
            flops=2 * nrows * width * (width + 12 * bsize),
            bytes_accessed=8 * 2**20,
            transcendentals=0,
        ),
        name="inner",
    )(
        *(
            pltpu.with_memory_space_constraint(array, pltpu.HBM)
            for array in (
                block_cols.T,
                live_slots,
                jac_blocks,
                basis,
                accumulation.reshape(nblk // 2, tile),
            )
        )
    )

    halved = across == 2
    image, *totals = pl.pallas_call(
        edge_kernel,
        out_shape=(
            jax.ShapeDtypeStruct((nrows, width), bf16),
            *(
                jax.ShapeDtypeStruct((width, width // 2 if halved else width), kind)
                for kind in ((f32, bf16) if halved else (bf16,))
            ),
        ),
        grid=(1,),
        in_specs=[
            whole(), whole(), whole(), whole(),
            pl.BlockSpec((tile, width), lambda i: (0, 0)),
            pl.BlockSpec((tile, width), lambda i: (nrows // tile - 1, 0)),
            whole(), whole(pl.ANY),
        ],
        out_specs=(whole(pl.ANY), *([whole()] * (1 + halved))),
        scratch_shapes=[
            pltpu.VMEM((2, tile, width), bf16),
            pltpu.SemaphoreType.DMA((2,)),
        ],
        input_output_aliases={7: 0},
        compiler_params=pltpu.CompilerParams(vmem_limit_bytes=32 * 2**20),
        name="edges",
    )(near, far, edge, arm, basis, basis, part, image)
    if halved:
        keep, send = totals
        got = lax.ppermute(send, "col", [(0, 1), (1, 0)])
        total = (keep + got.astype(f32)).astype(bf16)
        total = total.reshape(down, width // down, width // across)
        got = lax.all_to_all(total, "mesh", 0, 0, tiled=True)
    else:
        total = totals[0].reshape(down, width // down, across, width // across)
        total = total.transpose(0, 2, 1, 3)
        total = total.reshape(count, width // down, width // across)
        got = lax.all_to_all(total, AXES, 0, 0, tiled=True)
    projected = jnp.sum(got.astype(f32), axis=0) * (1.0 / (nrows * count))
    return (image, projected)


def solution(mesh):
    return jax.shard_map(
        local,
        mesh=mesh,
        in_specs=(
            P(AXES, None),
            P(AXES, None, None, None),
            P(AXES, None),
            P(AXES),
            P(AXES),
        ),
        out_specs=(P(AXES, None), P("mesh", "col")),
        check_vma=False,
    )
```

```python
import jax
import jax.numpy as jnp
from jax import lax
from jax.experimental import pallas as pl
from jax.experimental.pallas import tpu as pltpu
from jax.sharding import PartitionSpec as P

REACH = 2
AXES = ("mesh", "col")
ROWS_DOT = (((0,), (0,)), ((), ()))


def strip_of(cols_ref, live_ref, jac_ref, acc_ref, first, pair):
    _, slots, bsize, _ = jac_ref.shape
    tile = 2 * bsize
    half = lax.broadcasted_iota(jnp.int32, (1, tile), 1) // bsize
    row = lax.broadcasted_iota(jnp.int32, (bsize, tile), 0)
    lane = lax.broadcasted_iota(jnp.int32, (bsize, tile), 1)
    weight = acc_ref[pair : pair + 1, :]
    halves = []
    for side in range(2):
        g = 2 * pair + side
        tiles = [None, jnp.where(lane == row + side * bsize, weight, 0.0), None]
        for s in range(slots):
            place = cols_ref[s, g] - (first + 2 * pair) + REACH
            place = jnp.where(s < live_ref[g], place, -1)
            block = jac_ref[g, s]
            wide = jnp.concatenate([block, block], axis=1).astype(jnp.float32)
            for t in range(3):
                here = jnp.where(half + 2 * t == place, 1.0, 0.0)
                term = wide * here
                tiles[t] = term if tiles[t] is None else tiles[t] + term
        halves.append(jnp.concatenate(tiles, axis=1))
    strip = jnp.concatenate(halves, axis=0)
    high = strip.astype(jnp.bfloat16)
    low = (strip - high.astype(jnp.float32)).astype(jnp.bfloat16)
    return jnp.concatenate([high, low], axis=0)


def gathered_rows(cols_ref, live_ref, jac_ref, basis_ref, first, g):
    nblk, slots, bsize, _ = jac_ref.shape
    lane = lax.broadcasted_iota(jnp.int32, (1, slots * bsize), 1)
    keep = jnp.where(lane < live_ref[g] * bsize, 1.0, 0.0).astype(jnp.bfloat16)
    blocks = jnp.concatenate([jac_ref[g, s] for s in range(slots)], axis=1) * keep
    rows = []
    for s in range(slots):
        at = jnp.clip(cols_ref[s, g] - first, 0, nblk - 1) * bsize
        rows.append(basis_ref[pl.ds(pl.multiple_of(at, bsize), bsize), :])
    rows = jnp.concatenate(rows, axis=0)
    return jnp.dot(blocks, rows, preferred_element_type=jnp.float32)


def apply_strip(strip, rows):
    both = jnp.dot(strip, rows, preferred_element_type=jnp.float32)
    half = strip.shape[0] // 2
    return both[:half] + both[half:]


def slice_kernel(basis_hbm, far_ref, near_ref, sems):
    tile = far_ref.shape[0]
    last = basis_hbm.shape[0] - tile
    odd = lax.rem(lax.axis_index(AXES), 2)
    copies = []
    for i, (at, target) in enumerate(((odd, far_ref), (1 - odd, near_ref))):
        where = pl.ds(pl.multiple_of(at * last, tile), tile)
        copies.append(pltpu.make_async_copy(basis_hbm.at[where], target, sems.at[i]))
        copies[i].start()
    for copy in copies:
        copy.wait()


def inner_kernel(
    cols_ref, live_ref, jac_ref, basis_ref, acc_ref,
    image_ref, edge_ref, arm_ref, part_ref, staged, sems,
):
    nblk, _, bsize, _ = jac_ref.shape
    nrows = basis_ref.shape[0]
    tile = 2 * bsize
    pairs = nblk // 2
    first = lax.axis_index(AXES) * nblk

    def edge_strip(pair):
        return strip_of(cols_ref, live_ref, jac_ref, acc_ref, first, pair)

    row = lax.broadcasted_iota(jnp.int32, (tile, tile), 0)
    lane = lax.broadcasted_iota(jnp.int32, (tile, tile), 1)

    def project(start, stop):
        return lax.dot_general(
            basis_ref[start:stop, :], staged[start:stop, :], ROWS_DOT,
            preferred_element_type=jnp.float32,
        )

    def store(start, stop, at):
        where = pl.ds(start, stop - start)
        copy = pltpu.make_async_copy(staged.at[where], image_ref.at[where], sems.at[at])
        copy.start()
        return copy

    middle = (pairs // 2) * tile
    for pair in range(pairs):
        start = pair * tile
        if pair == 0:
            strip = edge_strip(pair)
            edge_ref[0] = apply_strip(strip[:, tile:], basis_ref[: 2 * tile, :])
            arm_ref[0] = strip[:, :tile]
        elif pair == pairs - 1:
            strip = edge_strip(pair)
            edge_ref[1] = apply_strip(strip[:, : 2 * tile], basis_ref[nrows - 2 * tile :, :])
            arm_ref[1] = strip[:, 2 * tile :]
        else:
            weight = jnp.where(lane == row, acc_ref[pair : pair + 1, :], 0.0)
            weight = jnp.sum(weight, axis=1, keepdims=True)
            coupled = [
                gathered_rows(cols_ref, live_ref, jac_ref, basis_ref, first, 2 * pair + side)
                for side in range(2)
            ]
            own = basis_ref[start : start + tile, :].astype(jnp.float32)
            total = jnp.concatenate(coupled, axis=0) + weight * own
            staged[start : start + tile, :] = total.astype(jnp.bfloat16)
        if start + tile == middle:
            early = store(tile, middle, 0)
            part_ref[...] = project(tile, middle)
    late = store(middle, nrows - tile, 1)
    part_ref[...] += project(middle, nrows - tile)
    early.wait()
    late.wait()


def edge_kernel(
    far_ref, near_ref, edge_ref, arm_ref, top_ref, bottom_ref, part_ref, _, image_ref, *rest,
):
    *total_refs, staged, sems = rest
    tile, width = top_ref.shape
    nrows = image_ref.shape[0]
    odd = lax.rem(lax.axis_index(AXES), 2) == 1
    near, far = near_ref[...], far_ref[...]
    halos = (jnp.where(odd, near, far), jnp.where(odd, far, near))
    total = part_ref[...]
    copies = []
    for side, own_ref in enumerate((top_ref, bottom_ref)):
        rows = edge_ref[side] + apply_strip(arm_ref[side], halos[side])
        rows = rows.astype(jnp.bfloat16)
        staged[side] = rows
        where = pl.ds(0 if side == 0 else nrows - tile, tile)
        copy = pltpu.make_async_copy(staged.at[side], image_ref.at[where], sems.at[side])
        copy.start()
        copies.append(copy)
        total = total + lax.dot_general(
            own_ref[...], rows, ROWS_DOT, preferred_element_type=jnp.float32
        )
    if len(total_refs) == 1:
        total_refs[0][...] = total.astype(jnp.bfloat16)
    else:
        keep_ref, send_ref = total_refs
        left, right = total[:, : width // 2], total[:, width // 2 :]
        second = lax.axis_index("col") == 1
        keep_ref[...] = jnp.where(second, right, left)
        send_ref[...] = jnp.where(second, left, right).astype(jnp.bfloat16)
    for copy in copies:
        copy.wait()


def whole(memory_space=pltpu.VMEM):
    return pl.BlockSpec(memory_space=memory_space)


def local(basis, jac_blocks, block_cols, live_slots, accumulation):
    nrows, width = basis.shape
    nblk, slots, bsize, _ = jac_blocks.shape
    tile = 2 * bsize
    down, across = (lax.axis_size(axis) for axis in AXES)
    count = down * across
    f32, bf16 = jnp.float32, jnp.bfloat16
    edge_shape = jax.ShapeDtypeStruct((tile, width), bf16)
    far_send, near_send = pl.pallas_call(
        slice_kernel,
        out_shape=(edge_shape, edge_shape),
        in_specs=[whole(pltpu.HBM)],
        out_specs=(whole(), whole()),
        scratch_shapes=[pltpu.SemaphoreType.DMA((2,))],
        compiler_params=pltpu.CompilerParams(vmem_limit_bytes=4 * 2**20),
        cost_estimate=pl.CostEstimate(
            flops=2 * nrows * width * width * slots, bytes_accessed=0, transcendentals=0
        ),
        name="halo_rows",
    )(pltpu.with_memory_space_constraint(basis, pltpu.HBM))
    swaps = [(i, i + 1) for i in range(1, count - 1, 2)]
    far = lax.ppermute(far_send, AXES, swaps + [(j, i) for i, j in swaps])
    swaps = [(i, i + 1) for i in range(0, count, 2)]
    near = lax.ppermute(near_send, AXES, swaps + [(j, i) for i, j in swaps])

    image, edge, arm, part = pl.pallas_call(
        inner_kernel,
        out_shape=(
            jax.ShapeDtypeStruct((nrows, width), bf16),
            jax.ShapeDtypeStruct((2, tile, width), f32),
            jax.ShapeDtypeStruct((2, 2 * tile, tile), bf16),
            jax.ShapeDtypeStruct((width, width), f32),
        ),
        in_specs=[whole(pltpu.SMEM), whole(pltpu.SMEM), whole(), whole(), whole()],
        out_specs=(whole(pltpu.HBM), whole(), whole(), whole()),
        scratch_shapes=[
            pltpu.VMEM((nrows, width), bf16),
            pltpu.SemaphoreType.DMA((2,)),
        ],
        compiler_params=pltpu.CompilerParams(vmem_limit_bytes=32 * 2**20),
        cost_estimate=pl.CostEstimate(
            flops=2 * nrows * width * (width + 12 * bsize),
            bytes_accessed=8 * 2**20,
            transcendentals=0,
        ),
        name="inner",
    )(
        block_cols.T,
        live_slots,
        jac_blocks,
        basis,
        accumulation.reshape(nblk // 2, tile),
    )

    halved = across == 2
    image, *totals = pl.pallas_call(
        edge_kernel,
        out_shape=(
            jax.ShapeDtypeStruct((nrows, width), bf16),
            *(
                jax.ShapeDtypeStruct((width, width // 2 if halved else width), kind)
                for kind in ((f32, bf16) if halved else (bf16,))
            ),
        ),
        grid=(1,),
        in_specs=[
            whole(), whole(), whole(), whole(),
            pl.BlockSpec((tile, width), lambda i: (0, 0)),
            pl.BlockSpec((tile, width), lambda i: (nrows // tile - 1, 0)),
            whole(), whole(pl.ANY),
        ],
        out_specs=(whole(pl.ANY), *([whole()] * (1 + halved))),
        scratch_shapes=[
            pltpu.VMEM((2, tile, width), bf16),
            pltpu.SemaphoreType.DMA((2,)),
        ],
        input_output_aliases={7: 0},
        compiler_params=pltpu.CompilerParams(vmem_limit_bytes=32 * 2**20),
        name="edges",
    )(far, near, edge, arm, basis, basis, part, image)
    if halved:
        keep, send = totals
        got = lax.ppermute(send, "col", [(0, 1), (1, 0)])
        total = (keep + got.astype(f32)).astype(bf16)
        total = total.reshape(down, width // down, width // across)
        got = lax.all_to_all(total, "mesh", 0, 0, tiled=True)
    else:
        total = totals[0].reshape(down, width // down, across, width // across)
        total = total.transpose(0, 2, 1, 3)
        total = total.reshape(count, width // down, width // across)
        got = lax.all_to_all(total, AXES, 0, 0, tiled=True)
    projected = jnp.sum(got.astype(f32), axis=0) * (1.0 / (nrows * count))
    return (image, projected)


def solution(mesh):
    return jax.shard_map(
        local,
        mesh=mesh,
        in_specs=(
            P(AXES, None),
            P(AXES, None, None, None),
            P(AXES, None),
            P(AXES),
            P(AXES),
        ),
        out_specs=(P(AXES, None), P("mesh", "col")),
        check_vma=False,
    )
```

```python
import jax
import jax.numpy as jnp
from jax import lax
from jax.experimental import pallas as pl
from jax.experimental.pallas import tpu as pltpu
from jax.sharding import PartitionSpec as P

REACH = 2
AXES = ("mesh", "col")
ROWS_DOT = (((0,), (0,)), ((), ()))


def strip_of(cols_ref, live_ref, jac_ref, acc_ref, first, pair):
    _, slots, bsize, _ = jac_ref.shape
    tile = 2 * bsize
    half = lax.broadcasted_iota(jnp.int32, (1, tile), 1) // bsize
    row = lax.broadcasted_iota(jnp.int32, (bsize, tile), 0)
    lane = lax.broadcasted_iota(jnp.int32, (bsize, tile), 1)
    weight = acc_ref[pair : pair + 1, :]
    halves = []
    for side in range(2):
        g = 2 * pair + side
        tiles = [None, jnp.where(lane == row + side * bsize, weight, 0.0), None]
        for s in range(slots):
            place = cols_ref[s, g] - (first + 2 * pair) + REACH
            place = jnp.where(s < live_ref[g], place, -1)
            block = jac_ref[g, s]
            wide = jnp.concatenate([block, block], axis=1).astype(jnp.float32)
            for t in range(3):
                here = jnp.where(half + 2 * t == place, 1.0, 0.0)
                term = wide * here
                tiles[t] = term if tiles[t] is None else tiles[t] + term
        halves.append(jnp.concatenate(tiles, axis=1))
    strip = jnp.concatenate(halves, axis=0)
    high = strip.astype(jnp.bfloat16)
    low = (strip - high.astype(jnp.float32)).astype(jnp.bfloat16)
    return jnp.concatenate([high, low], axis=0)


def apply_strip(strip, rows):
    both = jnp.dot(strip, rows, preferred_element_type=jnp.float32)
    half = strip.shape[0] // 2
    return both[:half] + both[half:]


def slice_kernel(basis_hbm, far_ref, near_ref, sems):
    tile = far_ref.shape[0]
    last = basis_hbm.shape[0] - tile
    odd = lax.rem(lax.axis_index(AXES), 2)
    copies = []
    for i, (at, target) in enumerate(((odd, far_ref), (1 - odd, near_ref))):
        where = pl.ds(pl.multiple_of(at * last, tile), tile)
        copies.append(pltpu.make_async_copy(basis_hbm.at[where], target, sems.at[i]))
        copies[i].start()
    for copy in copies:
        copy.wait()


def inner_kernel(
    cols_ref, live_ref, jac_ref, basis_ref, acc_ref,
    image_ref, edge_ref, arm_ref, part_ref, strips, staged, sems,
):
    nblk, _, bsize, _ = jac_ref.shape
    nrows = basis_ref.shape[0]
    tile = 2 * bsize
    pairs = nblk // 2
    first = lax.axis_index(AXES) * nblk

    def project(start, stop):
        return lax.dot_general(
            basis_ref[start:stop, :], staged[start:stop, :], ROWS_DOT,
            preferred_element_type=jnp.float32,
        )

    def store(start, stop, at):
        where = pl.ds(start, stop - start)
        copy = pltpu.make_async_copy(staged.at[where], image_ref.at[where], sems.at[at])
        copy.start()
        return copy

    def build(at):
        strips[at % 2] = strip_of(cols_ref, live_ref, jac_ref, acc_ref, first, order[at])

    order = [*range(1, pairs - 1), 0, pairs - 1]
    middle = (pairs // 2) * tile
    stored = tile
    copies = []
    build(0)
    for at, pair in enumerate(order):
        if at + 1 < pairs:
            build(at + 1)
        strip = strips[at % 2]
        start = pair * tile
        stop = start + tile
        if pair == 0:
            edge_ref[0] = apply_strip(strip[:, tile:], basis_ref[: 2 * tile, :])
            arm_ref[0] = strip[:, :tile]
        elif pair == pairs - 1:
            edge_ref[1] = apply_strip(strip[:, : 2 * tile], basis_ref[nrows - 2 * tile :, :])
            arm_ref[1] = strip[:, 2 * tile :]
        else:
            block = basis_ref[start - tile : start + 2 * tile, :]
            staged[start:stop, :] = apply_strip(strip, block).astype(jnp.bfloat16)
            if pair % 3 == 0 or pair == pairs - 2:
                copies.append(store(stored, stop, len(copies)))
                stored = stop
        if stop == middle:
            part_ref[...] = project(tile, middle)
        if pair == pairs - 2:
            part_ref[...] += project(middle, nrows - tile)
    for copy in copies:
        copy.wait()


def edge_kernel(
    far_ref, near_ref, edge_ref, arm_ref, top_ref, bottom_ref, part_ref, _, image_ref, *rest,
):
    *total_refs, staged, sems = rest
    tile, width = top_ref.shape
    nrows = image_ref.shape[0]
    odd = lax.rem(lax.axis_index(AXES), 2) == 1
    near, far = near_ref[...], far_ref[...]
    halos = (jnp.where(odd, near, far), jnp.where(odd, far, near))
    total = part_ref[...]
    copies = []
    for side, own_ref in enumerate((top_ref, bottom_ref)):
        rows = edge_ref[side] + apply_strip(arm_ref[side], halos[side])
        rows = rows.astype(jnp.bfloat16)
        staged[side] = rows
        where = pl.ds(0 if side == 0 else nrows - tile, tile)
        copy = pltpu.make_async_copy(staged.at[side], image_ref.at[where], sems.at[side])
        copy.start()
        copies.append(copy)
        total = total + lax.dot_general(
            own_ref[...], rows, ROWS_DOT, preferred_element_type=jnp.float32
        )
    if len(total_refs) == 1:
        total_refs[0][...] = total.astype(jnp.bfloat16)
    else:
        keep_ref, send_ref = total_refs
        left, right = total[:, : width // 2], total[:, width // 2 :]
        second = lax.axis_index("col") == 1
        keep_ref[...] = jnp.where(second, right, left)
        send_ref[...] = jnp.where(second, left, right).astype(jnp.bfloat16)
    for copy in copies:
        copy.wait()


def whole(memory_space=pltpu.VMEM):
    return pl.BlockSpec(memory_space=memory_space)


def local(basis, jac_blocks, block_cols, live_slots, accumulation):
    nrows, width = basis.shape
    nblk, slots, bsize, _ = jac_blocks.shape
    tile = 2 * bsize
    down, across = (lax.axis_size(axis) for axis in AXES)
    count = down * across
    f32, bf16 = jnp.float32, jnp.bfloat16
    edge_shape = jax.ShapeDtypeStruct((tile, width), bf16)
    far_send, near_send = pl.pallas_call(
        slice_kernel,
        out_shape=(edge_shape, edge_shape),
        in_specs=[whole(pltpu.HBM)],
        out_specs=(whole(), whole()),
        scratch_shapes=[pltpu.SemaphoreType.DMA((2,))],
        compiler_params=pltpu.CompilerParams(vmem_limit_bytes=4 * 2**20),
        cost_estimate=pl.CostEstimate(
            flops=2 * nrows * width * width * slots, bytes_accessed=0, transcendentals=0
        ),
        name="halo_rows",
    )(pltpu.with_memory_space_constraint(basis, pltpu.HBM))
    swaps = [(i, i + 1) for i in range(1, count - 1, 2)]
    far = lax.ppermute(far_send, AXES, swaps + [(j, i) for i, j in swaps])
    swaps = [(i, i + 1) for i in range(0, count, 2)]
    near = lax.ppermute(near_send, AXES, swaps + [(j, i) for i, j in swaps])

    image, edge, arm, part = pl.pallas_call(
        inner_kernel,
        out_shape=(
            jax.ShapeDtypeStruct((nrows, width), bf16),
            jax.ShapeDtypeStruct((2, tile, width), f32),
            jax.ShapeDtypeStruct((2, 2 * tile, tile), bf16),
            jax.ShapeDtypeStruct((width, width), f32),
        ),
        in_specs=[whole(pltpu.SMEM), whole(pltpu.SMEM), whole(), whole(), whole()],
        out_specs=(whole(pltpu.HBM), whole(), whole(), whole()),
        scratch_shapes=[
            pltpu.VMEM((2, 2 * tile, 3 * tile), bf16),
            pltpu.VMEM((nrows, width), bf16),
            pltpu.SemaphoreType.DMA((nblk // 6 + 1,)),
        ],
        compiler_params=pltpu.CompilerParams(vmem_limit_bytes=32 * 2**20),
        cost_estimate=pl.CostEstimate(
            flops=2 * nrows * width * (width + 12 * bsize),
            bytes_accessed=8 * 2**20,
            transcendentals=0,
        ),
        name="inner",
    )(
        block_cols.T,
        live_slots,
        jac_blocks,
        basis,
        accumulation.reshape(nblk // 2, tile),
    )

    halved = across == 2
    image, *totals = pl.pallas_call(
        edge_kernel,
        out_shape=(
            jax.ShapeDtypeStruct((nrows, width), bf16),
            *(
                jax.ShapeDtypeStruct((width, width // 2 if halved else width), kind)
                for kind in ((f32, bf16) if halved else (bf16,))
            ),
        ),
        grid=(1,),
        in_specs=[
            whole(), whole(), whole(), whole(),
            pl.BlockSpec((tile, width), lambda i: (0, 0)),
            pl.BlockSpec((tile, width), lambda i: (nrows // tile - 1, 0)),
            whole(), whole(pl.ANY),
        ],
        out_specs=(whole(pl.ANY), *([whole()] * (1 + halved))),
        scratch_shapes=[
            pltpu.VMEM((2, tile, width), bf16),
            pltpu.SemaphoreType.DMA((2,)),
        ],
        input_output_aliases={7: 0},
        compiler_params=pltpu.CompilerParams(vmem_limit_bytes=32 * 2**20),
        name="edges",
    )(far, near, edge, arm, basis, basis, part, image)
    if halved:
        keep, send = totals
        got = lax.ppermute(send, "col", [(0, 1), (1, 0)])
        total = (keep + got.astype(f32)).astype(bf16)
        total = total.reshape(down, width // down, width // across)
        got = lax.all_to_all(total, "mesh", 0, 0, tiled=True)
    else:
        total = totals[0].reshape(down, width // down, across, width // across)
        total = total.transpose(0, 2, 1, 3)
        total = total.reshape(count, width // down, width // across)
        got = lax.all_to_all(total, AXES, 0, 0, tiled=True)
    projected = jnp.sum(got.astype(f32), axis=0) * (1.0 / (nrows * count))
    return (image, projected)


def solution(mesh):
    return jax.shard_map(
        local,
        mesh=mesh,
        in_specs=(
            P(AXES, None),
            P(AXES, None, None, None),
            P(AXES, None),
            P(AXES),
            P(AXES),
        ),
        out_specs=(P(AXES, None), P("mesh", "col")),
        check_vma=False,
    )
```

```python
import jax
import jax.numpy as jnp
from jax import lax
from jax.experimental import pallas as pl
from jax.experimental.pallas import tpu as pltpu
from jax.sharding import PartitionSpec as P

REACH = 2
AXES = ("mesh", "col")
ROWS_DOT = (((0,), (0,)), ((), ()))


def strip_of(cols_ref, live_ref, jac_ref, acc_ref, first, pair):
    _, slots, bsize, _ = jac_ref.shape
    tile = 2 * bsize
    half = lax.broadcasted_iota(jnp.int32, (1, tile), 1) // bsize
    row = lax.broadcasted_iota(jnp.int32, (bsize, tile), 0)
    lane = lax.broadcasted_iota(jnp.int32, (bsize, tile), 1)
    weight = acc_ref[pair : pair + 1, :]
    halves = []
    for side in range(2):
        g = 2 * pair + side
        tiles = [None, jnp.where(lane == row + side * bsize, weight, 0.0), None]
        for s in range(slots):
            place = cols_ref[s, g] - (first + 2 * pair) + REACH
            place = jnp.where(s < live_ref[g], place, -1)
            block = jac_ref[g, s]
            wide = jnp.concatenate([block, block], axis=1).astype(jnp.float32)
            for t in range(3):
                here = jnp.where(half + 2 * t == place, 1.0, 0.0)
                term = wide * here
                tiles[t] = term if tiles[t] is None else tiles[t] + term
        halves.append(jnp.concatenate(tiles, axis=1))
    strip = jnp.concatenate(halves, axis=0)
    high = strip.astype(jnp.bfloat16)
    low = (strip - high.astype(jnp.float32)).astype(jnp.bfloat16)
    return jnp.concatenate([high, low], axis=0)


def gathered_rows(cols_ref, live_ref, jac_ref, basis_ref, first, g):
    nblk, slots, bsize, _ = jac_ref.shape
    lane = lax.broadcasted_iota(jnp.int32, (1, slots * bsize), 1)
    keep = jnp.where(lane < live_ref[g] * bsize, 1.0, 0.0).astype(jnp.bfloat16)
    blocks = jnp.concatenate([jac_ref[g, s] for s in range(slots)], axis=1) * keep
    rows = []
    for s in range(slots):
        at = jnp.clip(cols_ref[s, g] - first, 0, nblk - 1) * bsize
        rows.append(basis_ref[pl.ds(pl.multiple_of(at, bsize), bsize), :])
    rows = jnp.concatenate(rows, axis=0)
    return jnp.dot(blocks, rows, preferred_element_type=jnp.float32)


def apply_strip(strip, rows):
    both = jnp.dot(strip, rows, preferred_element_type=jnp.float32)
    half = strip.shape[0] // 2
    return both[:half] + both[half:]


def slice_kernel(basis_hbm, far_ref, near_ref, sems):
    tile = far_ref.shape[0]
    last = basis_hbm.shape[0] - tile
    odd = lax.rem(lax.axis_index(AXES), 2)
    copies = []
    for i, (at, target) in enumerate(((odd, far_ref), (1 - odd, near_ref))):
        where = pl.ds(pl.multiple_of(at * last, tile), tile)
        copies.append(pltpu.make_async_copy(basis_hbm.at[where], target, sems.at[i]))
        copies[i].start()
    for copy in copies:
        copy.wait()


def inner_kernel(
    cols_ref, live_ref, jac_ref, basis_ref, acc_ref,
    image_ref, edge_ref, arm_ref, part_ref, staged, sems,
):
    nblk, _, bsize, _ = jac_ref.shape
    nrows = basis_ref.shape[0]
    tile = 2 * bsize
    pairs = nblk // 2
    first = lax.axis_index(AXES) * nblk

    def project(start, stop):
        total = lax.dot_general(
            basis_ref[start:stop, :], staged[start:stop, :], ROWS_DOT,
            preferred_element_type=jnp.float32,
        )
        parts, _, wide = part_ref.shape
        return [total[:, i * wide : (i + 1) * wide] for i in range(parts)]

    def store(start, stop, at):
        where = pl.ds(start, stop - start)
        copy = pltpu.make_async_copy(staged.at[where], image_ref.at[where], sems.at[at])
        copy.start()
        return copy

    row = lax.broadcasted_iota(jnp.int32, (tile, tile), 0)
    lane = lax.broadcasted_iota(jnp.int32, (tile, tile), 1)
    middle = (pairs // 2) * tile
    stored = tile
    copies = []
    for pair in range(1, pairs - 1):
        start = pair * tile
        stop = start + tile
        weight = jnp.where(lane == row, acc_ref[pair : pair + 1, :], 0.0)
        weight = jnp.sum(weight, axis=1, keepdims=True)
        coupled = [
            gathered_rows(cols_ref, live_ref, jac_ref, basis_ref, first, 2 * pair + side)
            for side in range(2)
        ]
        own = basis_ref[start:stop, :].astype(jnp.float32)
        total = jnp.concatenate(coupled, axis=0) + weight * own
        staged[start:stop, :] = total.astype(jnp.bfloat16)
        if pair % 3 == 0 or pair == pairs - 2:
            copies.append(store(stored, stop, len(copies)))
            stored = stop
        if stop == middle:
            for i, half in enumerate(project(tile, middle)):
                part_ref[i] = half
    for side, pair in enumerate((0, pairs - 1)):
        strip = strip_of(cols_ref, live_ref, jac_ref, acc_ref, first, pair)
        if side == 0:
            edge_ref[0] = apply_strip(strip[:, tile:], basis_ref[: 2 * tile, :])
            arm_ref[0] = strip[:, :tile]
        else:
            edge_ref[1] = apply_strip(strip[:, : 2 * tile], basis_ref[nrows - 2 * tile :, :])
            arm_ref[1] = strip[:, 2 * tile :]
    for i, half in enumerate(project(middle, nrows - tile)):
        part_ref[i] += half
    for copy in copies:
        copy.wait()


def add_edges(part_ref, tiles, rows_ref, half):
    update = lax.dot_general(
        tiles, rows_ref[half], ROWS_DOT, preferred_element_type=jnp.float32
    )
    return part_ref[half] + update


def leaving_half(parts):
    return 1 - lax.axis_index("col") if parts == 2 else 0


def edge_kernel(
    far_ref, near_ref, edge_ref, arm_ref, top_ref, bottom_ref, part_ref, _,
    image_ref, rows_ref, send_ref, staged, sems,
):
    tile = top_ref.shape[0]
    nrows = image_ref.shape[0]
    parts, _, wide = rows_ref.shape
    odd = lax.rem(lax.axis_index(AXES), 2) == 1
    near, far = near_ref[...], far_ref[...]
    halos = (jnp.where(odd, near, far), jnp.where(odd, far, near))
    copies = []
    for side in range(2):
        rows = edge_ref[side] + apply_strip(arm_ref[side], halos[side])
        rows = rows.astype(jnp.bfloat16)
        staged[side] = rows
        for i in range(parts):
            rows_ref[i, side * tile : (side + 1) * tile, :] = rows[:, i * wide : (i + 1) * wide]
        where = pl.ds(0 if side == 0 else nrows - tile, tile)
        copy = pltpu.make_async_copy(staged.at[side], image_ref.at[where], sems.at[side])
        copy.start()
        copies.append(copy)
    tiles = jnp.concatenate([top_ref[...], bottom_ref[...]], axis=0)
    send = add_edges(part_ref, tiles, rows_ref, leaving_half(parts))
    send_ref[...] = send.astype(jnp.bfloat16)
    for copy in copies:
        copy.wait()


def keep_kernel(top_ref, bottom_ref, rows_ref, part_ref, keep_ref):
    tiles = jnp.concatenate([top_ref[...], bottom_ref[...]], axis=0)
    keep_ref[...] = add_edges(part_ref, tiles, rows_ref, 1 - leaving_half(2))


def whole(memory_space=pltpu.VMEM):
    return pl.BlockSpec(memory_space=memory_space)


def local(basis, jac_blocks, block_cols, live_slots, accumulation):
    nrows, width = basis.shape
    nblk, slots, bsize, _ = jac_blocks.shape
    tile = 2 * bsize
    down, across = (lax.axis_size(axis) for axis in AXES)
    count = down * across
    f32, bf16 = jnp.float32, jnp.bfloat16
    edge_shape = jax.ShapeDtypeStruct((tile, width), bf16)
    far_send, near_send = pl.pallas_call(
        slice_kernel,
        out_shape=(edge_shape, edge_shape),
        in_specs=[whole(pltpu.HBM)],
        out_specs=(whole(), whole()),
        scratch_shapes=[pltpu.SemaphoreType.DMA((2,))],
        compiler_params=pltpu.CompilerParams(vmem_limit_bytes=4 * 2**20),
        cost_estimate=pl.CostEstimate(
            flops=2 * nrows * width * width * slots, bytes_accessed=0, transcendentals=0
        ),
        name="halo_rows",
    )(pltpu.with_memory_space_constraint(basis, pltpu.HBM))
    swaps = [(i, i + 1) for i in range(1, count - 1, 2)]
    far = lax.ppermute(far_send, AXES, swaps + [(j, i) for i, j in swaps])
    swaps = [(i, i + 1) for i in range(0, count, 2)]
    near = lax.ppermute(near_send, AXES, swaps + [(j, i) for i, j in swaps])

    halved = across == 2
    parts = 2 if halved else 1
    wide = width // parts
    image, edge, arm, part = pl.pallas_call(
        inner_kernel,
        out_shape=(
            jax.ShapeDtypeStruct((nrows, width), bf16),
            jax.ShapeDtypeStruct((2, tile, width), f32),
            jax.ShapeDtypeStruct((2, 2 * tile, tile), bf16),
            jax.ShapeDtypeStruct((parts, width, wide), f32),
        ),
        in_specs=[whole(pltpu.SMEM), whole(pltpu.SMEM), whole(), whole(), whole()],
        out_specs=(whole(pltpu.HBM), whole(), whole(), whole()),
        scratch_shapes=[
            pltpu.VMEM((nrows, width), bf16),
            pltpu.SemaphoreType.DMA((nblk // 6 + 1,)),
        ],
        compiler_params=pltpu.CompilerParams(vmem_limit_bytes=32 * 2**20),
        cost_estimate=pl.CostEstimate(
            flops=2 * nrows * width * (width + 12 * bsize),
            bytes_accessed=8 * 2**20,
            transcendentals=0,
        ),
        name="inner",
    )(
        block_cols.T,
        live_slots,
        jac_blocks,
        basis,
        accumulation.reshape(nblk // 2, tile),
    )

    ends = [
        pl.BlockSpec((tile, width), lambda i: (0, 0)),
        pl.BlockSpec((tile, width), lambda i: (nrows // tile - 1, 0)),
    ]
    image, rows, send = pl.pallas_call(
        edge_kernel,
        out_shape=(
            jax.ShapeDtypeStruct((nrows, width), bf16),
            jax.ShapeDtypeStruct((parts, 2 * tile, wide), bf16),
            jax.ShapeDtypeStruct((width, wide), bf16),
        ),
        grid=(1,),
        in_specs=[whole(), whole(), whole(), whole(), *ends, whole(), whole(pl.ANY)],
        out_specs=(whole(pl.ANY), whole(), whole()),
        scratch_shapes=[
            pltpu.VMEM((2, tile, width), bf16),
            pltpu.SemaphoreType.DMA((2,)),
        ],
        input_output_aliases={7: 0},
        compiler_params=pltpu.CompilerParams(vmem_limit_bytes=32 * 2**20),
        name="edges",
    )(far, near, edge, arm, basis, basis, part, image)
    if halved:
        got = lax.ppermute(send, "col", [(0, 1), (1, 0)])
        keep = pl.pallas_call(
            keep_kernel,
            out_shape=jax.ShapeDtypeStruct((width, wide), f32),
            grid=(1,),
            in_specs=[*ends, whole(), whole()],
            out_specs=whole(),
            compiler_params=pltpu.CompilerParams(vmem_limit_bytes=32 * 2**20),
            cost_estimate=pl.CostEstimate(
                flops=4 * tile * width * width, bytes_accessed=2**21, transcendentals=0
            ),
            name="kept_half",
        )(basis, basis, rows, part)
        total = (keep + got.astype(f32)).astype(bf16)
        total = total.reshape(down, width // down, width // across)
        got = lax.all_to_all(total, "mesh", 0, 0, tiled=True)
    else:
        total = send.reshape(down, width // down, across, width // across)
        total = total.transpose(0, 2, 1, 3)
        total = total.reshape(count, width // down, width // across)
        got = lax.all_to_all(total, AXES, 0, 0, tiled=True)
    projected = jnp.sum(got.astype(f32), axis=0) * (1.0 / (nrows * count))
    return (image, projected)


def solution(mesh):
    return jax.shard_map(
        local,
        mesh=mesh,
        in_specs=(
            P(AXES, None),
            P(AXES, None, None, None),
            P(AXES, None),
            P(AXES),
            P(AXES),
        ),
        out_specs=(P(AXES, None), P("mesh", "col")),
        check_vma=False,
    )
```

```python
import functools

import jax
import jax.numpy as jnp
from jax import lax
from jax.experimental import pallas as pl
from jax.experimental.pallas import tpu as pltpu
from jax.sharding import PartitionSpec as P

REACH = 2
AXES = ("outer", "inner", "col")
ROWS_DOT = (((0,), (0,)), ((), ()))


def strip_of(cols_ref, live_ref, jac_ref, acc_ref, first, pair):
    _, slots, bsize, _ = jac_ref.shape
    tile = 2 * bsize
    half = lax.broadcasted_iota(jnp.int32, (1, tile), 1) // bsize
    row = lax.broadcasted_iota(jnp.int32, (bsize, tile), 0)
    lane = lax.broadcasted_iota(jnp.int32, (bsize, tile), 1)
    weight = acc_ref[pair : pair + 1, :]
    halves = []
    for side in range(2):
        g = 2 * pair + side
        tiles = [None, jnp.where(lane == row + side * bsize, weight, 0.0), None]
        for s in range(slots):
            place = cols_ref[s, g] - (first + 2 * pair) + REACH
            place = jnp.where(s < live_ref[g], place, -1)
            block = jac_ref[g, s]
            wide = jnp.concatenate([block, block], axis=1).astype(jnp.float32)
            for t in range(3):
                here = jnp.where(half + 2 * t == place, 1.0, 0.0)
                term = wide * here
                tiles[t] = term if tiles[t] is None else tiles[t] + term
        halves.append(jnp.concatenate(tiles, axis=1))
    strip = jnp.concatenate(halves, axis=0)
    high = strip.astype(jnp.bfloat16)
    low = (strip - high.astype(jnp.float32)).astype(jnp.bfloat16)
    return jnp.concatenate([high, low], axis=0)


def gathered_rows(cols_ref, live_ref, jac_ref, basis_ref, first, g):
    nblk, slots, bsize, _ = jac_ref.shape
    lane = lax.broadcasted_iota(jnp.int32, (1, slots * bsize), 1)
    keep = jnp.where(lane < live_ref[g] * bsize, 1.0, 0.0).astype(jnp.bfloat16)
    blocks = jnp.concatenate([jac_ref[g, s] for s in range(slots)], axis=1) * keep
    rows = []
    for s in range(slots):
        at = jnp.clip(cols_ref[s, g] - first, 0, nblk - 1) * bsize
        rows.append(basis_ref[pl.ds(pl.multiple_of(at, bsize), bsize), :])
    rows = jnp.concatenate(rows, axis=0)
    return jnp.dot(blocks, rows, preferred_element_type=jnp.float32)


def apply_strip(strip, rows):
    both = jnp.dot(strip, rows, preferred_element_type=jnp.float32)
    half = strip.shape[0] // 2
    return both[:half] + both[half:]


def slice_kernel(basis_hbm, far_ref, near_ref, sems):
    tile = far_ref.shape[0]
    last = basis_hbm.shape[0] - tile
    odd = lax.rem(lax.axis_index(AXES), 2)
    copies = []
    for i, (at, target) in enumerate(((odd, far_ref), (1 - odd, near_ref))):
        where = pl.ds(pl.multiple_of(at * last, tile), tile)
        copies.append(pltpu.make_async_copy(basis_hbm.at[where], target, sems.at[i]))
        copies[i].start()
    for copy in copies:
        copy.wait()


def inner_kernel(
    cols_ref, live_ref, jac_ref, basis_ref, acc_ref,
    image_ref, edge_ref, arm_ref, part_ref, staged, sems,
):
    nblk, _, bsize, _ = jac_ref.shape
    nrows = basis_ref.shape[0]
    tile = 2 * bsize
    pairs = nblk // 2
    first = lax.axis_index(AXES) * nblk

    def project(start, stop):
        total = lax.dot_general(
            basis_ref[start:stop, :], staged[start:stop, :], ROWS_DOT,
            preferred_element_type=jnp.float32,
        )
        parts, _, wide = part_ref.shape
        return [total[:, i * wide : (i + 1) * wide] for i in range(parts)]

    def store(start, stop, at):
        where = pl.ds(start, stop - start)
        copy = pltpu.make_async_copy(staged.at[where], image_ref.at[where], sems.at[at])
        copy.start()
        return copy

    row = lax.broadcasted_iota(jnp.int32, (tile, tile), 0)
    lane = lax.broadcasted_iota(jnp.int32, (tile, tile), 1)
    middle = (pairs // 2) * tile
    stored = tile
    copies = []
    for pair in range(1, pairs - 1):
        start = pair * tile
        stop = start + tile
        weight = jnp.where(lane == row, acc_ref[pair : pair + 1, :], 0.0)
        weight = jnp.sum(weight, axis=1, keepdims=True)
        coupled = [
            gathered_rows(cols_ref, live_ref, jac_ref, basis_ref, first, 2 * pair + side)
            for side in range(2)
        ]
        own = basis_ref[start:stop, :].astype(jnp.float32)
        total = jnp.concatenate(coupled, axis=0) + weight * own
        staged[start:stop, :] = total.astype(jnp.bfloat16)
        if pair % 3 == 0 or pair == pairs - 2:
            copies.append(store(stored, stop, len(copies)))
            stored = stop
        if stop == middle:
            for i, half in enumerate(project(tile, middle)):
                part_ref[i] = half
    for side, pair in enumerate((0, pairs - 1)):
        strip = strip_of(cols_ref, live_ref, jac_ref, acc_ref, first, pair)
        if side == 0:
            edge_ref[0] = apply_strip(strip[:, tile:], basis_ref[: 2 * tile, :])
            arm_ref[0] = strip[:, :tile]
        else:
            edge_ref[1] = apply_strip(strip[:, : 2 * tile], basis_ref[nrows - 2 * tile :, :])
            arm_ref[1] = strip[:, 2 * tile :]
    for i, half in enumerate(project(middle, nrows - tile)):
        part_ref[i] += half
    for copy in copies:
        copy.wait()


def add_edges(part_ref, tiles, rows_ref, half):
    update = lax.dot_general(
        tiles, rows_ref[half], ROWS_DOT, preferred_element_type=jnp.float32
    )
    return part_ref[half] + update


def put_blocks(ref, value, order):
    if order is None:
        ref[...] = value.astype(ref.dtype)
        return
    high = value.shape[0] // len(order)
    for to, source in enumerate(order):
        block = value[source * high : (source + 1) * high, :]
        ref[to * high : (to + 1) * high, :] = block.astype(ref.dtype)


def leaving_half(parts):
    return 1 - lax.axis_index("col") if parts == 2 else 0


def edge_kernel(
    order, far_ref, near_ref, edge_ref, arm_ref, top_ref, bottom_ref, part_ref, _,
    image_ref, rows_ref, send_ref, staged, sems,
):
    tile = top_ref.shape[0]
    nrows = image_ref.shape[0]
    parts, _, wide = rows_ref.shape
    odd = lax.rem(lax.axis_index(AXES), 2) == 1
    near, far = near_ref[...], far_ref[...]
    halos = (jnp.where(odd, near, far), jnp.where(odd, far, near))
    copies = []
    for side in range(2):
        rows = edge_ref[side] + apply_strip(arm_ref[side], halos[side])
        rows = rows.astype(jnp.bfloat16)
        staged[side] = rows
        for i in range(parts):
            rows_ref[i, side * tile : (side + 1) * tile, :] = rows[:, i * wide : (i + 1) * wide]
        where = pl.ds(0 if side == 0 else nrows - tile, tile)
        copy = pltpu.make_async_copy(staged.at[side], image_ref.at[where], sems.at[side])
        copy.start()
        copies.append(copy)
    tiles = jnp.concatenate([top_ref[...], bottom_ref[...]], axis=0)
    send = add_edges(part_ref, tiles, rows_ref, leaving_half(parts))
    put_blocks(send_ref, send, order)
    for copy in copies:
        copy.wait()


def keep_kernel(order, top_ref, bottom_ref, rows_ref, part_ref, keep_ref):
    tiles = jnp.concatenate([top_ref[...], bottom_ref[...]], axis=0)
    keep = add_edges(part_ref, tiles, rows_ref, 1 - leaving_half(2))
    put_blocks(keep_ref, keep, order)


def whole(memory_space=pltpu.VMEM):
    return pl.BlockSpec(memory_space=memory_space)


def local(basis, jac_blocks, block_cols, live_slots, accumulation):
    nrows, width = basis.shape
    nblk, slots, bsize, _ = jac_blocks.shape
    tile = 2 * bsize
    outer, inner, across = (lax.axis_size(axis) for axis in AXES)
    down = outer * inner
    count = down * across
    f32, bf16 = jnp.float32, jnp.bfloat16
    edge_shape = jax.ShapeDtypeStruct((tile, width), bf16)
    far_send, near_send = pl.pallas_call(
        slice_kernel,
        out_shape=(edge_shape, edge_shape),
        in_specs=[whole(pltpu.HBM)],
        out_specs=(whole(), whole()),
        scratch_shapes=[pltpu.SemaphoreType.DMA((2,))],
        compiler_params=pltpu.CompilerParams(vmem_limit_bytes=4 * 2**20),
        cost_estimate=pl.CostEstimate(
            flops=2 * nrows * width * width * slots, bytes_accessed=0, transcendentals=0
        ),
        name="halo_rows",
    )(pltpu.with_memory_space_constraint(basis, pltpu.HBM))
    swaps = [(i, i + 1) for i in range(1, count - 1, 2)]
    far = lax.ppermute(far_send, AXES, swaps + [(j, i) for i, j in swaps])
    swaps = [(i, i + 1) for i in range(0, count, 2)]
    near = lax.ppermute(near_send, AXES, swaps + [(j, i) for i, j in swaps])

    halved = across == 2
    parts = 2 if halved else 1
    wide = width // parts
    order = None
    if halved and (width // down) % 16 == 0:
        order = [o * inner + i for i in range(inner) for o in range(outer)]
    image, edge, arm, part = pl.pallas_call(
        inner_kernel,
        out_shape=(
            jax.ShapeDtypeStruct((nrows, width), bf16),
            jax.ShapeDtypeStruct((2, tile, width), f32),
            jax.ShapeDtypeStruct((2, 2 * tile, tile), bf16),
            jax.ShapeDtypeStruct((parts, width, wide), f32),
        ),
        in_specs=[whole(pltpu.SMEM), whole(pltpu.SMEM), whole(), whole(), whole()],
        out_specs=(whole(pltpu.HBM), whole(), whole(), whole()),
        scratch_shapes=[
            pltpu.VMEM((nrows, width), bf16),
            pltpu.SemaphoreType.DMA((nblk // 6 + 1,)),
        ],
        compiler_params=pltpu.CompilerParams(vmem_limit_bytes=32 * 2**20),
        cost_estimate=pl.CostEstimate(
            flops=2 * nrows * width * (width + 12 * bsize),
            bytes_accessed=8 * 2**20,
            transcendentals=0,
        ),
        name="inner",
    )(
        block_cols.T,
        live_slots,
        jac_blocks,
        basis,
        accumulation.reshape(nblk // 2, tile),
    )

    ends = [
        pl.BlockSpec((tile, width), lambda i: (0, 0)),
        pl.BlockSpec((tile, width), lambda i: (nrows // tile - 1, 0)),
    ]
    image, rows, send = pl.pallas_call(
        functools.partial(edge_kernel, order),
        out_shape=(
            jax.ShapeDtypeStruct((nrows, width), bf16),
            jax.ShapeDtypeStruct((parts, 2 * tile, wide), bf16),
            jax.ShapeDtypeStruct((width, wide), bf16),
        ),
        grid=(1,),
        in_specs=[whole(), whole(), whole(), whole(), *ends, whole(), whole(pl.ANY)],
        out_specs=(whole(pl.ANY), whole(), whole()),
        scratch_shapes=[
            pltpu.VMEM((2, tile, width), bf16),
            pltpu.SemaphoreType.DMA((2,)),
        ],
        input_output_aliases={7: 0},
        compiler_params=pltpu.CompilerParams(vmem_limit_bytes=32 * 2**20),
        name="edges",
    )(far, near, edge, arm, basis, basis, part, image)
    if halved:
        got = lax.ppermute(send, "col", [(0, 1), (1, 0)])
        keep = pl.pallas_call(
            functools.partial(keep_kernel, order),
            out_shape=jax.ShapeDtypeStruct((width, wide), f32),
            grid=(1,),
            in_specs=[*ends, whole(), whole()],
            out_specs=whole(),
            compiler_params=pltpu.CompilerParams(vmem_limit_bytes=32 * 2**20),
            cost_estimate=pl.CostEstimate(
                flops=4 * tile * width * width, bytes_accessed=2**21, transcendentals=0
            ),
            name="kept_half",
        )(basis, basis, rows, part)
        total = (keep + got.astype(f32)).astype(bf16)
        total = total.reshape(down, width // down, wide)
        group = AXES[:2] if order is None else (AXES[1], AXES[0])
        got = lax.all_to_all(total, group, 0, 0, tiled=True)
    else:
        total = send.reshape(down, width // down, across, width // across)
        total = total.transpose(0, 2, 1, 3)
        total = total.reshape(count, width // down, width // across)
        got = lax.all_to_all(total, AXES, 0, 0, tiled=True)
    projected = jnp.sum(got.astype(f32), axis=0) * (1.0 / (nrows * count))
    return (image, projected)


def solution(mesh):
    rows, cols = mesh.devices.shape
    outer = 4 if rows % 4 == 0 else 1
    split = jax.sharding.Mesh(mesh.devices.reshape(outer, rows // outer, cols), AXES)
    return jax.shard_map(
        local,
        mesh=split,
        in_specs=(
            P(AXES, None),
            P(AXES, None, None, None),
            P(AXES, None),
            P(AXES),
            P(AXES),
        ),
        out_specs=(P(AXES, None), P(AXES[:2], "col")),
        check_vma=False,
    )
```

```python
import functools

import jax
import jax.numpy as jnp
from jax import lax
from jax.experimental import pallas as pl
from jax.experimental.pallas import tpu as pltpu
from jax.sharding import PartitionSpec as P

REACH = 2
AXES = ("outer", "inner", "col")
ROWS_DOT = (((0,), (0,)), ((), ()))


def strip_of(cols_ref, live_ref, jac_ref, acc_ref, first, pair):
    _, slots, bsize, _ = jac_ref.shape
    tile = 2 * bsize
    half = lax.broadcasted_iota(jnp.int32, (1, tile), 1) // bsize
    row = lax.broadcasted_iota(jnp.int32, (bsize, tile), 0)
    lane = lax.broadcasted_iota(jnp.int32, (bsize, tile), 1)
    weight = acc_ref[pair : pair + 1, :]
    halves = []
    for side in range(2):
        g = 2 * pair + side
        tiles = [None, jnp.where(lane == row + side * bsize, weight, 0.0), None]
        for s in range(slots):
            place = cols_ref[s, g] - (first + 2 * pair) + REACH
            place = jnp.where(s < live_ref[g], place, -1)
            block = jac_ref[g, s]
            wide = jnp.concatenate([block, block], axis=1).astype(jnp.float32)
            for t in range(3):
                here = jnp.where(half + 2 * t == place, 1.0, 0.0)
                term = wide * here
                tiles[t] = term if tiles[t] is None else tiles[t] + term
        halves.append(jnp.concatenate(tiles, axis=1))
    strip = jnp.concatenate(halves, axis=0)
    high = strip.astype(jnp.bfloat16)
    low = (strip - high.astype(jnp.float32)).astype(jnp.bfloat16)
    return jnp.concatenate([high, low], axis=0)


def gathered_rows(cols_ref, live_ref, jac_ref, basis_ref, first, g):
    nblk, slots, bsize, _ = jac_ref.shape
    lane = lax.broadcasted_iota(jnp.int32, (1, slots * bsize), 1)
    keep = jnp.where(lane < live_ref[g] * bsize, 1.0, 0.0).astype(jnp.bfloat16)
    blocks = jnp.concatenate([jac_ref[g, s] for s in range(slots)], axis=1) * keep
    rows = []
    for s in range(slots):
        at = jnp.clip(cols_ref[s, g] - first, 0, nblk - 1) * bsize
        rows.append(basis_ref[pl.ds(pl.multiple_of(at, bsize), bsize), :])
    rows = jnp.concatenate(rows, axis=0)
    return jnp.dot(blocks, rows, preferred_element_type=jnp.float32)


def apply_strip(strip, rows):
    both = jnp.dot(strip, rows, preferred_element_type=jnp.float32)
    half = strip.shape[0] // 2
    return both[:half] + both[half:]


def slice_kernel(basis_hbm, far_ref, near_ref, sems):
    tile = far_ref.shape[0]
    last = basis_hbm.shape[0] - tile
    odd = lax.rem(lax.axis_index(AXES), 2)
    copies = []
    for i, (at, target) in enumerate(((odd, far_ref), (1 - odd, near_ref))):
        where = pl.ds(pl.multiple_of(at * last, tile), tile)
        copies.append(pltpu.make_async_copy(basis_hbm.at[where], target, sems.at[i]))
        copies[i].start()
    for copy in copies:
        copy.wait()


def inner_kernel(
    cols_ref, live_ref, jac_ref, basis_ref, acc_ref,
    image_ref, edge_ref, arm_ref, part_ref, staged, sems,
):
    nblk, _, bsize, _ = jac_ref.shape
    nrows = basis_ref.shape[0]
    tile = 2 * bsize
    pairs = nblk // 2
    first = lax.axis_index(AXES) * nblk

    def project(start, stop):
        total = lax.dot_general(
            basis_ref[start:stop, :], staged[start:stop, :], ROWS_DOT,
            preferred_element_type=jnp.float32,
        )
        parts, _, wide = part_ref.shape
        return [total[:, i * wide : (i + 1) * wide] for i in range(parts)]

    def store(start, stop, at):
        where = pl.ds(start, stop - start)
        copy = pltpu.make_async_copy(staged.at[where], image_ref.at[where], sems.at[at])
        copy.start()
        return copy

    row = lax.broadcasted_iota(jnp.int32, (tile, tile), 0)
    lane = lax.broadcasted_iota(jnp.int32, (tile, tile), 1)
    middle = (pairs // 2) * tile
    stored = tile
    copies = []
    for pair in range(1, pairs - 1):
        start = pair * tile
        stop = start + tile
        weight = jnp.where(lane == row, acc_ref[pair : pair + 1, :], 0.0)
        weight = jnp.sum(weight, axis=1, keepdims=True)
        coupled = [
            gathered_rows(cols_ref, live_ref, jac_ref, basis_ref, first, 2 * pair + side)
            for side in range(2)
        ]
        own = basis_ref[start:stop, :].astype(jnp.float32)
        total = jnp.concatenate(coupled, axis=0) + weight * own
        staged[start:stop, :] = total.astype(jnp.bfloat16)
        if pair % 3 == 0 or pair == pairs - 2:
            copies.append(store(stored, stop, len(copies)))
            stored = stop
        if stop == middle:
            for i, half in enumerate(project(tile, middle)):
                part_ref[i] = half
    for side, pair in enumerate((0, pairs - 1)):
        strip = strip_of(cols_ref, live_ref, jac_ref, acc_ref, first, pair)
        if side == 0:
            edge_ref[0] = apply_strip(strip[:, tile:], basis_ref[: 2 * tile, :])
            arm_ref[0] = strip[:, :tile]
        else:
            edge_ref[1] = apply_strip(strip[:, : 2 * tile], basis_ref[nrows - 2 * tile :, :])
            arm_ref[1] = strip[:, 2 * tile :]
    for i, half in enumerate(project(middle, nrows - tile)):
        part_ref[i] += half
    for copy in copies:
        copy.wait()


def add_edges(part_ref, tiles, rows_ref, half):
    update = lax.dot_general(
        tiles, rows_ref[half], ROWS_DOT, preferred_element_type=jnp.float32
    )
    return part_ref[half] + update


def put_blocks(ref, value, order):
    if order == sorted(order):
        ref[...] = value.astype(ref.dtype)
        return
    high = value.shape[0] // len(order)
    for to, source in enumerate(order):
        block = value[source * high : (source + 1) * high, :]
        ref[to * high : (to + 1) * high, :] = block.astype(ref.dtype)


def leaving_half(parts):
    return 1 - lax.axis_index("col") if parts == 2 else 0


def edge_kernel(
    order, far_ref, near_ref, edge_ref, arm_ref, top_ref, bottom_ref, part_ref, _,
    image_ref, rows_ref, send_ref, staged, sems,
):
    tile = top_ref.shape[0]
    nrows = image_ref.shape[0]
    parts, _, wide = rows_ref.shape
    odd = lax.rem(lax.axis_index(AXES), 2) == 1
    near, far = near_ref[...], far_ref[...]
    halos = (jnp.where(odd, near, far), jnp.where(odd, far, near))
    copies = []
    for side in range(2):
        rows = edge_ref[side] + apply_strip(arm_ref[side], halos[side])
        rows = rows.astype(jnp.bfloat16)
        staged[side] = rows
        for i in range(parts):
            rows_ref[i, side * tile : (side + 1) * tile, :] = rows[:, i * wide : (i + 1) * wide]
        where = pl.ds(0 if side == 0 else nrows - tile, tile)
        copy = pltpu.make_async_copy(staged.at[side], image_ref.at[where], sems.at[side])
        copy.start()
        copies.append(copy)
    tiles = jnp.concatenate([top_ref[...], bottom_ref[...]], axis=0)
    send = add_edges(part_ref, tiles, rows_ref, leaving_half(parts))
    put_blocks(send_ref, send, order)
    for copy in copies:
        copy.wait()


def keep_kernel(order, top_ref, bottom_ref, rows_ref, part_ref, keep_ref):
    tiles = jnp.concatenate([top_ref[...], bottom_ref[...]], axis=0)
    keep = add_edges(part_ref, tiles, rows_ref, 1 - leaving_half(2))
    put_blocks(keep_ref, keep, order)


def whole(memory_space=pltpu.VMEM):
    return pl.BlockSpec(memory_space=memory_space)


def local(basis, jac_blocks, block_cols, live_slots, accumulation):
    nrows, width = basis.shape
    nblk, slots, bsize, _ = jac_blocks.shape
    tile = 2 * bsize
    outer, inner, across = (lax.axis_size(axis) for axis in AXES)
    down = outer * inner
    count = down * across
    f32, bf16 = jnp.float32, jnp.bfloat16
    edge_shape = jax.ShapeDtypeStruct((tile, width), bf16)
    far_send, near_send = pl.pallas_call(
        slice_kernel,
        out_shape=(edge_shape, edge_shape),
        in_specs=[whole(pltpu.HBM)],
        out_specs=(whole(), whole()),
        scratch_shapes=[pltpu.SemaphoreType.DMA((2,))],
        compiler_params=pltpu.CompilerParams(vmem_limit_bytes=4 * 2**20),
        cost_estimate=pl.CostEstimate(
            flops=2 * nrows * width * width * slots, bytes_accessed=0, transcendentals=0
        ),
        name="halo_rows",
    )(pltpu.with_memory_space_constraint(basis, pltpu.HBM))
    swaps = [(i, i + 1) for i in range(1, count - 1, 2)]
    far = lax.ppermute(far_send, AXES, swaps + [(j, i) for i, j in swaps])
    swaps = [(i, i + 1) for i in range(0, count, 2)]
    near = lax.ppermute(near_send, AXES, swaps + [(j, i) for i, j in swaps])

    halved = across == 2
    parts = 2 if halved else 1
    wide = width // parts
    order = list(range(down))
    if halved and (width // down) % 16 == 0:
        order = [o * inner + i for i in range(inner) for o in reversed(range(outer))]
    image, edge, arm, part = pl.pallas_call(
        inner_kernel,
        out_shape=(
            jax.ShapeDtypeStruct((nrows, width), bf16),
            jax.ShapeDtypeStruct((2, tile, width), f32),
            jax.ShapeDtypeStruct((2, 2 * tile, tile), bf16),
            jax.ShapeDtypeStruct((parts, width, wide), f32),
        ),
        in_specs=[whole(pltpu.SMEM), whole(pltpu.SMEM), whole(), whole(), whole()],
        out_specs=(whole(pltpu.HBM), whole(), whole(), whole()),
        scratch_shapes=[
            pltpu.VMEM((nrows, width), bf16),
            pltpu.SemaphoreType.DMA((nblk // 6 + 1,)),
        ],
        compiler_params=pltpu.CompilerParams(vmem_limit_bytes=32 * 2**20),
        cost_estimate=pl.CostEstimate(
            flops=2 * nrows * width * (width + 12 * bsize),
            bytes_accessed=8 * 2**20,
            transcendentals=0,
        ),
        name="inner",
    )(
        block_cols.T,
        live_slots,
        jac_blocks,
        basis,
        accumulation.reshape(nblk // 2, tile),
    )

    ends = [
        pl.BlockSpec((tile, width), lambda i: (0, 0)),
        pl.BlockSpec((tile, width), lambda i: (nrows // tile - 1, 0)),
    ]
    image, rows, send = pl.pallas_call(
        functools.partial(edge_kernel, order),
        out_shape=(
            jax.ShapeDtypeStruct((nrows, width), bf16),
            jax.ShapeDtypeStruct((parts, 2 * tile, wide), bf16),
            jax.ShapeDtypeStruct((width, wide), bf16),
        ),
        grid=(1,),
        in_specs=[whole(), whole(), whole(), whole(), *ends, whole(), whole(pl.ANY)],
        out_specs=(whole(pl.ANY), whole(), whole()),
        scratch_shapes=[
            pltpu.VMEM((2, tile, width), bf16),
            pltpu.SemaphoreType.DMA((2,)),
        ],
        input_output_aliases={7: 0},
        compiler_params=pltpu.CompilerParams(vmem_limit_bytes=32 * 2**20),
        name="edges",
    )(far, near, edge, arm, basis, basis, part, image)
    if halved:
        got = lax.ppermute(send, "col", [(0, 1), (1, 0)])
        keep = pl.pallas_call(
            functools.partial(keep_kernel, order),
            out_shape=jax.ShapeDtypeStruct((width, wide), f32),
            grid=(1,),
            in_specs=[*ends, whole(), whole()],
            out_specs=whole(),
            compiler_params=pltpu.CompilerParams(vmem_limit_bytes=32 * 2**20),
            cost_estimate=pl.CostEstimate(
                flops=4 * tile * width * width, bytes_accessed=2**21, transcendentals=0
            ),
            name="kept_half",
        )(basis, basis, rows, part)
        total = (keep + got.astype(f32)).astype(bf16)
        total = total.reshape(down, width // down, wide)
        groups = [[m * across + c for m in order] for c in range(across)]
        got = lax.all_to_all(total, AXES, 0, 0, axis_index_groups=groups, tiled=True)
    else:
        total = send.reshape(down, width // down, across, width // across)
        total = total.transpose(0, 2, 1, 3)
        total = total.reshape(count, width // down, width // across)
        got = lax.all_to_all(total, AXES, 0, 0, tiled=True)
    projected = jnp.sum(got.astype(f32), axis=0) * (1.0 / (nrows * count))
    return (image, projected)


def solution(mesh):
    rows, cols = mesh.devices.shape
    outer = 4 if rows % 4 == 0 else 1
    split = jax.sharding.Mesh(mesh.devices.reshape(outer, rows // outer, cols), AXES)
    return jax.shard_map(
        local,
        mesh=split,
        in_specs=(
            P(AXES, None),
            P(AXES, None, None, None),
            P(AXES, None),
            P(AXES),
            P(AXES),
        ),
        out_specs=(P(AXES, None), P(AXES[:2], "col")),
        check_vma=False,
    )
```

```python
import functools

import jax
import jax.numpy as jnp
from jax import lax
from jax.experimental import pallas as pl
from jax.experimental.pallas import tpu as pltpu
from jax.sharding import PartitionSpec as P

REACH = 2
AXES = ("outer", "inner", "col")
ROWS_DOT = (((0,), (0,)), ((), ()))


def strip_of(cols_ref, live_ref, jac_ref, acc_ref, first, pair):
    _, slots, bsize, _ = jac_ref.shape
    tile = 2 * bsize
    half = lax.broadcasted_iota(jnp.int32, (1, tile), 1) // bsize
    row = lax.broadcasted_iota(jnp.int32, (bsize, tile), 0)
    lane = lax.broadcasted_iota(jnp.int32, (bsize, tile), 1)
    weight = acc_ref[pair : pair + 1, :]
    halves = []
    for side in range(2):
        g = 2 * pair + side
        tiles = [None, jnp.where(lane == row + side * bsize, weight, 0.0), None]
        for s in range(slots):
            place = cols_ref[s, g] - (first + 2 * pair) + REACH
            place = jnp.where(s < live_ref[g], place, -1)
            block = jac_ref[g, s]
            wide = jnp.concatenate([block, block], axis=1).astype(jnp.float32)
            for t in range(3):
                here = jnp.where(half + 2 * t == place, 1.0, 0.0)
                term = wide * here
                tiles[t] = term if tiles[t] is None else tiles[t] + term
        halves.append(jnp.concatenate(tiles, axis=1))
    strip = jnp.concatenate(halves, axis=0)
    high = strip.astype(jnp.bfloat16)
    low = (strip - high.astype(jnp.float32)).astype(jnp.bfloat16)
    return jnp.concatenate([high, low], axis=0)


def gathered_rows(cols_ref, live_ref, jac_ref, basis_ref, first, g):
    nblk, slots, bsize, _ = jac_ref.shape
    lane = lax.broadcasted_iota(jnp.int32, (1, slots * bsize), 1)
    keep = jnp.where(lane < live_ref[g] * bsize, 1.0, 0.0).astype(jnp.bfloat16)
    blocks = jnp.concatenate([jac_ref[g, s] for s in range(slots)], axis=1) * keep
    rows = []
    for s in range(slots):
        at = jnp.clip(cols_ref[s, g] - first, 0, nblk - 1) * bsize
        rows.append(basis_ref[pl.ds(pl.multiple_of(at, bsize), bsize), :])
    rows = jnp.concatenate(rows, axis=0)
    return jnp.dot(blocks, rows, preferred_element_type=jnp.float32)


def apply_strip(strip, rows):
    both = jnp.dot(strip, rows, preferred_element_type=jnp.float32)
    half = strip.shape[0] // 2
    return both[:half] + both[half:]


def slice_kernel(basis_hbm, far_ref, near_ref, sems):
    tile = far_ref.shape[0]
    last = basis_hbm.shape[0] - tile
    odd = lax.rem(lax.axis_index(AXES), 2)
    copies = []
    for i, (at, target) in enumerate(((odd, far_ref), (1 - odd, near_ref))):
        where = pl.ds(pl.multiple_of(at * last, tile), tile)
        copies.append(pltpu.make_async_copy(basis_hbm.at[where], target, sems.at[i]))
        copies[i].start()
    for copy in copies:
        copy.wait()


def inner_kernel(
    cols_ref, live_ref, jac_ref, basis_ref, acc_ref,
    image_ref, edge_ref, arm_ref, part_ref, staged, sems,
):
    nblk, _, bsize, _ = jac_ref.shape
    nrows = basis_ref.shape[0]
    tile = 2 * bsize
    pairs = nblk // 2
    first = lax.axis_index(AXES) * nblk

    def project(start, stop):
        total = lax.dot_general(
            basis_ref[start:stop, :], staged[start:stop, :], ROWS_DOT,
            preferred_element_type=jnp.float32,
        )
        parts, _, wide = part_ref.shape
        return [total[:, i * wide : (i + 1) * wide] for i in range(parts)]

    def store(start, stop, at):
        where = pl.ds(start, stop - start)
        copy = pltpu.make_async_copy(staged.at[where], image_ref.at[where], sems.at[at])
        copy.start()
        return copy

    row = lax.broadcasted_iota(jnp.int32, (tile, tile), 0)
    lane = lax.broadcasted_iota(jnp.int32, (tile, tile), 1)
    middle = (pairs // 2) * tile
    stored = tile
    copies = []
    for pair in range(1, pairs - 1):
        start = pair * tile
        stop = start + tile
        weight = jnp.where(lane == row, acc_ref[pair : pair + 1, :], 0.0)
        weight = jnp.sum(weight, axis=1, keepdims=True)
        coupled = [
            gathered_rows(cols_ref, live_ref, jac_ref, basis_ref, first, 2 * pair + side)
            for side in range(2)
        ]
        own = basis_ref[start:stop, :].astype(jnp.float32)
        total = jnp.concatenate(coupled, axis=0) + weight * own
        staged[start:stop, :] = total.astype(jnp.bfloat16)
        if pair % 3 == 0 or pair == pairs - 2:
            copies.append(store(stored, stop, len(copies)))
            stored = stop
        if stop == middle:
            for i, half in enumerate(project(tile, middle)):
                part_ref[i] = half
    for side, pair in enumerate((0, pairs - 1)):
        strip = strip_of(cols_ref, live_ref, jac_ref, acc_ref, first, pair)
        if side == 0:
            edge_ref[0] = apply_strip(strip[:, tile:], basis_ref[: 2 * tile, :])
            arm_ref[0] = strip[:, :tile]
        else:
            edge_ref[1] = apply_strip(strip[:, : 2 * tile], basis_ref[nrows - 2 * tile :, :])
            arm_ref[1] = strip[:, 2 * tile :]
    for i, half in enumerate(project(middle, nrows - tile)):
        part_ref[i] += half
    for copy in copies:
        copy.wait()


def add_edges(part_ref, tiles, rows_ref, half):
    update = lax.dot_general(
        tiles, rows_ref[half], ROWS_DOT, preferred_element_type=jnp.float32
    )
    return part_ref[half] + update


def put_blocks(ref, value, order):
    if order == sorted(order):
        ref[...] = value.astype(ref.dtype)
        return
    high = value.shape[0] // len(order)
    for to, source in enumerate(order):
        block = value[source * high : (source + 1) * high, :]
        ref[to * high : (to + 1) * high, :] = block.astype(ref.dtype)


def leaving_half(parts):
    return 1 - lax.axis_index("col") if parts == 2 else 0


def edge_kernel(
    order, far_ref, near_ref, edge_ref, arm_ref, top_ref, bottom_ref, part_ref, _,
    image_ref, rows_ref, send_ref, staged, sems,
):
    tile = top_ref.shape[0]
    nrows = image_ref.shape[0]
    parts, _, wide = rows_ref.shape
    odd = lax.rem(lax.axis_index(AXES), 2) == 1
    near, far = near_ref[...], far_ref[...]
    halos = (jnp.where(odd, near, far), jnp.where(odd, far, near))
    copies = []
    for side in range(2):
        rows = edge_ref[side] + apply_strip(arm_ref[side], halos[side])
        rows = rows.astype(jnp.bfloat16)
        staged[side] = rows
        for i in range(parts):
            rows_ref[i, side * tile : (side + 1) * tile, :] = rows[:, i * wide : (i + 1) * wide]
        where = pl.ds(0 if side == 0 else nrows - tile, tile)
        copy = pltpu.make_async_copy(staged.at[side], image_ref.at[where], sems.at[side])
        copy.start()
        copies.append(copy)
    tiles = jnp.concatenate([top_ref[...], bottom_ref[...]], axis=0)
    send = add_edges(part_ref, tiles, rows_ref, leaving_half(parts))
    put_blocks(send_ref, send, order)
    for copy in copies:
        copy.wait()


def keep_kernel(order, top_ref, bottom_ref, rows_ref, part_ref, keep_ref):
    tiles = jnp.concatenate([top_ref[...], bottom_ref[...]], axis=0)
    keep = add_edges(part_ref, tiles, rows_ref, 1 - leaving_half(2))
    put_blocks(keep_ref, keep, order)


def whole(memory_space=pltpu.VMEM):
    return pl.BlockSpec(memory_space=memory_space)


def local(basis, jac_blocks, block_cols, live_slots, accumulation):
    nrows, width = basis.shape
    nblk, slots, bsize, _ = jac_blocks.shape
    tile = 2 * bsize
    outer, inner, across = (lax.axis_size(axis) for axis in AXES)
    down = outer * inner
    count = down * across
    f32, bf16 = jnp.float32, jnp.bfloat16
    edge_shape = jax.ShapeDtypeStruct((tile, width), bf16)
    far_send, near_send = pl.pallas_call(
        slice_kernel,
        out_shape=(edge_shape, edge_shape),
        in_specs=[whole(pltpu.HBM)],
        out_specs=(whole(), whole()),
        scratch_shapes=[pltpu.SemaphoreType.DMA((2,))],
        compiler_params=pltpu.CompilerParams(vmem_limit_bytes=4 * 2**20),
        cost_estimate=pl.CostEstimate(
            flops=2 * nrows * width * width * slots, bytes_accessed=0, transcendentals=0
        ),
        name="halo_rows",
    )(pltpu.with_memory_space_constraint(basis, pltpu.HBM))
    swaps = [(i, i + 1) for i in range(1, count - 1, 2)]
    far = lax.ppermute(far_send, AXES, swaps + [(j, i) for i, j in swaps])
    swaps = [(i, i + 1) for i in range(0, count, 2)]
    near = lax.ppermute(near_send, AXES, swaps + [(j, i) for i, j in swaps])

    halved = across == 2
    parts = 2 if halved else 1
    wide = width // parts
    order = list(range(down))
    if halved and (width // down) % 16 == 0:
        order = [o * inner + i for i in reversed(range(inner)) for o in reversed(range(outer))]
    image, edge, arm, part = pl.pallas_call(
        inner_kernel,
        out_shape=(
            jax.ShapeDtypeStruct((nrows, width), bf16),
            jax.ShapeDtypeStruct((2, tile, width), f32),
            jax.ShapeDtypeStruct((2, 2 * tile, tile), bf16),
            jax.ShapeDtypeStruct((parts, width, wide), f32),
        ),
        in_specs=[whole(pltpu.SMEM), whole(pltpu.SMEM), whole(), whole(), whole()],
        out_specs=(whole(pltpu.HBM), whole(), whole(), whole()),
        scratch_shapes=[
            pltpu.VMEM((nrows, width), bf16),
            pltpu.SemaphoreType.DMA((nblk // 6 + 1,)),
        ],
        compiler_params=pltpu.CompilerParams(vmem_limit_bytes=32 * 2**20),
        cost_estimate=pl.CostEstimate(
            flops=2 * nrows * width * (width + 12 * bsize),
            bytes_accessed=8 * 2**20,
            transcendentals=0,
        ),
        name="inner",
    )(
        block_cols.T,
        live_slots,
        jac_blocks,
        basis,
        accumulation.reshape(nblk // 2, tile),
    )

    ends = [
        pl.BlockSpec((tile, width), lambda i: (0, 0)),
        pl.BlockSpec((tile, width), lambda i: (nrows // tile - 1, 0)),
    ]
    image, rows, send = pl.pallas_call(
        functools.partial(edge_kernel, order),
        out_shape=(
            jax.ShapeDtypeStruct((nrows, width), bf16),
            jax.ShapeDtypeStruct((parts, 2 * tile, wide), bf16),
            jax.ShapeDtypeStruct((width, wide), bf16),
        ),
        grid=(1,),
        in_specs=[whole(), whole(), whole(), whole(), *ends, whole(), whole(pl.ANY)],
        out_specs=(whole(pl.ANY), whole(), whole()),
        scratch_shapes=[
            pltpu.VMEM((2, tile, width), bf16),
            pltpu.SemaphoreType.DMA((2,)),
        ],
        input_output_aliases={7: 0},
        compiler_params=pltpu.CompilerParams(vmem_limit_bytes=32 * 2**20),
        name="edges",
    )(far, near, edge, arm, basis, basis, part, image)
    if halved:
        got = lax.ppermute(send, "col", [(0, 1), (1, 0)])
        keep = pl.pallas_call(
            functools.partial(keep_kernel, order),
            out_shape=jax.ShapeDtypeStruct((width, wide), f32),
            grid=(1,),
            in_specs=[*ends, whole(), whole()],
            out_specs=whole(),
            compiler_params=pltpu.CompilerParams(vmem_limit_bytes=32 * 2**20),
            cost_estimate=pl.CostEstimate(
                flops=4 * tile * width * width, bytes_accessed=2**21, transcendentals=0
            ),
            name="kept_half",
        )(basis, basis, rows, part)
        total = (keep + got.astype(f32)).astype(bf16)
        total = total.reshape(down, width // down, wide)
        groups = [[m * across + c for m in order] for c in range(across)]
        got = lax.all_to_all(total, AXES, 0, 0, axis_index_groups=groups, tiled=True)
    else:
        total = send.reshape(down, width // down, across, width // across)
        total = total.transpose(0, 2, 1, 3)
        total = total.reshape(count, width // down, width // across)
        got = lax.all_to_all(total, AXES, 0, 0, tiled=True)
    projected = jnp.sum(got.astype(f32), axis=0) * (1.0 / (nrows * count))
    return (image, projected)


def solution(mesh):
    rows, cols = mesh.devices.shape
    outer = 4 if rows % 4 == 0 else 1
    split = jax.sharding.Mesh(mesh.devices.reshape(outer, rows // outer, cols), AXES)
    return jax.shard_map(
        local,
        mesh=split,
        in_specs=(
            P(AXES, None),
            P(AXES, None, None, None),
            P(AXES, None),
            P(AXES),
            P(AXES),
        ),
        out_specs=(P(AXES, None), P(AXES[:2], "col")),
        check_vma=False,
    )
```

```python
import functools

import jax
import jax.numpy as jnp
from jax import lax
from jax.experimental import pallas as pl
from jax.experimental.pallas import tpu as pltpu
from jax.sharding import PartitionSpec as P

REACH = 2
AXES = ("outer", "inner", "col")
ROWS_DOT = (((0,), (0,)), ((), ()))


def strip_of(cols_ref, live_ref, jac_ref, acc_ref, first, pair):
    _, slots, bsize, _ = jac_ref.shape
    tile = 2 * bsize
    half = lax.broadcasted_iota(jnp.int32, (1, tile), 1) // bsize
    row = lax.broadcasted_iota(jnp.int32, (bsize, tile), 0)
    lane = lax.broadcasted_iota(jnp.int32, (bsize, tile), 1)
    weight = acc_ref[pair : pair + 1, :]
    halves = []
    for side in range(2):
        g = 2 * pair + side
        tiles = [None, jnp.where(lane == row + side * bsize, weight, 0.0), None]
        for s in range(slots):
            place = cols_ref[s, g] - (first + 2 * pair) + REACH
            place = jnp.where(s < live_ref[g], place, -1)
            block = jac_ref[g, s]
            wide = jnp.concatenate([block, block], axis=1).astype(jnp.float32)
            for t in range(3):
                here = jnp.where(half + 2 * t == place, 1.0, 0.0)
                term = wide * here
                tiles[t] = term if tiles[t] is None else tiles[t] + term
        halves.append(jnp.concatenate(tiles, axis=1))
    strip = jnp.concatenate(halves, axis=0)
    high = strip.astype(jnp.bfloat16)
    low = (strip - high.astype(jnp.float32)).astype(jnp.bfloat16)
    return jnp.concatenate([high, low], axis=0)


def gathered_rows(cols_ref, live_ref, jac_ref, basis_ref, first, g):
    nblk, slots, bsize, _ = jac_ref.shape
    lane = lax.broadcasted_iota(jnp.int32, (1, slots * bsize), 1)
    keep = jnp.where(lane < live_ref[g] * bsize, 1.0, 0.0).astype(jnp.bfloat16)
    blocks = jnp.concatenate([jac_ref[g, s] for s in range(slots)], axis=1) * keep
    rows = []
    for s in range(slots):
        at = jnp.clip(cols_ref[s, g] - first, 0, nblk - 1) * bsize
        rows.append(basis_ref[pl.ds(pl.multiple_of(at, bsize), bsize), :])
    rows = jnp.concatenate(rows, axis=0)
    return jnp.dot(blocks, rows, preferred_element_type=jnp.float32)


def apply_strip(strip, rows):
    both = jnp.dot(strip, rows, preferred_element_type=jnp.float32)
    half = strip.shape[0] // 2
    return both[:half] + both[half:]


def slice_kernel(basis_hbm, far_ref, near_ref, sems):
    tile = far_ref.shape[0]
    last = basis_hbm.shape[0] - tile
    odd = lax.rem(lax.axis_index(AXES), 2)
    copies = []
    for i, (at, target) in enumerate(((odd, far_ref), (1 - odd, near_ref))):
        where = pl.ds(pl.multiple_of(at * last, tile), tile)
        copies.append(pltpu.make_async_copy(basis_hbm.at[where], target, sems.at[i]))
        copies[i].start()
    for copy in copies:
        copy.wait()


def inner_kernel(
    cols_ref, live_ref, jac_ref, basis_ref, acc_ref,
    image_ref, edge_ref, arm_ref, part_ref, staged, sems,
):
    nblk, _, bsize, _ = jac_ref.shape
    nrows = basis_ref.shape[0]
    tile = 2 * bsize
    pairs = nblk // 2
    first = lax.axis_index(AXES) * nblk

    def project(start, stop):
        total = lax.dot_general(
            basis_ref[start:stop, :], staged[start:stop, :], ROWS_DOT,
            preferred_element_type=jnp.float32,
        )
        parts, _, wide = part_ref.shape
        return [total[:, i * wide : (i + 1) * wide] for i in range(parts)]

    def store(start, stop, at):
        where = pl.ds(start, stop - start)
        copy = pltpu.make_async_copy(staged.at[where], image_ref.at[where], sems.at[at])
        copy.start()
        return copy

    row = lax.broadcasted_iota(jnp.int32, (tile, tile), 0)
    lane = lax.broadcasted_iota(jnp.int32, (tile, tile), 1)
    middle = (pairs // 2) * tile
    stored = tile
    copies = []
    for pair in range(1, pairs - 1):
        start = pair * tile
        stop = start + tile
        weight = jnp.where(lane == row, acc_ref[pair : pair + 1, :], 0.0)
        weight = jnp.sum(weight, axis=1, keepdims=True)
        coupled = [
            gathered_rows(cols_ref, live_ref, jac_ref, basis_ref, first, 2 * pair + side)
            for side in range(2)
        ]
        own = basis_ref[start:stop, :].astype(jnp.float32)
        total = jnp.concatenate(coupled, axis=0) + weight * own
        staged[start:stop, :] = total.astype(jnp.bfloat16)
        if pair % 3 == 0 or pair == pairs - 2:
            copies.append(store(stored, stop, len(copies)))
            stored = stop
        if stop == middle:
            for i, half in enumerate(project(tile, middle)):
                part_ref[i] = half
    for side, pair in enumerate((0, pairs - 1)):
        strip = strip_of(cols_ref, live_ref, jac_ref, acc_ref, first, pair)
        if side == 0:
            edge_ref[0] = apply_strip(strip[:, tile:], basis_ref[: 2 * tile, :])
            arm_ref[0] = strip[:, :tile]
        else:
            edge_ref[1] = apply_strip(strip[:, : 2 * tile], basis_ref[nrows - 2 * tile :, :])
            arm_ref[1] = strip[:, 2 * tile :]
    for i, half in enumerate(project(middle, nrows - tile)):
        part_ref[i] += half
    for copy in copies:
        copy.wait()


def add_edges(part_ref, tiles, rows_ref, half):
    update = lax.dot_general(
        tiles, rows_ref[half], ROWS_DOT, preferred_element_type=jnp.float32
    )
    return part_ref[half] + update


def put_blocks(ref, value, order):
    if order == sorted(order):
        ref[...] = value.astype(ref.dtype)
        return
    high = value.shape[0] // len(order)
    for to, source in enumerate(order):
        block = value[source * high : (source + 1) * high, :]
        ref[to * high : (to + 1) * high, :] = block.astype(ref.dtype)


def leaving_half(parts):
    return 1 - lax.axis_index("col") if parts == 2 else 0


def edge_kernel(
    order, far_ref, near_ref, edge_ref, arm_ref, top_ref, bottom_ref, part_ref, _,
    image_ref, rows_ref, send_ref, staged, sems,
):
    tile = top_ref.shape[0]
    nrows = image_ref.shape[0]
    parts, _, wide = rows_ref.shape
    odd = lax.rem(lax.axis_index(AXES), 2) == 1
    near, far = near_ref[...], far_ref[...]
    halos = (jnp.where(odd, near, far), jnp.where(odd, far, near))
    copies = []
    for side in range(2):
        rows = edge_ref[side] + apply_strip(arm_ref[side], halos[side])
        rows = rows.astype(jnp.bfloat16)
        staged[side] = rows
        for i in range(parts):
            rows_ref[i, side * tile : (side + 1) * tile, :] = rows[:, i * wide : (i + 1) * wide]
        where = pl.ds(0 if side == 0 else nrows - tile, tile)
        copy = pltpu.make_async_copy(staged.at[side], image_ref.at[where], sems.at[side])
        copy.start()
        copies.append(copy)
    tiles = jnp.concatenate([top_ref[...], bottom_ref[...]], axis=0)
    send = add_edges(part_ref, tiles, rows_ref, leaving_half(parts))
    put_blocks(send_ref, send, order)
    for copy in copies:
        copy.wait()


def keep_kernel(order, top_ref, bottom_ref, rows_ref, part_ref, keep_ref):
    tiles = jnp.concatenate([top_ref[...], bottom_ref[...]], axis=0)
    keep = add_edges(part_ref, tiles, rows_ref, 1 - leaving_half(2))
    put_blocks(keep_ref, keep, order)


def whole(memory_space=pltpu.VMEM):
    return pl.BlockSpec(memory_space=memory_space)


def local(basis, jac_blocks, block_cols, live_slots, accumulation):
    nrows, width = basis.shape
    nblk, slots, bsize, _ = jac_blocks.shape
    tile = 2 * bsize
    outer, inner, across = (lax.axis_size(axis) for axis in AXES)
    down = outer * inner
    count = down * across
    f32, bf16 = jnp.float32, jnp.bfloat16
    edge_shape = jax.ShapeDtypeStruct((tile, width), bf16)
    far_send, near_send = pl.pallas_call(
        slice_kernel,
        out_shape=(edge_shape, edge_shape),
        in_specs=[whole(pltpu.HBM)],
        out_specs=(whole(), whole()),
        scratch_shapes=[pltpu.SemaphoreType.DMA((2,))],
        compiler_params=pltpu.CompilerParams(vmem_limit_bytes=4 * 2**20),
        cost_estimate=pl.CostEstimate(
            flops=2 * nrows * width * width * slots, bytes_accessed=0, transcendentals=0
        ),
        name="halo_rows",
    )(pltpu.with_memory_space_constraint(basis, pltpu.HBM))
    swaps = [(i, i + 1) for i in range(1, count - 1, 2)]
    far = lax.ppermute(far_send, AXES, swaps + [(j, i) for i, j in swaps])
    swaps = [(i, i + 1) for i in range(0, count, 2)]
    near = lax.ppermute(near_send, AXES, swaps + [(j, i) for i, j in swaps])

    halved = across == 2
    parts = 2 if halved else 1
    wide = width // parts
    order = list(range(down))
    if halved and (width // down) % 16 == 0:
        order = [o * inner + i for o in reversed(range(outer)) for i in range(inner)]
    image, edge, arm, part = pl.pallas_call(
        inner_kernel,
        out_shape=(
            jax.ShapeDtypeStruct((nrows, width), bf16),
            jax.ShapeDtypeStruct((2, tile, width), f32),
            jax.ShapeDtypeStruct((2, 2 * tile, tile), bf16),
            jax.ShapeDtypeStruct((parts, width, wide), f32),
        ),
        in_specs=[whole(pltpu.SMEM), whole(pltpu.SMEM), whole(), whole(), whole()],
        out_specs=(whole(pltpu.HBM), whole(), whole(), whole()),
        scratch_shapes=[
            pltpu.VMEM((nrows, width), bf16),
            pltpu.SemaphoreType.DMA((nblk // 6 + 1,)),
        ],
        compiler_params=pltpu.CompilerParams(vmem_limit_bytes=32 * 2**20),
        cost_estimate=pl.CostEstimate(
            flops=2 * nrows * width * (width + 12 * bsize),
            bytes_accessed=8 * 2**20,
            transcendentals=0,
        ),
        name="inner",
    )(
        block_cols.T,
        live_slots,
        jac_blocks,
        basis,
        accumulation.reshape(nblk // 2, tile),
    )

    ends = [
        pl.BlockSpec((tile, width), lambda i: (0, 0)),
        pl.BlockSpec((tile, width), lambda i: (nrows // tile - 1, 0)),
    ]
    image, rows, send = pl.pallas_call(
        functools.partial(edge_kernel, order),
        out_shape=(
            jax.ShapeDtypeStruct((nrows, width), bf16),
            jax.ShapeDtypeStruct((parts, 2 * tile, wide), bf16),
            jax.ShapeDtypeStruct((width, wide), bf16),
        ),
        grid=(1,),
        in_specs=[whole(), whole(), whole(), whole(), *ends, whole(), whole(pl.ANY)],
        out_specs=(whole(pl.ANY), whole(), whole()),
        scratch_shapes=[
            pltpu.VMEM((2, tile, width), bf16),
            pltpu.SemaphoreType.DMA((2,)),
        ],
        input_output_aliases={7: 0},
        compiler_params=pltpu.CompilerParams(vmem_limit_bytes=32 * 2**20),
        name="edges",
    )(far, near, edge, arm, basis, basis, part, image)
    if halved:
        got = lax.ppermute(send, "col", [(0, 1), (1, 0)])
        keep = pl.pallas_call(
            functools.partial(keep_kernel, order),
            out_shape=jax.ShapeDtypeStruct((width, wide), f32),
            grid=(1,),
            in_specs=[*ends, whole(), whole()],
            out_specs=whole(),
            compiler_params=pltpu.CompilerParams(vmem_limit_bytes=32 * 2**20),
            cost_estimate=pl.CostEstimate(
                flops=4 * tile * width * width, bytes_accessed=2**21, transcendentals=0
            ),
            name="kept_half",
        )(basis, basis, rows, part)
        total = (keep + got.astype(f32)).astype(bf16)
        total = total.reshape(down, width // down, wide)
        groups = [[m * across + c for m in order] for c in range(across)]
        got = lax.all_to_all(total, AXES, 0, 0, axis_index_groups=groups, tiled=True)
    else:
        total = send.reshape(down, width // down, across, width // across)
        total = total.transpose(0, 2, 1, 3)
        total = total.reshape(count, width // down, width // across)
        got = lax.all_to_all(total, AXES, 0, 0, tiled=True)
    projected = jnp.sum(got.astype(f32), axis=0) * (1.0 / (nrows * count))
    return (image, projected)


def solution(mesh):
    rows, cols = mesh.devices.shape
    outer = 4 if rows % 4 == 0 else 1
    split = jax.sharding.Mesh(mesh.devices.reshape(outer, rows // outer, cols), AXES)
    return jax.shard_map(
        local,
        mesh=split,
        in_specs=(
            P(AXES, None),
            P(AXES, None, None, None),
            P(AXES, None),
            P(AXES),
            P(AXES),
        ),
        out_specs=(P(AXES, None), P(AXES[:2], "col")),
        check_vma=False,
    )
```

```python
import functools

import jax
import jax.numpy as jnp
from jax import lax
from jax.experimental import pallas as pl
from jax.experimental.pallas import tpu as pltpu
from jax.sharding import PartitionSpec as P

REACH = 2
AXES = ("outer", "inner", "col")
ROWS_DOT = (((0,), (0,)), ((), ()))


def strip_of(cols_ref, live_ref, jac_ref, acc_ref, first, pair):
    _, slots, bsize, _ = jac_ref.shape
    tile = 2 * bsize
    half = lax.broadcasted_iota(jnp.int32, (1, tile), 1) // bsize
    row = lax.broadcasted_iota(jnp.int32, (bsize, tile), 0)
    lane = lax.broadcasted_iota(jnp.int32, (bsize, tile), 1)
    weight = acc_ref[pair : pair + 1, :]
    halves = []
    for side in range(2):
        g = 2 * pair + side
        tiles = [None, jnp.where(lane == row + side * bsize, weight, 0.0), None]
        for s in range(slots):
            place = cols_ref[s, g] - (first + 2 * pair) + REACH
            place = jnp.where(s < live_ref[g], place, -1)
            block = jac_ref[g, s]
            wide = jnp.concatenate([block, block], axis=1).astype(jnp.float32)
            for t in range(3):
                here = jnp.where(half + 2 * t == place, 1.0, 0.0)
                term = wide * here
                tiles[t] = term if tiles[t] is None else tiles[t] + term
        halves.append(jnp.concatenate(tiles, axis=1))
    strip = jnp.concatenate(halves, axis=0)
    high = strip.astype(jnp.bfloat16)
    low = (strip - high.astype(jnp.float32)).astype(jnp.bfloat16)
    return jnp.concatenate([high, low], axis=0)


def gathered_rows(cols_ref, live_ref, jac_ref, basis_ref, first, g):
    nblk, slots, bsize, _ = jac_ref.shape
    lane = lax.broadcasted_iota(jnp.int32, (1, slots * bsize), 1)
    keep = jnp.where(lane < live_ref[g] * bsize, 1.0, 0.0).astype(jnp.bfloat16)
    blocks = jnp.concatenate([jac_ref[g, s] for s in range(slots)], axis=1) * keep
    rows = []
    for s in range(slots):
        at = jnp.clip(cols_ref[s, g] - first, 0, nblk - 1) * bsize
        rows.append(basis_ref[pl.ds(pl.multiple_of(at, bsize), bsize), :])
    rows = jnp.concatenate(rows, axis=0)
    return jnp.dot(blocks, rows, preferred_element_type=jnp.float32)


def apply_strip(strip, rows):
    both = jnp.dot(strip, rows, preferred_element_type=jnp.float32)
    half = strip.shape[0] // 2
    return both[:half] + both[half:]


def slice_kernel(basis_hbm, far_ref, near_ref, sems):
    tile = far_ref.shape[0]
    last = basis_hbm.shape[0] - tile
    odd = lax.rem(lax.axis_index(AXES), 2)
    copies = []
    for i, (at, target) in enumerate(((odd, far_ref), (1 - odd, near_ref))):
        where = pl.ds(pl.multiple_of(at * last, tile), tile)
        copies.append(pltpu.make_async_copy(basis_hbm.at[where], target, sems.at[i]))
        copies[i].start()
    for copy in copies:
        copy.wait()


def inner_kernel(
    cols_ref, live_ref, jac_ref, basis_ref, acc_ref,
    image_ref, edge_ref, arm_ref, part_ref, staged, sems,
):
    nblk, _, bsize, _ = jac_ref.shape
    nrows = basis_ref.shape[0]
    tile = 2 * bsize
    pairs = nblk // 2
    first = lax.axis_index(AXES) * nblk

    def project(start, stop):
        total = lax.dot_general(
            basis_ref[start:stop, :], staged[start:stop, :], ROWS_DOT,
            preferred_element_type=jnp.float32,
        )
        parts, _, wide = part_ref.shape
        return [total[:, i * wide : (i + 1) * wide] for i in range(parts)]

    def store(start, stop, at):
        where = pl.ds(start, stop - start)
        copy = pltpu.make_async_copy(staged.at[where], image_ref.at[where], sems.at[at])
        copy.start()
        return copy

    row = lax.broadcasted_iota(jnp.int32, (tile, tile), 0)
    lane = lax.broadcasted_iota(jnp.int32, (tile, tile), 1)
    middle = (pairs // 2) * tile
    stored = tile
    copies = []
    for pair in range(1, pairs - 1):
        start = pair * tile
        stop = start + tile
        weight = jnp.where(lane == row, acc_ref[pair : pair + 1, :], 0.0)
        weight = jnp.sum(weight, axis=1, keepdims=True)
        coupled = [
            gathered_rows(cols_ref, live_ref, jac_ref, basis_ref, first, 2 * pair + side)
            for side in range(2)
        ]
        own = basis_ref[start:stop, :].astype(jnp.float32)
        total = jnp.concatenate(coupled, axis=0) + weight * own
        staged[start:stop, :] = total.astype(jnp.bfloat16)
        if pair % 3 == 0 or pair == pairs - 2:
            copies.append(store(stored, stop, len(copies)))
            stored = stop
        if stop == middle:
            for i, half in enumerate(project(tile, middle)):
                part_ref[i] = half
    for side, pair in enumerate((0, pairs - 1)):
        strip = strip_of(cols_ref, live_ref, jac_ref, acc_ref, first, pair)
        if side == 0:
            edge_ref[0] = apply_strip(strip[:, tile:], basis_ref[: 2 * tile, :])
            arm_ref[0] = strip[:, :tile]
        else:
            edge_ref[1] = apply_strip(strip[:, : 2 * tile], basis_ref[nrows - 2 * tile :, :])
            arm_ref[1] = strip[:, 2 * tile :]
    for i, half in enumerate(project(middle, nrows - tile)):
        part_ref[i] += half
    for copy in copies:
        copy.wait()


def add_edges(part_ref, tiles, rows_ref, half):
    update = lax.dot_general(
        tiles, rows_ref[half], ROWS_DOT, preferred_element_type=jnp.float32
    )
    return part_ref[half] + update


def put_blocks(ref, value, order):
    if order == sorted(order):
        ref[...] = value.astype(ref.dtype)
        return
    high = value.shape[0] // len(order)
    for to, source in enumerate(order):
        block = value[source * high : (source + 1) * high, :]
        ref[to * high : (to + 1) * high, :] = block.astype(ref.dtype)


def leaving_half(parts):
    return 1 - lax.axis_index("col") if parts == 2 else 0


def edge_kernel(
    order, far_ref, near_ref, edge_ref, arm_ref, top_ref, bottom_ref, part_ref, _,
    image_ref, rows_ref, send_ref, staged, sems,
):
    tile = top_ref.shape[0]
    nrows = image_ref.shape[0]
    parts, _, wide = rows_ref.shape
    odd = lax.rem(lax.axis_index(AXES), 2) == 1
    near, far = near_ref[...], far_ref[...]
    halos = (jnp.where(odd, near, far), jnp.where(odd, far, near))
    copies = []
    for side in range(2):
        rows = edge_ref[side] + apply_strip(arm_ref[side], halos[side])
        rows = rows.astype(jnp.bfloat16)
        staged[side] = rows
        for i in range(parts):
            rows_ref[i, side * tile : (side + 1) * tile, :] = rows[:, i * wide : (i + 1) * wide]
        where = pl.ds(0 if side == 0 else nrows - tile, tile)
        copy = pltpu.make_async_copy(staged.at[side], image_ref.at[where], sems.at[side])
        copy.start()
        copies.append(copy)
    tiles = jnp.concatenate([top_ref[...], bottom_ref[...]], axis=0)
    send = add_edges(part_ref, tiles, rows_ref, leaving_half(parts))
    put_blocks(send_ref, send, order)
    for copy in copies:
        copy.wait()


def keep_kernel(order, top_ref, bottom_ref, rows_ref, part_ref, keep_ref):
    tiles = jnp.concatenate([top_ref[...], bottom_ref[...]], axis=0)
    keep = add_edges(part_ref, tiles, rows_ref, 1 - leaving_half(2))
    put_blocks(keep_ref, keep, order)


def whole(memory_space=pltpu.VMEM):
    return pl.BlockSpec(memory_space=memory_space)


def local(basis, jac_blocks, block_cols, live_slots, accumulation):
    nrows, width = basis.shape
    nblk, slots, bsize, _ = jac_blocks.shape
    tile = 2 * bsize
    outer, inner, across = (lax.axis_size(axis) for axis in AXES)
    down = outer * inner
    count = down * across
    f32, bf16 = jnp.float32, jnp.bfloat16
    edge_shape = jax.ShapeDtypeStruct((tile, width), bf16)
    far_send, near_send = pl.pallas_call(
        slice_kernel,
        out_shape=(edge_shape, edge_shape),
        in_specs=[whole(pltpu.HBM)],
        out_specs=(whole(), whole()),
        scratch_shapes=[pltpu.SemaphoreType.DMA((2,))],
        compiler_params=pltpu.CompilerParams(vmem_limit_bytes=4 * 2**20),
        cost_estimate=pl.CostEstimate(
            flops=2 * nrows * width * width * slots, bytes_accessed=0, transcendentals=0
        ),
        name="halo_rows",
    )(pltpu.with_memory_space_constraint(basis, pltpu.HBM))
    swaps = [(i, i + 1) for i in range(1, count - 1, 2)]
    far = lax.ppermute(far_send, AXES, swaps + [(j, i) for i, j in swaps])
    swaps = [(i, i + 1) for i in range(0, count, 2)]
    near = lax.ppermute(near_send, AXES, swaps + [(j, i) for i, j in swaps])

    halved = across == 2
    parts = 2 if halved else 1
    wide = width // parts
    order = list(range(down))
    if halved and (width // down) % 16 == 0:
        order = [down - 1, 0, *range(down - 2, 0, -1)]
    image, edge, arm, part = pl.pallas_call(
        inner_kernel,
        out_shape=(
            jax.ShapeDtypeStruct((nrows, width), bf16),
            jax.ShapeDtypeStruct((2, tile, width), f32),
            jax.ShapeDtypeStruct((2, 2 * tile, tile), bf16),
            jax.ShapeDtypeStruct((parts, width, wide), f32),
        ),
        in_specs=[whole(pltpu.SMEM), whole(pltpu.SMEM), whole(), whole(), whole()],
        out_specs=(whole(pltpu.HBM), whole(), whole(), whole()),
        scratch_shapes=[
            pltpu.VMEM((nrows, width), bf16),
            pltpu.SemaphoreType.DMA((nblk // 6 + 1,)),
        ],
        compiler_params=pltpu.CompilerParams(vmem_limit_bytes=32 * 2**20),
        cost_estimate=pl.CostEstimate(
            flops=2 * nrows * width * (width + 12 * bsize),
            bytes_accessed=8 * 2**20,
            transcendentals=0,
        ),
        name="inner",
    )(
        block_cols.T,
        live_slots,
        jac_blocks,
        basis,
        accumulation.reshape(nblk // 2, tile),
    )

    ends = [
        pl.BlockSpec((tile, width), lambda i: (0, 0)),
        pl.BlockSpec((tile, width), lambda i: (nrows // tile - 1, 0)),
    ]
    image, rows, send = pl.pallas_call(
        functools.partial(edge_kernel, order),
        out_shape=(
            jax.ShapeDtypeStruct((nrows, width), bf16),
            jax.ShapeDtypeStruct((parts, 2 * tile, wide), bf16),
            jax.ShapeDtypeStruct((width, wide), bf16),
        ),
        grid=(1,),
        in_specs=[whole(), whole(), whole(), whole(), *ends, whole(), whole(pl.ANY)],
        out_specs=(whole(pl.ANY), whole(), whole()),
        scratch_shapes=[
            pltpu.VMEM((2, tile, width), bf16),
            pltpu.SemaphoreType.DMA((2,)),
        ],
        input_output_aliases={7: 0},
        compiler_params=pltpu.CompilerParams(vmem_limit_bytes=32 * 2**20),
        name="edges",
    )(far, near, edge, arm, basis, basis, part, image)
    if halved:
        got = lax.ppermute(send, "col", [(0, 1), (1, 0)])
        keep = pl.pallas_call(
            functools.partial(keep_kernel, order),
            out_shape=jax.ShapeDtypeStruct((width, wide), f32),
            grid=(1,),
            in_specs=[*ends, whole(), whole()],
            out_specs=whole(),
            compiler_params=pltpu.CompilerParams(vmem_limit_bytes=32 * 2**20),
            cost_estimate=pl.CostEstimate(
                flops=4 * tile * width * width, bytes_accessed=2**21, transcendentals=0
            ),
            name="kept_half",
        )(basis, basis, rows, part)
        total = (keep + got.astype(f32)).astype(bf16)
        total = total.reshape(down, width // down, wide)
        groups = [[m * across + c for m in order] for c in range(across)]
        got = lax.all_to_all(total, AXES, 0, 0, axis_index_groups=groups, tiled=True)
    else:
        total = send.reshape(down, width // down, across, width // across)
        total = total.transpose(0, 2, 1, 3)
        total = total.reshape(count, width // down, width // across)
        got = lax.all_to_all(total, AXES, 0, 0, tiled=True)
    projected = jnp.sum(got.astype(f32), axis=0) * (1.0 / (nrows * count))
    return (image, projected)


def solution(mesh):
    rows, cols = mesh.devices.shape
    outer = 4 if rows % 4 == 0 else 1
    split = jax.sharding.Mesh(mesh.devices.reshape(outer, rows // outer, cols), AXES)
    return jax.shard_map(
        local,
        mesh=split,
        in_specs=(
            P(AXES, None),
            P(AXES, None, None, None),
            P(AXES, None),
            P(AXES),
            P(AXES),
        ),
        out_specs=(P(AXES, None), P(AXES[:2], "col")),
        check_vma=False,
    )
```

```python
import functools

import jax
import jax.numpy as jnp
from jax import lax
from jax.experimental import pallas as pl
from jax.experimental.pallas import tpu as pltpu
from jax.sharding import PartitionSpec as P

REACH = 2
AXES = ("outer", "inner", "col")
ROWS_DOT = (((0,), (0,)), ((), ()))


def strip_of(cols_ref, live_ref, jac_ref, acc_ref, first, pair):
    _, slots, bsize, _ = jac_ref.shape
    tile = 2 * bsize
    half = lax.broadcasted_iota(jnp.int32, (1, tile), 1) // bsize
    row = lax.broadcasted_iota(jnp.int32, (bsize, tile), 0)
    lane = lax.broadcasted_iota(jnp.int32, (bsize, tile), 1)
    weight = acc_ref[pair : pair + 1, :]
    halves = []
    for side in range(2):
        g = 2 * pair + side
        tiles = [None, jnp.where(lane == row + side * bsize, weight, 0.0), None]
        for s in range(slots):
            place = cols_ref[s, g] - (first + 2 * pair) + REACH
            place = jnp.where(s < live_ref[g], place, -1)
            block = jac_ref[g, s]
            wide = jnp.concatenate([block, block], axis=1).astype(jnp.float32)
            for t in range(3):
                here = jnp.where(half + 2 * t == place, 1.0, 0.0)
                term = wide * here
                tiles[t] = term if tiles[t] is None else tiles[t] + term
        halves.append(jnp.concatenate(tiles, axis=1))
    strip = jnp.concatenate(halves, axis=0)
    high = strip.astype(jnp.bfloat16)
    low = (strip - high.astype(jnp.float32)).astype(jnp.bfloat16)
    return jnp.concatenate([high, low], axis=0)


def gathered_rows(cols_ref, live_ref, jac_ref, basis_ref, first, g):
    nblk, slots, bsize, _ = jac_ref.shape
    lane = lax.broadcasted_iota(jnp.int32, (1, slots * bsize), 1)
    keep = jnp.where(lane < live_ref[g] * bsize, 1.0, 0.0).astype(jnp.bfloat16)
    blocks = jnp.concatenate([jac_ref[g, s] for s in range(slots)], axis=1) * keep
    rows = []
    for s in range(slots):
        at = jnp.clip(cols_ref[s, g] - first, 0, nblk - 1) * bsize
        rows.append(basis_ref[pl.ds(pl.multiple_of(at, bsize), bsize), :])
    rows = jnp.concatenate(rows, axis=0)
    return jnp.dot(blocks, rows, preferred_element_type=jnp.float32)


def apply_strip(strip, rows):
    both = jnp.dot(strip, rows, preferred_element_type=jnp.float32)
    half = strip.shape[0] // 2
    return both[:half] + both[half:]


def slice_kernel(basis_hbm, far_ref, tiles_ref, sems):
    tile = far_ref.shape[0]
    last = basis_hbm.shape[0] - tile
    odd = lax.rem(lax.axis_index(AXES), 2)
    far = pl.ds(pl.multiple_of(odd * last, tile), tile)
    copies = []
    for i, (source, target) in enumerate((
        (far, far_ref),
        (pl.ds(0, tile), tiles_ref.at[pl.ds(0, tile)]),
        (pl.ds(last, tile), tiles_ref.at[pl.ds(tile, tile)]),
    )):
        copies.append(pltpu.make_async_copy(basis_hbm.at[source], target, sems.at[i]))
        copies[i].start(priority=1)
    for copy in copies:
        copy.wait()


def inner_kernel(
    cols_ref, live_ref, jac_ref, basis_ref, acc_ref,
    image_ref, edge_ref, arm_ref, *rest,
):
    *sum_refs, part_ref, staged, sems = rest
    nblk, _, bsize, _ = jac_ref.shape
    nrows = basis_ref.shape[0]
    tile = 2 * bsize
    pairs = nblk // 2
    first = lax.axis_index(AXES) * nblk

    def project(start, stop):
        total = lax.dot_general(
            basis_ref[start:stop, :], staged[start:stop, :], ROWS_DOT,
            preferred_element_type=jnp.float32,
        )
        parts, _, wide = part_ref.shape
        return [total[:, i * wide : (i + 1) * wide] for i in range(parts)]

    def store(start, stop, at):
        where = pl.ds(start, stop - start)
        copy = pltpu.make_async_copy(staged.at[where], image_ref.at[where], sems.at[at])
        copy.start()
        return copy

    row = lax.broadcasted_iota(jnp.int32, (tile, tile), 0)
    lane = lax.broadcasted_iota(jnp.int32, (tile, tile), 1)
    middle = (pairs // 2) * tile
    stored = tile
    copies = []
    for pair in range(1, pairs - 1):
        start = pair * tile
        stop = start + tile
        weight = jnp.where(lane == row, acc_ref[pair : pair + 1, :], 0.0)
        weight = jnp.sum(weight, axis=1, keepdims=True)
        coupled = [
            gathered_rows(cols_ref, live_ref, jac_ref, basis_ref, first, 2 * pair + side)
            for side in range(2)
        ]
        own = basis_ref[start:stop, :].astype(jnp.float32)
        total = jnp.concatenate(coupled, axis=0) + weight * own
        staged[start:stop, :] = total.astype(jnp.bfloat16)
        if pair % 3 == 0 or pair == pairs - 2:
            copies.append(store(stored, stop, len(copies)))
            stored = stop
        if stop == middle:
            for i, half in enumerate(project(tile, middle)):
                part_ref[i] = half
    for side, pair in enumerate((0, pairs - 1)):
        strip = strip_of(cols_ref, live_ref, jac_ref, acc_ref, first, pair)
        if side == 0:
            edge_ref[0] = apply_strip(strip[:, tile:], basis_ref[: 2 * tile, :])
            arm_ref[0] = strip[:, :tile]
        else:
            edge_ref[1] = apply_strip(strip[:, : 2 * tile], basis_ref[nrows - 2 * tile :, :])
            arm_ref[1] = strip[:, 2 * tile :]
    sums = [part_ref[i] + half for i, half in enumerate(project(middle, nrows - tile))]
    if len(sums) == 1:
        sum_refs[0][...] = sums[0]
    else:
        second = lax.axis_index("col") == 1
        sum_refs[0][...] = jnp.where(second, sums[1], sums[0])
        sum_refs[1][...] = jnp.where(second, sums[0], sums[1]).astype(jnp.bfloat16)
    for copy in copies:
        copy.wait()


def put_blocks(ref, value, order):
    if order == sorted(order):
        ref[...] = value.astype(ref.dtype)
        return
    high = value.shape[0] // len(order)
    for to, source in enumerate(order):
        block = value[source * high : (source + 1) * high, :]
        ref[to * high : (to + 1) * high, :] = block.astype(ref.dtype)


def edge_kernel(
    far_ref, near_ref, edge_ref, arm_ref, _, image_ref, *rest,
):
    *rows_refs, staged, sems = rest
    tile, width = far_ref.shape
    nrows = image_ref.shape[0]
    odd = lax.rem(lax.axis_index(AXES), 2) == 1
    far = far_ref[...]
    halos = (
        jnp.where(odd, near_ref[tile:, :], far),
        jnp.where(odd, far, near_ref[:tile, :]),
    )
    copies = []
    for side in range(2):
        rows = edge_ref[side] + apply_strip(arm_ref[side], halos[side])
        rows = rows.astype(jnp.bfloat16)
        staged[side] = rows
        at = slice(side * tile, (side + 1) * tile)
        if len(rows_refs) == 1:
            rows_refs[0][at, :] = rows
        else:
            second = lax.axis_index("col") == 1
            left, right = rows[:, : width // 2], rows[:, width // 2 :]
            rows_refs[0][at, :] = jnp.where(second, right, left)
            rows_refs[1][at, :] = jnp.where(second, left, right)
        where = pl.ds(0 if side == 0 else nrows - tile, tile)
        copy = pltpu.make_async_copy(staged.at[side], image_ref.at[where], sems.at[side])
        copy.start()
        copies.append(copy)
    for copy in copies:
        copy.wait()


def update_kernel(order, tiles_ref, rows_ref, *refs):
    *terms, out_ref = refs
    total = lax.dot_general(
        tiles_ref[...], rows_ref[...], ROWS_DOT, preferred_element_type=jnp.float32
    )
    for term in terms:
        total = total + term[...].astype(jnp.float32)
    put_blocks(out_ref, total, order)


def update(name, order, kind, *arrays):
    tiles, rows = arrays[:2]
    shape = (tiles.shape[1], rows.shape[1])
    return pl.pallas_call(
        functools.partial(update_kernel, order),
        out_shape=jax.ShapeDtypeStruct(shape, kind),
        in_specs=[whole()] * len(arrays),
        out_specs=whole(),
        compiler_params=pltpu.CompilerParams(vmem_limit_bytes=32 * 2**20),
        cost_estimate=pl.CostEstimate(
            flops=2 * rows.size * shape[0], bytes_accessed=2**21, transcendentals=0
        ),
        name=name,
    )(*arrays)


def whole(memory_space=pltpu.VMEM):
    return pl.BlockSpec(memory_space=memory_space)


def local(basis, jac_blocks, block_cols, live_slots, accumulation):
    nrows, width = basis.shape
    nblk, slots, bsize, _ = jac_blocks.shape
    tile = 2 * bsize
    outer, inner, across = (lax.axis_size(axis) for axis in AXES)
    down = outer * inner
    count = down * across
    f32, bf16 = jnp.float32, jnp.bfloat16
    edge_shape = jax.ShapeDtypeStruct((tile, width), bf16)
    far_send, tiles = pl.pallas_call(
        slice_kernel,
        out_shape=(edge_shape, jax.ShapeDtypeStruct((2 * tile, width), bf16)),
        in_specs=[whole(pltpu.HBM)],
        out_specs=(whole(), whole()),
        scratch_shapes=[pltpu.SemaphoreType.DMA((3,))],
        compiler_params=pltpu.CompilerParams(vmem_limit_bytes=4 * 2**20),
        cost_estimate=pl.CostEstimate(
            flops=2 * nrows * width * width * slots, bytes_accessed=0, transcendentals=0
        ),
        name="halo_rows",
    )(pltpu.with_memory_space_constraint(basis, pltpu.HBM))
    swaps = [(i, i + 1) for i in range(1, count - 1, 2)]
    far = lax.ppermute(far_send, AXES, swaps + [(j, i) for i, j in swaps])
    swaps = [(i, i + 1) for i in range(0, count, 2)]
    near = lax.ppermute(tiles, AXES, swaps + [(j, i) for i, j in swaps])

    halved = across == 2
    parts = 2 if halved else 1
    wide = width // parts
    order = list(range(down))
    if halved and (width // down) % 16 == 0:
        order = [o * inner + i for i in range(inner) for o in reversed(range(outer))]
    image, edge, arm, *sums = pl.pallas_call(
        inner_kernel,
        out_shape=(
            jax.ShapeDtypeStruct((nrows, width), bf16),
            jax.ShapeDtypeStruct((2, tile, width), f32),
            jax.ShapeDtypeStruct((2, 2 * tile, tile), bf16),
            *(jax.ShapeDtypeStruct((width, wide), kind) for kind in (f32, bf16)[:parts]),
        ),
        in_specs=[whole(pltpu.SMEM), whole(pltpu.SMEM), whole(), whole(), whole()],
        out_specs=(whole(pltpu.HBM), *([whole()] * (2 + parts))),
        scratch_shapes=[
            pltpu.VMEM((parts, width, wide), f32),
            pltpu.VMEM((nrows, width), bf16),
            pltpu.SemaphoreType.DMA((nblk // 6 + 1,)),
        ],
        compiler_params=pltpu.CompilerParams(vmem_limit_bytes=32 * 2**20),
        cost_estimate=pl.CostEstimate(
            flops=2 * nrows * width * (width + 12 * bsize),
            bytes_accessed=8 * 2**20,
            transcendentals=0,
        ),
        name="inner",
    )(
        block_cols.T,
        live_slots,
        jac_blocks,
        basis,
        accumulation.reshape(nblk // 2, tile),
    )

    if halved:
        swap = [(0, 1), (1, 0)]
        leaving, far = lax.optimization_barrier((sums[1], far))
        early = lax.ppermute(leaving, "col", swap)
    image, *rows = pl.pallas_call(
        edge_kernel,
        out_shape=(
            jax.ShapeDtypeStruct((nrows, width), bf16),
            *([jax.ShapeDtypeStruct((2 * tile, wide), bf16)] * parts),
        ),
        in_specs=[whole(), whole(), whole(), whole(), whole(pl.ANY)],
        out_specs=(whole(pl.ANY), *([whole()] * parts)),
        scratch_shapes=[
            pltpu.VMEM((2, tile, width), bf16),
            pltpu.SemaphoreType.DMA((2,)),
        ],
        input_output_aliases={4: 0},
        compiler_params=pltpu.CompilerParams(vmem_limit_bytes=32 * 2**20),
        name="edges",
    )(far, near, edge, arm, image)
    if halved:
        late = lax.ppermute(rows[1], "col", swap)
        kept = update("own_rows", [0], f32, tiles, rows[0], sums[0])
        total = update("sibling_rows", order, bf16, near, late, kept, early)
        total = total.reshape(down, width // down, wide)
        groups = [[m * across + c for m in order] for c in range(across)]
        got = lax.all_to_all(total, AXES, 0, 0, axis_index_groups=groups, tiled=True)
    else:
        total = update("own_rows", [0], bf16, tiles, rows[0], sums[0])
        total = total.reshape(down, width // down, across, width // across)
        total = total.transpose(0, 2, 1, 3)
        total = total.reshape(count, width // down, width // across)
        got = lax.all_to_all(total, AXES, 0, 0, tiled=True)
    projected = jnp.sum(got.astype(f32), axis=0) * (1.0 / (nrows * count))
    return (image, projected)


def solution(mesh):
    rows, cols = mesh.devices.shape
    outer = 4 if rows % 4 == 0 else 1
    split = jax.sharding.Mesh(mesh.devices.reshape(outer, rows // outer, cols), AXES)
    return jax.shard_map(
        local,
        mesh=split,
        in_specs=(
            P(AXES, None),
            P(AXES, None, None, None),
            P(AXES, None),
            P(AXES),
            P(AXES),
        ),
        out_specs=(P(AXES, None), P(AXES[:2], "col")),
        check_vma=False,
    )
```

```python
import functools

import jax
import jax.numpy as jnp
from jax import lax
from jax.experimental import pallas as pl
from jax.experimental.pallas import tpu as pltpu
from jax.sharding import PartitionSpec as P

REACH = 2
AXES = ("outer", "inner", "col")
ROWS_DOT = (((0,), (0,)), ((), ()))


def strip_of(cols_ref, live_ref, jac_ref, acc_ref, first, pair):
    _, slots, bsize, _ = jac_ref.shape
    tile = 2 * bsize
    half = lax.broadcasted_iota(jnp.int32, (1, tile), 1) // bsize
    row = lax.broadcasted_iota(jnp.int32, (bsize, tile), 0)
    lane = lax.broadcasted_iota(jnp.int32, (bsize, tile), 1)
    weight = acc_ref[pair : pair + 1, :]
    halves = []
    for side in range(2):
        g = 2 * pair + side
        tiles = [None, jnp.where(lane == row + side * bsize, weight, 0.0), None]
        for s in range(slots):
            place = cols_ref[s, g] - (first + 2 * pair) + REACH
            place = jnp.where(s < live_ref[g], place, -1)
            block = jac_ref[g, s]
            wide = jnp.concatenate([block, block], axis=1).astype(jnp.float32)
            for t in range(3):
                here = jnp.where(half + 2 * t == place, 1.0, 0.0)
                term = wide * here
                tiles[t] = term if tiles[t] is None else tiles[t] + term
        halves.append(jnp.concatenate(tiles, axis=1))
    strip = jnp.concatenate(halves, axis=0)
    high = strip.astype(jnp.bfloat16)
    low = (strip - high.astype(jnp.float32)).astype(jnp.bfloat16)
    return jnp.concatenate([high, low], axis=0)


def gathered_rows(cols_ref, live_ref, jac_ref, basis_ref, first, g):
    nblk, slots, bsize, _ = jac_ref.shape
    lane = lax.broadcasted_iota(jnp.int32, (1, slots * bsize), 1)
    keep = jnp.where(lane < live_ref[g] * bsize, 1.0, 0.0).astype(jnp.bfloat16)
    blocks = jnp.concatenate([jac_ref[g, s] for s in range(slots)], axis=1) * keep
    rows = []
    for s in range(slots):
        at = jnp.clip(cols_ref[s, g] - first, 0, nblk - 1) * bsize
        rows.append(basis_ref[pl.ds(pl.multiple_of(at, bsize), bsize), :])
    rows = jnp.concatenate(rows, axis=0)
    return jnp.dot(blocks, rows, preferred_element_type=jnp.float32)


def apply_strip(strip, rows):
    both = jnp.dot(strip, rows, preferred_element_type=jnp.float32)
    half = strip.shape[0] // 2
    return both[:half] + both[half:]


def slice_kernel(basis_hbm, far_ref, near_ref, sems):
    tile = far_ref.shape[0]
    last = basis_hbm.shape[0] - tile
    odd = lax.rem(lax.axis_index(AXES), 2)
    copies = []
    for i, (at, target) in enumerate(((odd, far_ref), (1 - odd, near_ref))):
        where = pl.ds(pl.multiple_of(at * last, tile), tile)
        copies.append(pltpu.make_async_copy(basis_hbm.at[where], target, sems.at[i]))
        copies[i].start()
    for copy in copies:
        copy.wait()


def inner_kernel(
    cols_ref, live_ref, jac_ref, basis_ref, acc_ref,
    image_ref, edge_ref, arm_ref, part_ref, staged, sems,
):
    nblk, _, bsize, _ = jac_ref.shape
    nrows = basis_ref.shape[0]
    tile = 2 * bsize
    pairs = nblk // 2
    first = lax.axis_index(AXES) * nblk

    def project(start, stop):
        total = lax.dot_general(
            basis_ref[start:stop, :], staged[start:stop, :], ROWS_DOT,
            preferred_element_type=jnp.float32,
        )
        parts, _, wide = part_ref.shape
        return [total[:, i * wide : (i + 1) * wide] for i in range(parts)]

    def store(start, stop, at):
        where = pl.ds(start, stop - start)
        copy = pltpu.make_async_copy(staged.at[where], image_ref.at[where], sems.at[at])
        copy.start()
        return copy

    row = lax.broadcasted_iota(jnp.int32, (tile, tile), 0)
    lane = lax.broadcasted_iota(jnp.int32, (tile, tile), 1)
    middle = (pairs // 2) * tile
    stored = tile
    copies = []
    for pair in range(1, pairs - 1):
        start = pair * tile
        stop = start + tile
        weight = jnp.where(lane == row, acc_ref[pair : pair + 1, :], 0.0)
        weight = jnp.sum(weight, axis=1, keepdims=True)
        coupled = [
            gathered_rows(cols_ref, live_ref, jac_ref, basis_ref, first, 2 * pair + side)
            for side in range(2)
        ]
        own = basis_ref[start:stop, :].astype(jnp.float32)
        total = jnp.concatenate(coupled, axis=0) + weight * own
        staged[start:stop, :] = total.astype(jnp.bfloat16)
        if pair % 3 == 0 or pair == pairs - 2:
            copies.append(store(stored, stop, len(copies)))
            stored = stop
        if stop == middle:
            for i, half in enumerate(project(tile, middle)):
                part_ref[i] = half
    for side, pair in enumerate((0, pairs - 1)):
        strip = strip_of(cols_ref, live_ref, jac_ref, acc_ref, first, pair)
        if side == 0:
            edge_ref[0] = apply_strip(strip[:, tile:], basis_ref[: 2 * tile, :])
            arm_ref[0] = strip[:, :tile]
        else:
            edge_ref[1] = apply_strip(strip[:, : 2 * tile], basis_ref[nrows - 2 * tile :, :])
            arm_ref[1] = strip[:, 2 * tile :]
    for i, half in enumerate(project(middle, nrows - tile)):
        part_ref[i] += half
    for copy in copies:
        copy.wait()


def end_tiles(basis_ref, tile):
    nrows = basis_ref.shape[0]
    return jnp.concatenate([basis_ref[:tile, :], basis_ref[nrows - tile :, :]], axis=0)


def add_edges(part_ref, tiles, rows_ref, half):
    update = lax.dot_general(
        tiles, rows_ref[half], ROWS_DOT, preferred_element_type=jnp.float32
    )
    return part_ref[half] + update


def put_blocks(ref, value, order):
    if order == sorted(order):
        ref[...] = value.astype(ref.dtype)
        return
    high = value.shape[0] // len(order)
    for to, source in enumerate(order):
        block = value[source * high : (source + 1) * high, :]
        ref[to * high : (to + 1) * high, :] = block.astype(ref.dtype)


def leaving_half(parts):
    return 1 - lax.axis_index("col") if parts == 2 else 0


def edge_kernel(
    order, far_ref, near_ref, edge_ref, arm_ref, basis_ref, part_ref, rows_ref, send_ref,
):
    tile = far_ref.shape[0]
    parts, _, wide = rows_ref.shape
    odd = lax.rem(lax.axis_index(AXES), 2) == 1
    near, far = near_ref[...], far_ref[...]
    halos = (jnp.where(odd, near, far), jnp.where(odd, far, near))
    for side in range(2):
        rows = edge_ref[side] + apply_strip(arm_ref[side], halos[side])
        rows = rows.astype(jnp.bfloat16)
        for i in range(parts):
            rows_ref[i, side * tile : (side + 1) * tile, :] = rows[:, i * wide : (i + 1) * wide]
    send = add_edges(part_ref, end_tiles(basis_ref, tile), rows_ref, leaving_half(parts))
    put_blocks(send_ref, send, order)


def keep_kernel(order, basis_ref, rows_ref, part_ref, _, image_ref, *rest):
    *keep_refs, sems = rest
    nrows = image_ref.shape[0]
    parts, rows, wide = rows_ref.shape
    tile = rows // 2
    copies = []
    for side, start in enumerate((0, nrows - tile)):
        for i in range(parts):
            source = rows_ref.at[i, pl.ds(side * tile, tile)]
            target = image_ref.at[pl.ds(start, tile), pl.ds(i * wide, wide)]
            copy = pltpu.make_async_copy(source, target, sems.at[side * parts + i])
            copy.start()
            copies.append(copy)
    for keep_ref in keep_refs:
        keep = add_edges(part_ref, end_tiles(basis_ref, tile), rows_ref, 1 - leaving_half(parts))
        put_blocks(keep_ref, keep, order)
    for copy in copies:
        copy.wait()


def whole(memory_space=pltpu.VMEM):
    return pl.BlockSpec(memory_space=memory_space)


def local(basis, jac_blocks, block_cols, live_slots, accumulation):
    nrows, width = basis.shape
    nblk, slots, bsize, _ = jac_blocks.shape
    tile = 2 * bsize
    outer, inner, across = (lax.axis_size(axis) for axis in AXES)
    down = outer * inner
    count = down * across
    f32, bf16 = jnp.float32, jnp.bfloat16
    edge_shape = jax.ShapeDtypeStruct((tile, width), bf16)
    far_send, near_send = pl.pallas_call(
        slice_kernel,
        out_shape=(edge_shape, edge_shape),
        in_specs=[whole(pltpu.HBM)],
        out_specs=(whole(), whole()),
        scratch_shapes=[pltpu.SemaphoreType.DMA((2,))],
        compiler_params=pltpu.CompilerParams(vmem_limit_bytes=4 * 2**20),
        cost_estimate=pl.CostEstimate(
            flops=2 * nrows * width * width * slots, bytes_accessed=0, transcendentals=0
        ),
        name="halo_rows",
    )(pltpu.with_memory_space_constraint(basis, pltpu.HBM))
    swaps = [(i, i + 1) for i in range(1, count - 1, 2)]
    far = lax.ppermute(far_send, AXES, swaps + [(j, i) for i, j in swaps])
    swaps = [(i, i + 1) for i in range(0, count, 2)]
    near = lax.ppermute(near_send, AXES, swaps + [(j, i) for i, j in swaps])

    halved = across == 2
    parts = 2 if halved else 1
    wide = width // parts
    order = list(range(down))
    if halved and (width // down) % 16 == 0:
        order = [o * inner + i for i in range(inner) for o in reversed(range(outer))]
    image, edge, arm, part = pl.pallas_call(
        inner_kernel,
        out_shape=(
            jax.ShapeDtypeStruct((nrows, width), bf16),
            jax.ShapeDtypeStruct((2, tile, width), f32),
            jax.ShapeDtypeStruct((2, 2 * tile, tile), bf16),
            jax.ShapeDtypeStruct((parts, width, wide), f32),
        ),
        in_specs=[whole(pltpu.SMEM), whole(pltpu.SMEM), whole(), whole(), whole()],
        out_specs=(whole(pltpu.HBM), whole(), whole(), whole()),
        scratch_shapes=[
            pltpu.VMEM((nrows, width), bf16),
            pltpu.SemaphoreType.DMA((nblk // 6 + 1,)),
        ],
        compiler_params=pltpu.CompilerParams(vmem_limit_bytes=32 * 2**20),
        cost_estimate=pl.CostEstimate(
            flops=2 * nrows * width * (width + 12 * bsize),
            bytes_accessed=8 * 2**20,
            transcendentals=0,
        ),
        name="inner",
    )(
        block_cols.T,
        live_slots,
        jac_blocks,
        basis,
        accumulation.reshape(nblk // 2, tile),
    )

    rows, send = pl.pallas_call(
        functools.partial(edge_kernel, order),
        out_shape=(
            jax.ShapeDtypeStruct((parts, 2 * tile, wide), bf16),
            jax.ShapeDtypeStruct((width, wide), bf16),
        ),
        in_specs=[whole()] * 6,
        out_specs=(whole(), whole()),
        compiler_params=pltpu.CompilerParams(vmem_limit_bytes=32 * 2**20),
        name="edges",
    )(far, near, edge, arm, basis, part)
    image, *keep = pl.pallas_call(
        functools.partial(keep_kernel, order),
        out_shape=(
            jax.ShapeDtypeStruct((nrows, width), bf16),
            *([jax.ShapeDtypeStruct((width, wide), f32)] if halved else []),
        ),
        in_specs=[whole(), whole(), whole(), whole(pl.ANY)],
        out_specs=(whole(pl.ANY), *([whole()] if halved else [])),
        scratch_shapes=[pltpu.SemaphoreType.DMA((2 * parts,))],
        input_output_aliases={3: 0},
        compiler_params=pltpu.CompilerParams(vmem_limit_bytes=32 * 2**20),
        cost_estimate=pl.CostEstimate(
            flops=4 * tile * width * width, bytes_accessed=2**21, transcendentals=0
        ),
        name="kept_half",
    )(basis, rows, part, image)
    if halved:
        got = lax.ppermute(send, "col", [(0, 1), (1, 0)])
        total = (keep[0] + got.astype(f32)).astype(bf16)
        total = total.reshape(down, width // down, wide)
        groups = [[m * across + c for m in order] for c in range(across)]
        got = lax.all_to_all(total, AXES, 0, 0, axis_index_groups=groups, tiled=True)
    else:
        total = send.reshape(down, width // down, across, width // across)
        total = total.transpose(0, 2, 1, 3)
        total = total.reshape(count, width // down, width // across)
        got = lax.all_to_all(total, AXES, 0, 0, tiled=True)
    projected = jnp.sum(got.astype(f32), axis=0) * (1.0 / (nrows * count))
    return (image, projected)


def solution(mesh):
    rows, cols = mesh.devices.shape
    outer = 4 if rows % 4 == 0 else 1
    split = jax.sharding.Mesh(mesh.devices.reshape(outer, rows // outer, cols), AXES)
    return jax.shard_map(
        local,
        mesh=split,
        in_specs=(
            P(AXES, None),
            P(AXES, None, None, None),
            P(AXES, None),
            P(AXES),
            P(AXES),
        ),
        out_specs=(P(AXES, None), P(AXES[:2], "col")),
        check_vma=False,
    )
```

```python
import functools

import jax
import jax.numpy as jnp
from jax import lax
from jax.experimental import pallas as pl
from jax.experimental.pallas import tpu as pltpu
from jax.sharding import PartitionSpec as P

REACH = 2
AXES = ("outer", "inner", "col")
ROWS_DOT = (((0,), (0,)), ((), ()))


def strip_of(cols_ref, live_ref, jac_ref, acc_ref, first, pair):
    _, slots, bsize, _ = jac_ref.shape
    tile = 2 * bsize
    half = lax.broadcasted_iota(jnp.int32, (1, tile), 1) // bsize
    row = lax.broadcasted_iota(jnp.int32, (bsize, tile), 0)
    lane = lax.broadcasted_iota(jnp.int32, (bsize, tile), 1)
    weight = acc_ref[pair : pair + 1, :]
    halves = []
    for side in range(2):
        g = 2 * pair + side
        tiles = [None, jnp.where(lane == row + side * bsize, weight, 0.0), None]
        for s in range(slots):
            place = cols_ref[s, g] - (first + 2 * pair) + REACH
            place = jnp.where(s < live_ref[g], place, -1)
            block = jac_ref[g, s]
            wide = jnp.concatenate([block, block], axis=1).astype(jnp.float32)
            for t in range(3):
                here = jnp.where(half + 2 * t == place, 1.0, 0.0)
                term = wide * here
                tiles[t] = term if tiles[t] is None else tiles[t] + term
        halves.append(jnp.concatenate(tiles, axis=1))
    strip = jnp.concatenate(halves, axis=0)
    high = strip.astype(jnp.bfloat16)
    low = (strip - high.astype(jnp.float32)).astype(jnp.bfloat16)
    return jnp.concatenate([high, low], axis=0)


def gathered_rows(cols_ref, live_ref, jac_ref, basis_ref, first, g):
    nblk, slots, bsize, _ = jac_ref.shape
    lane = lax.broadcasted_iota(jnp.int32, (1, slots * bsize), 1)
    keep = jnp.where(lane < live_ref[g] * bsize, 1.0, 0.0).astype(jnp.bfloat16)
    blocks = jnp.concatenate([jac_ref[g, s] for s in range(slots)], axis=1) * keep
    rows = []
    for s in range(slots):
        at = jnp.clip(cols_ref[s, g] - first, 0, nblk - 1) * bsize
        rows.append(basis_ref[pl.ds(pl.multiple_of(at, bsize), bsize), :])
    rows = jnp.concatenate(rows, axis=0)
    return jnp.dot(blocks, rows, preferred_element_type=jnp.float32)


def apply_strip(strip, rows):
    both = jnp.dot(strip, rows, preferred_element_type=jnp.float32)
    half = strip.shape[0] // 2
    return both[:half] + both[half:]


def slice_kernel(basis_hbm, far_ref, near_ref, sems):
    tile = far_ref.shape[0]
    last = basis_hbm.shape[0] - tile
    odd = lax.rem(lax.axis_index(AXES), 2)
    copies = []
    for i, (at, target) in enumerate(((odd, far_ref), (1 - odd, near_ref))):
        where = pl.ds(pl.multiple_of(at * last, tile), tile)
        copies.append(pltpu.make_async_copy(basis_hbm.at[where], target, sems.at[i]))
        copies[i].start()
    for copy in copies:
        copy.wait()


def inner_kernel(
    cols_ref, live_ref, jac_ref, basis_ref, acc_ref,
    image_ref, edge_ref, arm_ref, part_ref, staged, sems,
):
    nblk, _, bsize, _ = jac_ref.shape
    nrows = basis_ref.shape[0]
    tile = 2 * bsize
    pairs = nblk // 2
    first = lax.axis_index(AXES) * nblk

    def project(start, stop):
        total = lax.dot_general(
            basis_ref[start:stop, :], staged[start:stop, :], ROWS_DOT,
            preferred_element_type=jnp.float32,
        )
        parts, _, wide = part_ref.shape
        return [total[:, i * wide : (i + 1) * wide] for i in range(parts)]

    def store(start, stop, at):
        where = pl.ds(start, stop - start)
        copy = pltpu.make_async_copy(staged.at[where], image_ref.at[where], sems.at[at])
        copy.start()
        return copy

    row = lax.broadcasted_iota(jnp.int32, (tile, tile), 0)
    lane = lax.broadcasted_iota(jnp.int32, (tile, tile), 1)
    middle = (pairs // 2) * tile
    stored = tile
    copies = []
    for pair in range(1, pairs - 1):
        start = pair * tile
        stop = start + tile
        weight = jnp.where(lane == row, acc_ref[pair : pair + 1, :], 0.0)
        weight = jnp.sum(weight, axis=1, keepdims=True)
        coupled = [
            gathered_rows(cols_ref, live_ref, jac_ref, basis_ref, first, 2 * pair + side)
            for side in range(2)
        ]
        own = basis_ref[start:stop, :].astype(jnp.float32)
        total = jnp.concatenate(coupled, axis=0) + weight * own
        staged[start:stop, :] = total.astype(jnp.bfloat16)
        if pair % 3 == 0 or pair == pairs - 2:
            copies.append(store(stored, stop, len(copies)))
            stored = stop
        if stop == middle:
            for i, half in enumerate(project(tile, middle)):
                part_ref[i] = half
    for side, pair in enumerate((0, pairs - 1)):
        strip = strip_of(cols_ref, live_ref, jac_ref, acc_ref, first, pair)
        if side == 0:
            edge_ref[0] = apply_strip(strip[:, tile:], basis_ref[: 2 * tile, :])
            arm_ref[0] = strip[:, :tile]
        else:
            edge_ref[1] = apply_strip(strip[:, : 2 * tile], basis_ref[nrows - 2 * tile :, :])
            arm_ref[1] = strip[:, 2 * tile :]
    for i, half in enumerate(project(middle, nrows - tile)):
        part_ref[i] += half
    for copy in copies:
        copy.wait()


def end_tiles(basis_ref, tile):
    nrows = basis_ref.shape[0]
    return jnp.concatenate([basis_ref[:tile, :], basis_ref[nrows - tile :, :]], axis=0)


def add_edges(part_ref, tiles, rows_ref, half):
    update = lax.dot_general(
        tiles, rows_ref[half], ROWS_DOT, preferred_element_type=jnp.float32
    )
    return part_ref[half] + update


def put_blocks(ref, value, orders, core):
    high = value.shape[0] // len(orders[0])
    blocks = [value[i * high : (i + 1) * high, :] for i in range(len(orders[0]))]
    for to, (first, second) in enumerate(zip(orders[0], orders[-1])):
        block = blocks[first]
        if first != second:
            block = jnp.where(core == 1, blocks[second], block)
        ref[to * high : (to + 1) * high, :] = block.astype(ref.dtype)


def leaving_half(parts):
    return 1 - lax.axis_index("col") if parts == 2 else 0


def edge_kernel(
    orders, far_ref, near_ref, edge_ref, arm_ref, basis_ref, part_ref, rows_ref, send_ref,
):
    tile = far_ref.shape[0]
    parts, _, wide = rows_ref.shape
    odd = lax.rem(lax.axis_index(AXES), 2) == 1
    near, far = near_ref[...], far_ref[...]
    halos = (jnp.where(odd, near, far), jnp.where(odd, far, near))
    for side in range(2):
        rows = edge_ref[side] + apply_strip(arm_ref[side], halos[side])
        rows = rows.astype(jnp.bfloat16)
        for i in range(parts):
            rows_ref[i, side * tile : (side + 1) * tile, :] = rows[:, i * wide : (i + 1) * wide]
    leaving = leaving_half(parts)
    send = add_edges(part_ref, end_tiles(basis_ref, tile), rows_ref, leaving)
    put_blocks(send_ref, send, orders, leaving)


def keep_kernel(orders, basis_ref, rows_ref, part_ref, _, image_ref, *rest):
    *keep_refs, sems = rest
    nrows = image_ref.shape[0]
    parts, rows, wide = rows_ref.shape
    tile = rows // 2
    copies = []
    for side, start in enumerate((0, nrows - tile)):
        for i in range(parts):
            source = rows_ref.at[i, pl.ds(side * tile, tile)]
            target = image_ref.at[pl.ds(start, tile), pl.ds(i * wide, wide)]
            copy = pltpu.make_async_copy(source, target, sems.at[side * parts + i])
            copy.start()
            copies.append(copy)
    for keep_ref in keep_refs:
        own = 1 - leaving_half(parts)
        keep = add_edges(part_ref, end_tiles(basis_ref, tile), rows_ref, own)
        put_blocks(keep_ref, keep, orders, own)
    for copy in copies:
        copy.wait()


def whole(memory_space=pltpu.VMEM):
    return pl.BlockSpec(memory_space=memory_space)


def local(basis, jac_blocks, block_cols, live_slots, accumulation):
    nrows, width = basis.shape
    nblk, slots, bsize, _ = jac_blocks.shape
    tile = 2 * bsize
    outer, inner, across = (lax.axis_size(axis) for axis in AXES)
    down = outer * inner
    count = down * across
    f32, bf16 = jnp.float32, jnp.bfloat16
    edge_shape = jax.ShapeDtypeStruct((tile, width), bf16)
    far_send, near_send = pl.pallas_call(
        slice_kernel,
        out_shape=(edge_shape, edge_shape),
        in_specs=[whole(pltpu.HBM)],
        out_specs=(whole(), whole()),
        scratch_shapes=[pltpu.SemaphoreType.DMA((2,))],
        compiler_params=pltpu.CompilerParams(vmem_limit_bytes=4 * 2**20),
        cost_estimate=pl.CostEstimate(
            flops=2 * nrows * width * width * slots, bytes_accessed=0, transcendentals=0
        ),
        name="halo_rows",
    )(pltpu.with_memory_space_constraint(basis, pltpu.HBM))
    swaps = [(i, i + 1) for i in range(1, count - 1, 2)]
    far = lax.ppermute(far_send, AXES, swaps + [(j, i) for i, j in swaps])
    swaps = [(i, i + 1) for i in range(0, count, 2)]
    near = lax.ppermute(near_send, AXES, swaps + [(j, i) for i, j in swaps])

    halved = across == 2
    parts = 2 if halved else 1
    wide = width // parts
    orders = [[0]]
    if halved:
        orders = [list(range(down))] * 2
        if (width // down) % 16 == 0:
            lines = [[o * inner + i for o in reversed(range(outer))] for i in range(inner)]
            orders = [sum(lines, []), sum(lines[:1] + lines[:0:-1], [])]
    image, edge, arm, part = pl.pallas_call(
        inner_kernel,
        out_shape=(
            jax.ShapeDtypeStruct((nrows, width), bf16),
            jax.ShapeDtypeStruct((2, tile, width), f32),
            jax.ShapeDtypeStruct((2, 2 * tile, tile), bf16),
            jax.ShapeDtypeStruct((parts, width, wide), f32),
        ),
        in_specs=[whole(pltpu.SMEM), whole(pltpu.SMEM), whole(), whole(), whole()],
        out_specs=(whole(pltpu.HBM), whole(), whole(), whole()),
        scratch_shapes=[
            pltpu.VMEM((nrows, width), bf16),
            pltpu.SemaphoreType.DMA((nblk // 6 + 1,)),
        ],
        compiler_params=pltpu.CompilerParams(vmem_limit_bytes=32 * 2**20),
        cost_estimate=pl.CostEstimate(
            flops=2 * nrows * width * (width + 12 * bsize),
            bytes_accessed=8 * 2**20,
            transcendentals=0,
        ),
        name="inner",
    )(
        block_cols.T,
        live_slots,
        jac_blocks,
        basis,
        accumulation.reshape(nblk // 2, tile),
    )

    rows, send = pl.pallas_call(
        functools.partial(edge_kernel, orders),
        out_shape=(
            jax.ShapeDtypeStruct((parts, 2 * tile, wide), bf16),
            jax.ShapeDtypeStruct((width, wide), bf16),
        ),
        in_specs=[whole()] * 6,
        out_specs=(whole(), whole()),
        compiler_params=pltpu.CompilerParams(vmem_limit_bytes=32 * 2**20),
        name="edges",
    )(far, near, edge, arm, basis, part)
    image, *keep = pl.pallas_call(
        functools.partial(keep_kernel, orders),
        out_shape=(
            jax.ShapeDtypeStruct((nrows, width), bf16),
            *([jax.ShapeDtypeStruct((width, wide), f32)] if halved else []),
        ),
        in_specs=[whole(), whole(), whole(), whole(pl.ANY)],
        out_specs=(whole(pl.ANY), *([whole()] if halved else [])),
        scratch_shapes=[pltpu.SemaphoreType.DMA((2 * parts,))],
        input_output_aliases={3: 0},
        compiler_params=pltpu.CompilerParams(vmem_limit_bytes=32 * 2**20),
        cost_estimate=pl.CostEstimate(
            flops=4 * tile * width * width, bytes_accessed=2**21, transcendentals=0
        ),
        name="kept_half",
    )(basis, rows, part, image)
    if halved:
        got = lax.ppermute(send, "col", [(0, 1), (1, 0)])
        total = (keep[0] + got.astype(f32)).astype(bf16)
        total = total.reshape(down, width // down, wide)
        groups = [[m * across + c for m in orders[c]] for c in range(across)]
        got = lax.all_to_all(total, AXES, 0, 0, axis_index_groups=groups, tiled=True)
    else:
        total = send.reshape(down, width // down, across, width // across)
        total = total.transpose(0, 2, 1, 3)
        total = total.reshape(count, width // down, width // across)
        got = lax.all_to_all(total, AXES, 0, 0, tiled=True)
    projected = jnp.sum(got.astype(f32), axis=0) * (1.0 / (nrows * count))
    return (image, projected)


def solution(mesh):
    rows, cols = mesh.devices.shape
    outer = 4 if rows % 4 == 0 else 1
    split = jax.sharding.Mesh(mesh.devices.reshape(outer, rows // outer, cols), AXES)
    return jax.shard_map(
        local,
        mesh=split,
        in_specs=(
            P(AXES, None),
            P(AXES, None, None, None),
            P(AXES, None),
            P(AXES),
            P(AXES),
        ),
        out_specs=(P(AXES, None), P(AXES[:2], "col")),
        check_vma=False,
    )
```

```python
import functools

import jax
import jax.numpy as jnp
from jax import lax
from jax.experimental import pallas as pl
from jax.experimental.pallas import tpu as pltpu
from jax.sharding import PartitionSpec as P

REACH = 2
AXES = ("outer", "inner", "col")
ROWS_DOT = (((0,), (0,)), ((), ()))


def strip_of(cols_ref, live_ref, jac_ref, acc_ref, first, pair):
    _, slots, bsize, _ = jac_ref.shape
    tile = 2 * bsize
    half = lax.broadcasted_iota(jnp.int32, (1, tile), 1) // bsize
    row = lax.broadcasted_iota(jnp.int32, (bsize, tile), 0)
    lane = lax.broadcasted_iota(jnp.int32, (bsize, tile), 1)
    weight = acc_ref[pair : pair + 1, :]
    halves = []
    for side in range(2):
        g = 2 * pair + side
        tiles = [None, jnp.where(lane == row + side * bsize, weight, 0.0), None]
        for s in range(slots):
            place = cols_ref[s, g] - (first + 2 * pair) + REACH
            place = jnp.where(s < live_ref[g], place, -1)
            block = jac_ref[g, s]
            wide = jnp.concatenate([block, block], axis=1).astype(jnp.float32)
            for t in range(3):
                here = jnp.where(half + 2 * t == place, 1.0, 0.0)
                term = wide * here
                tiles[t] = term if tiles[t] is None else tiles[t] + term
        halves.append(jnp.concatenate(tiles, axis=1))
    strip = jnp.concatenate(halves, axis=0)
    high = strip.astype(jnp.bfloat16)
    low = (strip - high.astype(jnp.float32)).astype(jnp.bfloat16)
    return jnp.concatenate([high, low], axis=0)


def gathered_rows(cols_ref, live_ref, jac_ref, basis_ref, first, g):
    nblk, slots, bsize, _ = jac_ref.shape
    lane = lax.broadcasted_iota(jnp.int32, (1, slots * bsize), 1)
    keep = jnp.where(lane < live_ref[g] * bsize, 1.0, 0.0).astype(jnp.bfloat16)
    blocks = jnp.concatenate([jac_ref[g, s] for s in range(slots)], axis=1) * keep
    rows = []
    for s in range(slots):
        at = jnp.clip(cols_ref[s, g] - first, 0, nblk - 1) * bsize
        rows.append(basis_ref[pl.ds(pl.multiple_of(at, bsize), bsize), :])
    rows = jnp.concatenate(rows, axis=0)
    return jnp.dot(blocks, rows, preferred_element_type=jnp.float32)


def apply_strip(strip, rows):
    both = jnp.dot(strip, rows, preferred_element_type=jnp.float32)
    half = strip.shape[0] // 2
    return both[:half] + both[half:]


def far_kernel(basis_hbm, far_ref, sem):
    tile = far_ref.shape[0]
    last = basis_hbm.shape[0] - tile
    odd = lax.rem(lax.axis_index(AXES), 2)
    where = pl.ds(pl.multiple_of(odd * last, tile), tile)
    copy = pltpu.make_async_copy(basis_hbm.at[where], far_ref, sem)
    copy.start()
    copy.wait()


def near_kernel(basis_ref, near_ref):
    tile = near_ref.shape[0]
    last = basis_ref.shape[0] - tile
    odd = lax.rem(lax.axis_index(AXES), 2)
    where = pl.ds(pl.multiple_of((1 - odd) * last, tile), tile)
    near_ref[...] = basis_ref[where, :]


def inner_kernel(
    cols_ref, live_ref, jac_ref, basis_ref, acc_ref,
    image_ref, edge_ref, arm_ref, part_ref, staged, sems,
):
    nblk, _, bsize, _ = jac_ref.shape
    nrows = basis_ref.shape[0]
    tile = 2 * bsize
    pairs = nblk // 2
    first = lax.axis_index(AXES) * nblk

    def project(start, stop):
        total = lax.dot_general(
            basis_ref[start:stop, :], staged[start:stop, :], ROWS_DOT,
            preferred_element_type=jnp.float32,
        )
        parts, _, wide = part_ref.shape
        return [total[:, i * wide : (i + 1) * wide] for i in range(parts)]

    def store(start, stop, at):
        where = pl.ds(start, stop - start)
        copy = pltpu.make_async_copy(staged.at[where], image_ref.at[where], sems.at[at])
        copy.start()
        return copy

    row = lax.broadcasted_iota(jnp.int32, (tile, tile), 0)
    lane = lax.broadcasted_iota(jnp.int32, (tile, tile), 1)
    middle = (pairs // 2) * tile
    stored = tile
    copies = []
    for pair in range(1, pairs - 1):
        start = pair * tile
        stop = start + tile
        weight = jnp.where(lane == row, acc_ref[pair : pair + 1, :], 0.0)
        weight = jnp.sum(weight, axis=1, keepdims=True)
        coupled = [
            gathered_rows(cols_ref, live_ref, jac_ref, basis_ref, first, 2 * pair + side)
            for side in range(2)
        ]
        own = basis_ref[start:stop, :].astype(jnp.float32)
        total = jnp.concatenate(coupled, axis=0) + weight * own
        staged[start:stop, :] = total.astype(jnp.bfloat16)
        if pair % 3 == 0 or pair == pairs - 2:
            copies.append(store(stored, stop, len(copies)))
            stored = stop
        if stop == middle:
            for i, half in enumerate(project(tile, middle)):
                part_ref[i] = half
    for side, pair in enumerate((0, pairs - 1)):
        strip = strip_of(cols_ref, live_ref, jac_ref, acc_ref, first, pair)
        if side == 0:
            edge_ref[0] = apply_strip(strip[:, tile:], basis_ref[: 2 * tile, :])
            arm_ref[0] = strip[:, :tile]
        else:
            edge_ref[1] = apply_strip(strip[:, : 2 * tile], basis_ref[nrows - 2 * tile :, :])
            arm_ref[1] = strip[:, 2 * tile :]
    for i, half in enumerate(project(middle, nrows - tile)):
        part_ref[i] += half
    for copy in copies:
        copy.wait()


def end_tiles(basis_ref, tile):
    nrows = basis_ref.shape[0]
    return jnp.concatenate([basis_ref[:tile, :], basis_ref[nrows - tile :, :]], axis=0)


def add_edges(part_ref, tiles, rows_ref, half):
    update = lax.dot_general(
        tiles, rows_ref[half], ROWS_DOT, preferred_element_type=jnp.float32
    )
    return part_ref[half] + update


def put_blocks(ref, value, orders, core):
    high = value.shape[0] // len(orders[0])
    blocks = [value[i * high : (i + 1) * high, :] for i in range(len(orders[0]))]
    for to, (first, second) in enumerate(zip(orders[0], orders[-1])):
        block = blocks[first]
        if first != second:
            block = jnp.where(core == 1, blocks[second], block)
        ref[to * high : (to + 1) * high, :] = block.astype(ref.dtype)


def leaving_half(parts):
    return 1 - lax.axis_index("col") if parts == 2 else 0


def edge_kernel(
    orders, far_ref, near_ref, edge_ref, arm_ref, basis_ref, part_ref, rows_ref, send_ref,
):
    tile = far_ref.shape[0]
    parts, _, wide = rows_ref.shape
    odd = lax.rem(lax.axis_index(AXES), 2) == 1
    near, far = near_ref[...], far_ref[...]
    halos = (jnp.where(odd, near, far), jnp.where(odd, far, near))
    for side in range(2):
        rows = edge_ref[side] + apply_strip(arm_ref[side], halos[side])
        rows = rows.astype(jnp.bfloat16)
        for i in range(parts):
            rows_ref[i, side * tile : (side + 1) * tile, :] = rows[:, i * wide : (i + 1) * wide]
    leaving = leaving_half(parts)
    send = add_edges(part_ref, end_tiles(basis_ref, tile), rows_ref, leaving)
    put_blocks(send_ref, send, orders, leaving)


def keep_kernel(orders, basis_ref, rows_ref, part_ref, _, image_ref, *rest):
    *keep_refs, sems = rest
    nrows = image_ref.shape[0]
    parts, rows, wide = rows_ref.shape
    tile = rows // 2
    copies = []
    for side, start in enumerate((0, nrows - tile)):
        for i in range(parts):
            source = rows_ref.at[i, pl.ds(side * tile, tile)]
            target = image_ref.at[pl.ds(start, tile), pl.ds(i * wide, wide)]
            copy = pltpu.make_async_copy(source, target, sems.at[side * parts + i])
            copy.start()
            copies.append(copy)
    for keep_ref in keep_refs:
        own = 1 - leaving_half(parts)
        keep = add_edges(part_ref, end_tiles(basis_ref, tile), rows_ref, own)
        put_blocks(keep_ref, keep, orders, own)
    for copy in copies:
        copy.wait()


def whole(memory_space=pltpu.VMEM):
    return pl.BlockSpec(memory_space=memory_space)


def local(basis, jac_blocks, block_cols, live_slots, accumulation):
    nrows, width = basis.shape
    nblk, slots, bsize, _ = jac_blocks.shape
    tile = 2 * bsize
    outer, inner, across = (lax.axis_size(axis) for axis in AXES)
    down = outer * inner
    count = down * across
    f32, bf16 = jnp.float32, jnp.bfloat16
    edge_shape = jax.ShapeDtypeStruct((tile, width), bf16)
    far_send = pl.pallas_call(
        far_kernel,
        out_shape=edge_shape,
        in_specs=[whole(pltpu.HBM)],
        out_specs=whole(),
        scratch_shapes=[pltpu.SemaphoreType.DMA],
        compiler_params=pltpu.CompilerParams(vmem_limit_bytes=4 * 2**20),
        cost_estimate=pl.CostEstimate(
            flops=2 * nrows * width * width * slots, bytes_accessed=0, transcendentals=0
        ),
        name="far_rows",
    )(pltpu.with_memory_space_constraint(basis, pltpu.HBM))
    near_send = pl.pallas_call(
        near_kernel,
        out_shape=edge_shape,
        in_specs=[whole()],
        out_specs=whole(),
        compiler_params=pltpu.CompilerParams(vmem_limit_bytes=4 * 2**20),
        name="near_rows",
    )(basis)
    swaps = [(i, i + 1) for i in range(1, count - 1, 2)]
    far = lax.ppermute(far_send, AXES, swaps + [(j, i) for i, j in swaps])
    swaps = [(i, i + 1) for i in range(0, count, 2)]
    near = lax.ppermute(near_send, AXES, swaps + [(j, i) for i, j in swaps])

    halved = across == 2
    parts = 2 if halved else 1
    wide = width // parts
    orders = [[0]]
    if halved:
        orders = [list(range(down))] * 2
        if (width // down) % 16 == 0:
            lines = [[o * inner + i for o in reversed(range(outer))] for i in range(inner)]
            orders = [sum(lines, []), sum(lines[:1] + lines[:0:-1], [])]
    image, edge, arm, part = pl.pallas_call(
        inner_kernel,
        out_shape=(
            jax.ShapeDtypeStruct((nrows, width), bf16),
            jax.ShapeDtypeStruct((2, tile, width), f32),
            jax.ShapeDtypeStruct((2, 2 * tile, tile), bf16),
            jax.ShapeDtypeStruct((parts, width, wide), f32),
        ),
        in_specs=[whole(pltpu.SMEM), whole(pltpu.SMEM), whole(), whole(), whole()],
        out_specs=(whole(pltpu.HBM), whole(), whole(), whole()),
        scratch_shapes=[
            pltpu.VMEM((nrows, width), bf16),
            pltpu.SemaphoreType.DMA((nblk // 6 + 1,)),
        ],
        compiler_params=pltpu.CompilerParams(vmem_limit_bytes=32 * 2**20),
        cost_estimate=pl.CostEstimate(
            flops=2 * nrows * width * (width + 12 * bsize),
            bytes_accessed=8 * 2**20,
            transcendentals=0,
        ),
        name="inner",
    )(
        block_cols.T,
        live_slots,
        jac_blocks,
        basis,
        accumulation.reshape(nblk // 2, tile),
    )

    rows, send = pl.pallas_call(
        functools.partial(edge_kernel, orders),
        out_shape=(
            jax.ShapeDtypeStruct((parts, 2 * tile, wide), bf16),
            jax.ShapeDtypeStruct((width, wide), bf16),
        ),
        in_specs=[whole()] * 6,
        out_specs=(whole(), whole()),
        compiler_params=pltpu.CompilerParams(vmem_limit_bytes=32 * 2**20),
        name="edges",
    )(far, near, edge, arm, basis, part)
    image, *keep = pl.pallas_call(
        functools.partial(keep_kernel, orders),
        out_shape=(
            jax.ShapeDtypeStruct((nrows, width), bf16),
            *([jax.ShapeDtypeStruct((width, wide), f32)] if halved else []),
        ),
        in_specs=[whole(), whole(), whole(), whole(pl.ANY)],
        out_specs=(whole(pl.ANY), *([whole()] if halved else [])),
        scratch_shapes=[pltpu.SemaphoreType.DMA((2 * parts,))],
        input_output_aliases={3: 0},
        compiler_params=pltpu.CompilerParams(vmem_limit_bytes=32 * 2**20),
        cost_estimate=pl.CostEstimate(
            flops=4 * tile * width * width, bytes_accessed=2**21, transcendentals=0
        ),
        name="kept_half",
    )(basis, rows, part, image)
    if halved:
        got = lax.ppermute(send, "col", [(0, 1), (1, 0)])
        total = (keep[0] + got.astype(f32)).astype(bf16)
        total = total.reshape(down, width // down, wide)
        groups = [[m * across + c for m in orders[c]] for c in range(across)]
        got = lax.all_to_all(total, AXES, 0, 0, axis_index_groups=groups, tiled=True)
    else:
        total = send.reshape(down, width // down, across, width // across)
        total = total.transpose(0, 2, 1, 3)
        total = total.reshape(count, width // down, width // across)
        got = lax.all_to_all(total, AXES, 0, 0, tiled=True)
    projected = jnp.sum(got.astype(f32), axis=0) * (1.0 / (nrows * count))
    return (image, projected)


def solution(mesh):
    rows, cols = mesh.devices.shape
    outer = 4 if rows % 4 == 0 else 1
    split = jax.sharding.Mesh(mesh.devices.reshape(outer, rows // outer, cols), AXES)
    return jax.shard_map(
        local,
        mesh=split,
        in_specs=(
            P(AXES, None),
            P(AXES, None, None, None),
            P(AXES, None),
            P(AXES),
            P(AXES),
        ),
        out_specs=(P(AXES, None), P(AXES[:2], "col")),
        check_vma=False,
    )
```

```python
import functools

import jax
import jax.numpy as jnp
from jax import lax
from jax.experimental import pallas as pl
from jax.experimental.pallas import tpu as pltpu
from jax.sharding import PartitionSpec as P

REACH = 2
AXES = ("outer", "inner", "col")
ROWS_DOT = (((0,), (0,)), ((), ()))


def strip_of(cols_ref, live_ref, jac_ref, acc_ref, first, pair):
    _, slots, bsize, _ = jac_ref.shape
    tile = 2 * bsize
    half = lax.broadcasted_iota(jnp.int32, (1, tile), 1) // bsize
    row = lax.broadcasted_iota(jnp.int32, (bsize, tile), 0)
    lane = lax.broadcasted_iota(jnp.int32, (bsize, tile), 1)
    weight = acc_ref[pair : pair + 1, :]
    halves = []
    for side in range(2):
        g = 2 * pair + side
        tiles = [None, jnp.where(lane == row + side * bsize, weight, 0.0), None]
        for s in range(slots):
            place = cols_ref[s, g] - (first + 2 * pair) + REACH
            place = jnp.where(s < live_ref[g], place, -1)
            block = jac_ref[g, s]
            wide = jnp.concatenate([block, block], axis=1).astype(jnp.float32)
            for t in range(3):
                here = jnp.where(half + 2 * t == place, 1.0, 0.0)
                term = wide * here
                tiles[t] = term if tiles[t] is None else tiles[t] + term
        halves.append(jnp.concatenate(tiles, axis=1))
    strip = jnp.concatenate(halves, axis=0)
    high = strip.astype(jnp.bfloat16)
    low = (strip - high.astype(jnp.float32)).astype(jnp.bfloat16)
    return jnp.concatenate([high, low], axis=0)


def gathered_rows(cols_ref, live_ref, jac_ref, basis_ref, first, g):
    nblk, slots, bsize, _ = jac_ref.shape
    lane = lax.broadcasted_iota(jnp.int32, (1, slots * bsize), 1)
    keep = jnp.where(lane < live_ref[g] * bsize, 1.0, 0.0).astype(jnp.bfloat16)
    blocks = jnp.concatenate([jac_ref[g, s] for s in range(slots)], axis=1) * keep
    rows = []
    for s in range(slots):
        at = jnp.clip(cols_ref[s, g] - first, 0, nblk - 1) * bsize
        rows.append(basis_ref[pl.ds(pl.multiple_of(at, bsize), bsize), :])
    rows = jnp.concatenate(rows, axis=0)
    return jnp.dot(blocks, rows, preferred_element_type=jnp.float32)


def apply_strip(strip, rows):
    both = jnp.dot(strip, rows, preferred_element_type=jnp.float32)
    half = strip.shape[0] // 2
    return both[:half] + both[half:]


def far_kernel(basis_hbm, far_ref, sem):
    tile = far_ref.shape[0]
    last = basis_hbm.shape[0] - tile
    odd = lax.rem(lax.axis_index(AXES), 2)
    where = pl.ds(pl.multiple_of(odd * last, tile), tile)
    copy = pltpu.make_async_copy(basis_hbm.at[where], far_ref, sem)
    copy.start()
    copy.wait()


def hand_on_kernel(rows_ref, out_ref):
    out_ref[...] = rows_ref[...]


def near_kernel(basis_ref, near_ref):
    tile = near_ref.shape[0]
    last = basis_ref.shape[0] - tile
    odd = lax.rem(lax.axis_index(AXES), 2)
    where = pl.ds(pl.multiple_of((1 - odd) * last, tile), tile)
    near_ref[...] = basis_ref[where, :]


def inner_kernel(
    cols_ref, live_ref, jac_ref, basis_ref, acc_ref,
    image_ref, edge_ref, arm_ref, part_ref, staged, sems,
):
    nblk, _, bsize, _ = jac_ref.shape
    nrows = basis_ref.shape[0]
    tile = 2 * bsize
    pairs = nblk // 2
    first = lax.axis_index(AXES) * nblk

    def project(start, stop):
        total = lax.dot_general(
            basis_ref[start:stop, :], staged[start:stop, :], ROWS_DOT,
            preferred_element_type=jnp.float32,
        )
        parts, _, wide = part_ref.shape
        return [total[:, i * wide : (i + 1) * wide] for i in range(parts)]

    def store(start, stop, at):
        where = pl.ds(start, stop - start)
        copy = pltpu.make_async_copy(staged.at[where], image_ref.at[where], sems.at[at])
        copy.start()
        return copy

    row = lax.broadcasted_iota(jnp.int32, (tile, tile), 0)
    lane = lax.broadcasted_iota(jnp.int32, (tile, tile), 1)
    middle = (pairs // 2) * tile
    stored = tile
    copies = []
    for pair in range(1, pairs - 1):
        start = pair * tile
        stop = start + tile
        weight = jnp.where(lane == row, acc_ref[pair : pair + 1, :], 0.0)
        weight = jnp.sum(weight, axis=1, keepdims=True)
        coupled = [
            gathered_rows(cols_ref, live_ref, jac_ref, basis_ref, first, 2 * pair + side)
            for side in range(2)
        ]
        own = basis_ref[start:stop, :].astype(jnp.float32)
        total = jnp.concatenate(coupled, axis=0) + weight * own
        staged[start:stop, :] = total.astype(jnp.bfloat16)
        if pair % 3 == 0 or pair == pairs - 2:
            copies.append(store(stored, stop, len(copies)))
            stored = stop
        if stop == middle:
            for i, half in enumerate(project(tile, middle)):
                part_ref[i] = half
    for side, pair in enumerate((0, pairs - 1)):
        strip = strip_of(cols_ref, live_ref, jac_ref, acc_ref, first, pair)
        if side == 0:
            edge_ref[0] = apply_strip(strip[:, tile:], basis_ref[: 2 * tile, :])
            arm_ref[0] = strip[:, :tile]
        else:
            edge_ref[1] = apply_strip(strip[:, : 2 * tile], basis_ref[nrows - 2 * tile :, :])
            arm_ref[1] = strip[:, 2 * tile :]
    for i, half in enumerate(project(middle, nrows - tile)):
        part_ref[i] += half
    for copy in copies:
        copy.wait()


def end_tiles(basis_ref, tile):
    nrows = basis_ref.shape[0]
    return jnp.concatenate([basis_ref[:tile, :], basis_ref[nrows - tile :, :]], axis=0)


def add_edges(part_ref, tiles, rows_ref, half):
    update = lax.dot_general(
        tiles, rows_ref[half], ROWS_DOT, preferred_element_type=jnp.float32
    )
    return part_ref[half] + update


def put_blocks(ref, value, orders, core):
    high = value.shape[0] // len(orders[0])
    blocks = [value[i * high : (i + 1) * high, :] for i in range(len(orders[0]))]
    for to, (first, second) in enumerate(zip(orders[0], orders[-1])):
        block = blocks[first]
        if first != second:
            block = jnp.where(core == 1, blocks[second], block)
        ref[to * high : (to + 1) * high, :] = block.astype(ref.dtype)


def leaving_half(parts):
    return 1 - lax.axis_index("col") if parts == 2 else 0


def edge_kernel(
    orders, far_ref, near_ref, edge_ref, arm_ref, basis_ref, part_ref, rows_ref, send_ref,
):
    tile = far_ref.shape[0]
    parts, _, wide = rows_ref.shape
    odd = lax.rem(lax.axis_index(AXES), 2) == 1
    near, far = near_ref[...], far_ref[...]
    halos = (jnp.where(odd, near, far), jnp.where(odd, far, near))
    for side in range(2):
        rows = edge_ref[side] + apply_strip(arm_ref[side], halos[side])
        rows = rows.astype(jnp.bfloat16)
        for i in range(parts):
            rows_ref[i, side * tile : (side + 1) * tile, :] = rows[:, i * wide : (i + 1) * wide]
    leaving = leaving_half(parts)
    send = add_edges(part_ref, end_tiles(basis_ref, tile), rows_ref, leaving)
    put_blocks(send_ref, send, orders, leaving)


def keep_kernel(orders, basis_ref, rows_ref, part_ref, _, image_ref, *rest):
    *keep_refs, sems = rest
    nrows = image_ref.shape[0]
    parts, rows, wide = rows_ref.shape
    tile = rows // 2
    copies = []
    for side, start in enumerate((0, nrows - tile)):
        for i in range(parts):
            source = rows_ref.at[i, pl.ds(side * tile, tile)]
            target = image_ref.at[pl.ds(start, tile), pl.ds(i * wide, wide)]
            copy = pltpu.make_async_copy(source, target, sems.at[side * parts + i])
            copy.start()
            copies.append(copy)
    for keep_ref in keep_refs:
        own = 1 - leaving_half(parts)
        keep = add_edges(part_ref, end_tiles(basis_ref, tile), rows_ref, own)
        put_blocks(keep_ref, keep, orders, own)
    for copy in copies:
        copy.wait()


def whole(memory_space=pltpu.VMEM):
    return pl.BlockSpec(memory_space=memory_space)


def local(basis, jac_blocks, block_cols, live_slots, accumulation):
    nrows, width = basis.shape
    nblk, slots, bsize, _ = jac_blocks.shape
    tile = 2 * bsize
    outer, inner, across = (lax.axis_size(axis) for axis in AXES)
    down = outer * inner
    count = down * across
    f32, bf16 = jnp.float32, jnp.bfloat16
    edge_shape = jax.ShapeDtypeStruct((tile, width), bf16)
    far_rows = pl.pallas_call(
        far_kernel,
        out_shape=edge_shape,
        in_specs=[whole(pltpu.HBM)],
        out_specs=whole(),
        scratch_shapes=[pltpu.SemaphoreType.DMA],
        compiler_params=pltpu.CompilerParams(vmem_limit_bytes=4 * 2**20),
        cost_estimate=pl.CostEstimate(flops=0, bytes_accessed=0, transcendentals=0),
        name="far_rows",
    )(pltpu.with_memory_space_constraint(basis, pltpu.HBM))
    far_send = pl.pallas_call(
        hand_on_kernel,
        out_shape=edge_shape,
        in_specs=[whole()],
        out_specs=whole(),
        compiler_params=pltpu.CompilerParams(vmem_limit_bytes=4 * 2**20),
        cost_estimate=pl.CostEstimate(
            flops=2 * nrows * width * width * slots, bytes_accessed=0, transcendentals=0
        ),
        name="hand_on",
    )(far_rows)
    near_send = pl.pallas_call(
        near_kernel,
        out_shape=edge_shape,
        in_specs=[whole()],
        out_specs=whole(),
        compiler_params=pltpu.CompilerParams(vmem_limit_bytes=4 * 2**20),
        name="near_rows",
    )(basis)
    swaps = [(i, i + 1) for i in range(1, count - 1, 2)]
    far = lax.ppermute(far_send, AXES, swaps + [(j, i) for i, j in swaps])
    swaps = [(i, i + 1) for i in range(0, count, 2)]
    near = lax.ppermute(near_send, AXES, swaps + [(j, i) for i, j in swaps])

    halved = across == 2
    parts = 2 if halved else 1
    wide = width // parts
    orders = [[0]]
    if halved:
        orders = [list(range(down))] * 2
        if (width // down) % 16 == 0:
            lines = [[o * inner + i for o in reversed(range(outer))] for i in range(inner)]
            orders = [sum(lines, []), sum(lines[:1] + lines[:0:-1], [])]
    image, edge, arm, part = pl.pallas_call(
        inner_kernel,
        out_shape=(
            jax.ShapeDtypeStruct((nrows, width), bf16),
            jax.ShapeDtypeStruct((2, tile, width), f32),
            jax.ShapeDtypeStruct((2, 2 * tile, tile), bf16),
            jax.ShapeDtypeStruct((parts, width, wide), f32),
        ),
        in_specs=[whole(pltpu.SMEM), whole(pltpu.SMEM), whole(), whole(), whole()],
        out_specs=(whole(pltpu.HBM), whole(), whole(), whole()),
        scratch_shapes=[
            pltpu.VMEM((nrows, width), bf16),
            pltpu.SemaphoreType.DMA((nblk // 6 + 1,)),
        ],
        compiler_params=pltpu.CompilerParams(vmem_limit_bytes=32 * 2**20),
        cost_estimate=pl.CostEstimate(
            flops=2 * nrows * width * (width + 12 * bsize),
            bytes_accessed=8 * 2**20,
            transcendentals=0,
        ),
        name="inner",
    )(
        block_cols.T,
        live_slots,
        jac_blocks,
        basis,
        accumulation.reshape(nblk // 2, tile),
    )

    rows, send = pl.pallas_call(
        functools.partial(edge_kernel, orders),
        out_shape=(
            jax.ShapeDtypeStruct((parts, 2 * tile, wide), bf16),
            jax.ShapeDtypeStruct((width, wide), bf16),
        ),
        in_specs=[whole()] * 6,
        out_specs=(whole(), whole()),
        compiler_params=pltpu.CompilerParams(vmem_limit_bytes=32 * 2**20),
        name="edges",
    )(far, near, edge, arm, basis, part)
    image, *keep = pl.pallas_call(
        functools.partial(keep_kernel, orders),
        out_shape=(
            jax.ShapeDtypeStruct((nrows, width), bf16),
            *([jax.ShapeDtypeStruct((width, wide), f32)] if halved else []),
        ),
        in_specs=[whole(), whole(), whole(), whole(pl.ANY)],
        out_specs=(whole(pl.ANY), *([whole()] if halved else [])),
        scratch_shapes=[pltpu.SemaphoreType.DMA((2 * parts,))],
        input_output_aliases={3: 0},
        compiler_params=pltpu.CompilerParams(vmem_limit_bytes=32 * 2**20),
        cost_estimate=pl.CostEstimate(
            flops=4 * tile * width * width, bytes_accessed=2**21, transcendentals=0
        ),
        name="kept_half",
    )(basis, rows, part, image)
    if halved:
        got = lax.ppermute(send, "col", [(0, 1), (1, 0)])
        total = (keep[0] + got.astype(f32)).astype(bf16)
        total = total.reshape(down, width // down, wide)
        groups = [[m * across + c for m in orders[c]] for c in range(across)]
        got = lax.all_to_all(total, AXES, 0, 0, axis_index_groups=groups, tiled=True)
    else:
        total = send.reshape(down, width // down, across, width // across)
        total = total.transpose(0, 2, 1, 3)
        total = total.reshape(count, width // down, width // across)
        got = lax.all_to_all(total, AXES, 0, 0, tiled=True)
    projected = jnp.sum(got.astype(f32), axis=0) * (1.0 / (nrows * count))
    return (image, projected)


def solution(mesh):
    rows, cols = mesh.devices.shape
    outer = 4 if rows % 4 == 0 else 1
    split = jax.sharding.Mesh(mesh.devices.reshape(outer, rows // outer, cols), AXES)
    return jax.shard_map(
        local,
        mesh=split,
        in_specs=(
            P(AXES, None),
            P(AXES, None, None, None),
            P(AXES, None),
            P(AXES),
            P(AXES),
        ),
        out_specs=(P(AXES, None), P(AXES[:2], "col")),
        check_vma=False,
    )
```

```python
import functools

import jax
import jax.numpy as jnp
from jax import lax
from jax.experimental import pallas as pl
from jax.experimental.pallas import tpu as pltpu
from jax.sharding import PartitionSpec as P

REACH = 2
AXES = ("outer", "inner", "col")
ROWS_DOT = (((0,), (0,)), ((), ()))


def strip_of(cols_ref, live_ref, jac_ref, acc_ref, first, pair):
    _, slots, bsize, _ = jac_ref.shape
    tile = 2 * bsize
    half = lax.broadcasted_iota(jnp.int32, (1, tile), 1) // bsize
    row = lax.broadcasted_iota(jnp.int32, (bsize, tile), 0)
    lane = lax.broadcasted_iota(jnp.int32, (bsize, tile), 1)
    weight = acc_ref[pair : pair + 1, :]
    halves = []
    for side in range(2):
        g = 2 * pair + side
        tiles = [None, jnp.where(lane == row + side * bsize, weight, 0.0), None]
        for s in range(slots):
            place = cols_ref[s, g] - (first + 2 * pair) + REACH
            place = jnp.where(s < live_ref[g], place, -1)
            block = jac_ref[g, s]
            wide = jnp.concatenate([block, block], axis=1).astype(jnp.float32)
            for t in range(3):
                here = jnp.where(half + 2 * t == place, 1.0, 0.0)
                term = wide * here
                tiles[t] = term if tiles[t] is None else tiles[t] + term
        halves.append(jnp.concatenate(tiles, axis=1))
    strip = jnp.concatenate(halves, axis=0)
    high = strip.astype(jnp.bfloat16)
    low = (strip - high.astype(jnp.float32)).astype(jnp.bfloat16)
    return jnp.concatenate([high, low], axis=0)


def gathered_rows(cols_ref, live_ref, jac_ref, basis_ref, first, g):
    nblk, slots, bsize, _ = jac_ref.shape
    lane = lax.broadcasted_iota(jnp.int32, (1, slots * bsize), 1)
    keep = jnp.where(lane < live_ref[g] * bsize, 1.0, 0.0).astype(jnp.bfloat16)
    blocks = jnp.concatenate([jac_ref[g, s] for s in range(slots)], axis=1) * keep
    rows = []
    for s in range(slots):
        at = jnp.clip(cols_ref[s, g] - first, 0, nblk - 1) * bsize
        rows.append(basis_ref[pl.ds(pl.multiple_of(at, bsize), bsize), :])
    rows = jnp.concatenate(rows, axis=0)
    return jnp.dot(blocks, rows, preferred_element_type=jnp.float32)


def apply_strip(strip, rows):
    both = jnp.dot(strip, rows, preferred_element_type=jnp.float32)
    half = strip.shape[0] // 2
    return both[:half] + both[half:]


def far_kernel(basis_hbm, far_ref, sem):
    tile = far_ref.shape[0]
    last = basis_hbm.shape[0] - tile
    odd = lax.rem(lax.axis_index(AXES), 2)
    where = pl.ds(pl.multiple_of(odd * last, tile), tile)
    copy = pltpu.make_async_copy(basis_hbm.at[where], far_ref, sem)
    copy.start()
    copy.wait()


def hand_on_kernel(rows_ref, out_ref):
    out_ref[...] = rows_ref[...]


def near_kernel(basis_ref, near_ref):
    tile = near_ref.shape[0]
    last = basis_ref.shape[0] - tile
    odd = lax.rem(lax.axis_index(AXES), 2)
    where = pl.ds(pl.multiple_of((1 - odd) * last, tile), tile)
    near_ref[...] = basis_ref[where, :]


def inner_kernel(
    cols_ref, live_ref, jac_ref, basis_ref, acc_ref,
    image_ref, edge_ref, arm_ref, part_ref, staged, sems,
):
    nblk, _, bsize, _ = jac_ref.shape
    nrows = basis_ref.shape[0]
    tile = 2 * bsize
    pairs = nblk // 2
    first = lax.axis_index(AXES) * nblk

    def project(start, stop):
        total = lax.dot_general(
            basis_ref[start:stop, :], staged[start:stop, :], ROWS_DOT,
            preferred_element_type=jnp.float32,
        )
        parts, _, wide = part_ref.shape
        return [total[:, i * wide : (i + 1) * wide] for i in range(parts)]

    def store(start, stop, at):
        where = pl.ds(start, stop - start)
        copy = pltpu.make_async_copy(staged.at[where], image_ref.at[where], sems.at[at])
        copy.start()
        return copy

    row = lax.broadcasted_iota(jnp.int32, (tile, tile), 0)
    lane = lax.broadcasted_iota(jnp.int32, (tile, tile), 1)
    middle = (pairs // 2) * tile
    stored = tile
    copies = []
    for pair in range(1, pairs - 1):
        start = pair * tile
        stop = start + tile
        weight = jnp.where(lane == row, acc_ref[pair : pair + 1, :], 0.0)
        weight = jnp.sum(weight, axis=1, keepdims=True)
        coupled = [
            gathered_rows(cols_ref, live_ref, jac_ref, basis_ref, first, 2 * pair + side)
            for side in range(2)
        ]
        own = basis_ref[start:stop, :].astype(jnp.float32)
        total = jnp.concatenate(coupled, axis=0) + weight * own
        staged[start:stop, :] = total.astype(jnp.bfloat16)
        if pair % 3 == 0 or pair == pairs - 2:
            copies.append(store(stored, stop, len(copies)))
            stored = stop
        if stop == middle:
            for i, half in enumerate(project(tile, middle)):
                part_ref[i] = half
    for side, pair in enumerate((0, pairs - 1)):
        strip = strip_of(cols_ref, live_ref, jac_ref, acc_ref, first, pair)
        if side == 0:
            edge_ref[0] = apply_strip(strip[:, tile:], basis_ref[: 2 * tile, :])
            arm_ref[0] = strip[:, :tile]
        else:
            edge_ref[1] = apply_strip(strip[:, : 2 * tile], basis_ref[nrows - 2 * tile :, :])
            arm_ref[1] = strip[:, 2 * tile :]
    for i, half in enumerate(project(middle, nrows - tile)):
        part_ref[i] += half
    for copy in copies:
        copy.wait()


def end_tiles(basis_ref, tile):
    nrows = basis_ref.shape[0]
    return jnp.concatenate([basis_ref[:tile, :], basis_ref[nrows - tile :, :]], axis=0)


def add_edges(part_ref, tiles, rows_ref, half):
    update = lax.dot_general(
        tiles, rows_ref[half], ROWS_DOT, preferred_element_type=jnp.float32
    )
    return part_ref[half] + update


def put_blocks(ref, value, orders, core):
    high = value.shape[0] // len(orders[0])
    blocks = [value[i * high : (i + 1) * high, :] for i in range(len(orders[0]))]
    for to, (first, second) in enumerate(zip(orders[0], orders[-1])):
        block = blocks[first]
        if first != second:
            block = jnp.where(core == 1, blocks[second], block)
        ref[to * high : (to + 1) * high, :] = block.astype(ref.dtype)


def leaving_half(parts):
    return 1 - lax.axis_index("col") if parts == 2 else 0


def edge_kernel(
    orders, far_ref, near_ref, edge_ref, arm_ref, basis_ref, part_ref, rows_ref, send_ref,
):
    tile = far_ref.shape[0]
    parts, _, wide = rows_ref.shape
    odd = lax.rem(lax.axis_index(AXES), 2) == 1
    near, far = near_ref[...], far_ref[...]
    halos = (jnp.where(odd, near, far), jnp.where(odd, far, near))
    for side in range(2):
        rows = edge_ref[side] + apply_strip(arm_ref[side], halos[side])
        rows = rows.astype(jnp.bfloat16)
        for i in range(parts):
            rows_ref[i, side * tile : (side + 1) * tile, :] = rows[:, i * wide : (i + 1) * wide]
    leaving = leaving_half(parts)
    send = add_edges(part_ref, end_tiles(basis_ref, tile), rows_ref, leaving)
    put_blocks(send_ref, send, orders, leaving)


def keep_kernel(orders, basis_ref, rows_ref, part_ref, _, image_ref, *rest):
    *keep_refs, sems = rest
    nrows = image_ref.shape[0]
    parts, rows, wide = rows_ref.shape
    tile = rows // 2
    copies = []
    for side, start in enumerate((0, nrows - tile)):
        for i in range(parts):
            source = rows_ref.at[i, pl.ds(side * tile, tile)]
            target = image_ref.at[pl.ds(start, tile), pl.ds(i * wide, wide)]
            copy = pltpu.make_async_copy(source, target, sems.at[side * parts + i])
            copy.start()
            copies.append(copy)
    for keep_ref in keep_refs:
        own = 1 - leaving_half(parts)
        keep = add_edges(part_ref, end_tiles(basis_ref, tile), rows_ref, own)
        put_blocks(keep_ref, keep, orders, own)
    for copy in copies:
        copy.wait()


def whole(memory_space=pltpu.VMEM):
    return pl.BlockSpec(memory_space=memory_space)


def local(basis, jac_blocks, block_cols, live_slots, accumulation):
    nrows, width = basis.shape
    nblk, slots, bsize, _ = jac_blocks.shape
    tile = 2 * bsize
    outer, inner, across = (lax.axis_size(axis) for axis in AXES)
    down = outer * inner
    count = down * across
    f32, bf16 = jnp.float32, jnp.bfloat16
    edge_shape = jax.ShapeDtypeStruct((tile, width), bf16)
    far_rows = pl.pallas_call(
        far_kernel,
        out_shape=edge_shape,
        in_specs=[whole(pltpu.HBM)],
        out_specs=whole(),
        scratch_shapes=[pltpu.SemaphoreType.DMA],
        compiler_params=pltpu.CompilerParams(vmem_limit_bytes=4 * 2**20),
        cost_estimate=pl.CostEstimate(flops=0, bytes_accessed=0, transcendentals=0),
        name="far_rows",
    )(pltpu.with_memory_space_constraint(basis, pltpu.HBM))
    far_send = pl.pallas_call(
        hand_on_kernel,
        out_shape=edge_shape,
        in_specs=[whole()],
        out_specs=whole(),
        compiler_params=pltpu.CompilerParams(vmem_limit_bytes=4 * 2**20),
        cost_estimate=pl.CostEstimate(
            flops=2 * nrows * width * width * slots, bytes_accessed=0, transcendentals=0
        ),
        name="hand_on",
    )(far_rows)
    near_send = pl.pallas_call(
        near_kernel,
        out_shape=edge_shape,
        in_specs=[whole()],
        out_specs=whole(),
        compiler_params=pltpu.CompilerParams(vmem_limit_bytes=4 * 2**20),
        name="near_rows",
    )(basis)
    swaps = [(i, i + 1) for i in range(1, count - 1, 2)]
    far = lax.ppermute(far_send, AXES, swaps + [(j, i) for i, j in swaps])
    swaps = [(i, i + 1) for i in range(0, count, 2)]
    near = lax.ppermute(near_send, AXES, swaps + [(j, i) for i, j in swaps])

    halved = across == 2
    parts = 2 if halved else 1
    wide = width // parts
    orders = [[0]]
    if halved:
        orders = [list(range(down))] * 2
        if (width // down) % 16 == 0:
            around = [*range(0, inner, 2), *range(1, inner, 2)[::-1]]
            lines = [[o * inner + i for o in reversed(range(outer))] for i in around]
            orders = [sum(lines, []), sum(lines[:1] + lines[:0:-1], [])]
    image, edge, arm, part = pl.pallas_call(
        inner_kernel,
        out_shape=(
            jax.ShapeDtypeStruct((nrows, width), bf16),
            jax.ShapeDtypeStruct((2, tile, width), f32),
            jax.ShapeDtypeStruct((2, 2 * tile, tile), bf16),
            jax.ShapeDtypeStruct((parts, width, wide), f32),
        ),
        in_specs=[whole(pltpu.SMEM), whole(pltpu.SMEM), whole(), whole(), whole()],
        out_specs=(whole(pltpu.HBM), whole(), whole(), whole()),
        scratch_shapes=[
            pltpu.VMEM((nrows, width), bf16),
            pltpu.SemaphoreType.DMA((nblk // 6 + 1,)),
        ],
        compiler_params=pltpu.CompilerParams(vmem_limit_bytes=32 * 2**20),
        cost_estimate=pl.CostEstimate(
            flops=2 * nrows * width * (width + 12 * bsize),
            bytes_accessed=8 * 2**20,
            transcendentals=0,
        ),
        name="inner",
    )(
        block_cols.T,
        live_slots,
        jac_blocks,
        basis,
        accumulation.reshape(nblk // 2, tile),
    )

    rows, send = pl.pallas_call(
        functools.partial(edge_kernel, orders),
        out_shape=(
            jax.ShapeDtypeStruct((parts, 2 * tile, wide), bf16),
            jax.ShapeDtypeStruct((width, wide), bf16),
        ),
        in_specs=[whole()] * 6,
        out_specs=(whole(), whole()),
        compiler_params=pltpu.CompilerParams(vmem_limit_bytes=32 * 2**20),
        name="edges",
    )(far, near, edge, arm, basis, part)
    image, *keep = pl.pallas_call(
        functools.partial(keep_kernel, orders),
        out_shape=(
            jax.ShapeDtypeStruct((nrows, width), bf16),
            *([jax.ShapeDtypeStruct((width, wide), f32)] if halved else []),
        ),
        in_specs=[whole(), whole(), whole(), whole(pl.ANY)],
        out_specs=(whole(pl.ANY), *([whole()] if halved else [])),
        scratch_shapes=[pltpu.SemaphoreType.DMA((2 * parts,))],
        input_output_aliases={3: 0},
        compiler_params=pltpu.CompilerParams(vmem_limit_bytes=32 * 2**20),
        cost_estimate=pl.CostEstimate(
            flops=4 * tile * width * width, bytes_accessed=2**21, transcendentals=0
        ),
        name="kept_half",
    )(basis, rows, part, image)
    if halved:
        got = lax.ppermute(send, "col", [(0, 1), (1, 0)])
        total = (keep[0] + got.astype(f32)).astype(bf16)
        total = total.reshape(down, width // down, wide)
        groups = [[m * across + c for m in orders[c]] for c in range(across)]
        got = lax.all_to_all(total, AXES, 0, 0, axis_index_groups=groups, tiled=True)
    else:
        total = send.reshape(down, width // down, across, width // across)
        total = total.transpose(0, 2, 1, 3)
        total = total.reshape(count, width // down, width // across)
        got = lax.all_to_all(total, AXES, 0, 0, tiled=True)
    projected = jnp.sum(got.astype(f32), axis=0) * (1.0 / (nrows * count))
    return (image, projected)


def solution(mesh):
    rows, cols = mesh.devices.shape
    outer = 4 if rows % 4 == 0 else 1
    split = jax.sharding.Mesh(mesh.devices.reshape(outer, rows // outer, cols), AXES)
    return jax.shard_map(
        local,
        mesh=split,
        in_specs=(
            P(AXES, None),
            P(AXES, None, None, None),
            P(AXES, None),
            P(AXES),
            P(AXES),
        ),
        out_specs=(P(AXES, None), P(AXES[:2], "col")),
        check_vma=False,
    )
```

```python
import functools

import jax
import jax.numpy as jnp
from jax import lax
from jax.experimental import pallas as pl
from jax.experimental.pallas import tpu as pltpu
from jax.sharding import PartitionSpec as P

REACH = 2
AXES = ("outer", "inner", "col")
ROWS_DOT = (((0,), (0,)), ((), ()))


def strip_of(cols_ref, live_ref, jac_ref, acc_ref, first, pair):
    _, slots, bsize, _ = jac_ref.shape
    tile = 2 * bsize
    half = lax.broadcasted_iota(jnp.int32, (1, tile), 1) // bsize
    row = lax.broadcasted_iota(jnp.int32, (bsize, tile), 0)
    lane = lax.broadcasted_iota(jnp.int32, (bsize, tile), 1)
    weight = acc_ref[pair : pair + 1, :]
    halves = []
    for side in range(2):
        g = 2 * pair + side
        tiles = [None, jnp.where(lane == row + side * bsize, weight, 0.0), None]
        for s in range(slots):
            place = cols_ref[s, g] - (first + 2 * pair) + REACH
            place = jnp.where(s < live_ref[g], place, -1)
            block = jac_ref[g, s]
            wide = jnp.concatenate([block, block], axis=1).astype(jnp.float32)
            for t in range(3):
                here = jnp.where(half + 2 * t == place, 1.0, 0.0)
                term = wide * here
                tiles[t] = term if tiles[t] is None else tiles[t] + term
        halves.append(jnp.concatenate(tiles, axis=1))
    strip = jnp.concatenate(halves, axis=0)
    high = strip.astype(jnp.bfloat16)
    low = (strip - high.astype(jnp.float32)).astype(jnp.bfloat16)
    return jnp.concatenate([high, low], axis=0)


def gathered_rows(cols_ref, live_ref, jac_ref, basis_ref, first, g):
    nblk, slots, bsize, _ = jac_ref.shape
    lane = lax.broadcasted_iota(jnp.int32, (1, slots * bsize), 1)
    keep = jnp.where(lane < live_ref[g] * bsize, 1.0, 0.0).astype(jnp.bfloat16)
    blocks = jnp.concatenate([jac_ref[g, s] for s in range(slots)], axis=1) * keep
    rows = []
    for s in range(slots):
        at = jnp.clip(cols_ref[s, g] - first, 0, nblk - 1) * bsize
        rows.append(basis_ref[pl.ds(pl.multiple_of(at, bsize), bsize), :])
    rows = jnp.concatenate(rows, axis=0)
    return jnp.dot(blocks, rows, preferred_element_type=jnp.float32)


def apply_strip(strip, rows):
    both = jnp.dot(strip, rows, preferred_element_type=jnp.float32)
    half = strip.shape[0] // 2
    return both[:half] + both[half:]


def far_kernel(basis_hbm, far_ref, sems):
    tile = far_ref.shape[0]
    last = basis_hbm.shape[0] - tile
    odd = lax.rem(lax.axis_index(AXES), 2)
    count = sems.shape[0]
    size = tile // count
    copies = []
    for i in range(count):
        source = pl.ds(pl.multiple_of(odd * last + i * size, size), size)
        target = far_ref.at[pl.ds(i * size, size)]
        copies.append(pltpu.make_async_copy(basis_hbm.at[source], target, sems.at[i]))
        copies[i].start()
    for copy in copies:
        copy.wait()


def hand_on_kernel(rows_ref, out_ref):
    out_ref[...] = rows_ref[...]


def near_kernel(basis_ref, near_ref):
    tile = near_ref.shape[0]
    last = basis_ref.shape[0] - tile
    odd = lax.rem(lax.axis_index(AXES), 2)
    where = pl.ds(pl.multiple_of((1 - odd) * last, tile), tile)
    near_ref[...] = basis_ref[where, :]


def inner_kernel(
    cols_ref, live_ref, jac_ref, basis_ref, acc_ref,
    image_ref, edge_ref, arm_ref, part_ref, staged, sems,
):
    nblk, _, bsize, _ = jac_ref.shape
    nrows = basis_ref.shape[0]
    tile = 2 * bsize
    pairs = nblk // 2
    first = lax.axis_index(AXES) * nblk

    def project(start, stop):
        total = lax.dot_general(
            basis_ref[start:stop, :], staged[start:stop, :], ROWS_DOT,
            preferred_element_type=jnp.float32,
        )
        parts, _, wide = part_ref.shape
        return [total[:, i * wide : (i + 1) * wide] for i in range(parts)]

    def store(start, stop, at):
        where = pl.ds(start, stop - start)
        copy = pltpu.make_async_copy(staged.at[where], image_ref.at[where], sems.at[at])
        copy.start()
        return copy

    row = lax.broadcasted_iota(jnp.int32, (tile, tile), 0)
    lane = lax.broadcasted_iota(jnp.int32, (tile, tile), 1)
    middle = (pairs // 2) * tile
    stored = tile
    copies = []
    for pair in range(1, pairs - 1):
        start = pair * tile
        stop = start + tile
        weight = jnp.where(lane == row, acc_ref[pair : pair + 1, :], 0.0)
        weight = jnp.sum(weight, axis=1, keepdims=True)
        coupled = [
            gathered_rows(cols_ref, live_ref, jac_ref, basis_ref, first, 2 * pair + side)
            for side in range(2)
        ]
        own = basis_ref[start:stop, :].astype(jnp.float32)
        total = jnp.concatenate(coupled, axis=0) + weight * own
        staged[start:stop, :] = total.astype(jnp.bfloat16)
        if pair % 3 == 0 or pair == pairs - 2:
            copies.append(store(stored, stop, len(copies)))
            stored = stop
        if stop == middle:
            for i, half in enumerate(project(tile, middle)):
                part_ref[i] = half
    for side, pair in enumerate((0, pairs - 1)):
        strip = strip_of(cols_ref, live_ref, jac_ref, acc_ref, first, pair)
        if side == 0:
            edge_ref[0] = apply_strip(strip[:, tile:], basis_ref[: 2 * tile, :])
            arm_ref[0] = strip[:, :tile]
        else:
            edge_ref[1] = apply_strip(strip[:, : 2 * tile], basis_ref[nrows - 2 * tile :, :])
            arm_ref[1] = strip[:, 2 * tile :]
    for i, half in enumerate(project(middle, nrows - tile)):
        part_ref[i] += half
    for copy in copies:
        copy.wait()


def end_tiles(basis_ref, tile):
    nrows = basis_ref.shape[0]
    return jnp.concatenate([basis_ref[:tile, :], basis_ref[nrows - tile :, :]], axis=0)


def add_edges(part_ref, tiles, rows_ref, half):
    update = lax.dot_general(
        tiles, rows_ref[half], ROWS_DOT, preferred_element_type=jnp.float32
    )
    return part_ref[half] + update


def put_blocks(ref, value, orders, core):
    high = value.shape[0] // len(orders[0])
    blocks = [value[i * high : (i + 1) * high, :] for i in range(len(orders[0]))]
    for to, (first, second) in enumerate(zip(orders[0], orders[-1])):
        block = blocks[first]
        if first != second:
            block = jnp.where(core == 1, blocks[second], block)
        ref[to * high : (to + 1) * high, :] = block.astype(ref.dtype)


def leaving_half(parts):
    return 1 - lax.axis_index("col") if parts == 2 else 0


def edge_kernel(
    orders, far_ref, near_ref, edge_ref, arm_ref, basis_ref, part_ref, rows_ref, send_ref,
):
    tile = far_ref.shape[0]
    parts, _, wide = rows_ref.shape
    odd = lax.rem(lax.axis_index(AXES), 2) == 1
    near, far = near_ref[...], far_ref[...]
    halos = (jnp.where(odd, near, far), jnp.where(odd, far, near))
    for side in range(2):
        rows = edge_ref[side] + apply_strip(arm_ref[side], halos[side])
        rows = rows.astype(jnp.bfloat16)
        for i in range(parts):
            rows_ref[i, side * tile : (side + 1) * tile, :] = rows[:, i * wide : (i + 1) * wide]
    leaving = leaving_half(parts)
    send = add_edges(part_ref, end_tiles(basis_ref, tile), rows_ref, leaving)
    put_blocks(send_ref, send, orders, leaving)


def keep_kernel(orders, basis_ref, rows_ref, part_ref, _, image_ref, *rest):
    *keep_refs, sems = rest
    nrows = image_ref.shape[0]
    parts, rows, wide = rows_ref.shape
    tile = rows // 2
    copies = []
    for side, start in enumerate((0, nrows - tile)):
        for i in range(parts):
            source = rows_ref.at[i, pl.ds(side * tile, tile)]
            target = image_ref.at[pl.ds(start, tile), pl.ds(i * wide, wide)]
            copy = pltpu.make_async_copy(source, target, sems.at[side * parts + i])
            copy.start()
            copies.append(copy)
    for keep_ref in keep_refs:
        own = 1 - leaving_half(parts)
        keep = add_edges(part_ref, end_tiles(basis_ref, tile), rows_ref, own)
        put_blocks(keep_ref, keep, orders, own)
    for copy in copies:
        copy.wait()


def whole(memory_space=pltpu.VMEM):
    return pl.BlockSpec(memory_space=memory_space)


def local(basis, jac_blocks, block_cols, live_slots, accumulation):
    nrows, width = basis.shape
    nblk, slots, bsize, _ = jac_blocks.shape
    tile = 2 * bsize
    outer, inner, across = (lax.axis_size(axis) for axis in AXES)
    down = outer * inner
    count = down * across
    f32, bf16 = jnp.float32, jnp.bfloat16
    edge_shape = jax.ShapeDtypeStruct((tile, width), bf16)
    far_rows = pl.pallas_call(
        far_kernel,
        out_shape=edge_shape,
        in_specs=[whole(pltpu.HBM)],
        out_specs=whole(),
        scratch_shapes=[pltpu.SemaphoreType.DMA((4,))],
        compiler_params=pltpu.CompilerParams(vmem_limit_bytes=4 * 2**20),
        cost_estimate=pl.CostEstimate(flops=0, bytes_accessed=0, transcendentals=0),
        name="far_rows",
    )(pltpu.with_memory_space_constraint(basis, pltpu.HBM))
    far_send = pl.pallas_call(
        hand_on_kernel,
        out_shape=edge_shape,
        in_specs=[whole()],
        out_specs=whole(),
        compiler_params=pltpu.CompilerParams(vmem_limit_bytes=4 * 2**20),
        cost_estimate=pl.CostEstimate(
            flops=2 * nrows * width * width * slots, bytes_accessed=0, transcendentals=0
        ),
        name="hand_on",
    )(far_rows)
    near_send = pl.pallas_call(
        near_kernel,
        out_shape=edge_shape,
        in_specs=[whole()],
        out_specs=whole(),
        compiler_params=pltpu.CompilerParams(vmem_limit_bytes=4 * 2**20),
        name="near_rows",
    )(basis)
    swaps = [(i, i + 1) for i in range(1, count - 1, 2)]
    far = lax.ppermute(far_send, AXES, swaps + [(j, i) for i, j in swaps])
    swaps = [(i, i + 1) for i in range(0, count, 2)]
    near = lax.ppermute(near_send, AXES, swaps + [(j, i) for i, j in swaps])

    halved = across == 2
    parts = 2 if halved else 1
    wide = width // parts
    orders = [[0]]
    if halved:
        orders = [list(range(down))] * 2
        if (width // down) % 16 == 0:
            lines = [[o * inner + i for o in reversed(range(outer))] for i in range(inner)]
            orders = [sum(lines, []), sum(lines[:1] + lines[:0:-1], [])]
    image, edge, arm, part = pl.pallas_call(
        inner_kernel,
        out_shape=(
            jax.ShapeDtypeStruct((nrows, width), bf16),
            jax.ShapeDtypeStruct((2, tile, width), f32),
            jax.ShapeDtypeStruct((2, 2 * tile, tile), bf16),
            jax.ShapeDtypeStruct((parts, width, wide), f32),
        ),
        in_specs=[whole(pltpu.SMEM), whole(pltpu.SMEM), whole(), whole(), whole()],
        out_specs=(whole(pltpu.HBM), whole(), whole(), whole()),
        scratch_shapes=[
            pltpu.VMEM((nrows, width), bf16),
            pltpu.SemaphoreType.DMA((nblk // 6 + 1,)),
        ],
        compiler_params=pltpu.CompilerParams(vmem_limit_bytes=32 * 2**20),
        cost_estimate=pl.CostEstimate(
            flops=2 * nrows * width * (width + 12 * bsize),
            bytes_accessed=8 * 2**20,
            transcendentals=0,
        ),
        name="inner",
    )(
        block_cols.T,
        live_slots,
        jac_blocks,
        basis,
        accumulation.reshape(nblk // 2, tile),
    )

    rows, send = pl.pallas_call(
        functools.partial(edge_kernel, orders),
        out_shape=(
            jax.ShapeDtypeStruct((parts, 2 * tile, wide), bf16),
            jax.ShapeDtypeStruct((width, wide), bf16),
        ),
        in_specs=[whole()] * 6,
        out_specs=(whole(), whole()),
        compiler_params=pltpu.CompilerParams(vmem_limit_bytes=32 * 2**20),
        name="edges",
    )(far, near, edge, arm, basis, part)
    image, *keep = pl.pallas_call(
        functools.partial(keep_kernel, orders),
        out_shape=(
            jax.ShapeDtypeStruct((nrows, width), bf16),
            *([jax.ShapeDtypeStruct((width, wide), f32)] if halved else []),
        ),
        in_specs=[whole(), whole(), whole(), whole(pl.ANY)],
        out_specs=(whole(pl.ANY), *([whole()] if halved else [])),
        scratch_shapes=[pltpu.SemaphoreType.DMA((2 * parts,))],
        input_output_aliases={3: 0},
        compiler_params=pltpu.CompilerParams(vmem_limit_bytes=32 * 2**20),
        cost_estimate=pl.CostEstimate(
            flops=4 * tile * width * width, bytes_accessed=2**21, transcendentals=0
        ),
        name="kept_half",
    )(basis, rows, part, image)
    if halved:
        got = lax.ppermute(send, "col", [(0, 1), (1, 0)])
        total = (keep[0] + got.astype(f32)).astype(bf16)
        total = total.reshape(down, width // down, wide)
        groups = [[m * across + c for m in orders[c]] for c in range(across)]
        got = lax.all_to_all(total, AXES, 0, 0, axis_index_groups=groups, tiled=True)
    else:
        total = send.reshape(down, width // down, across, width // across)
        total = total.transpose(0, 2, 1, 3)
        total = total.reshape(count, width // down, width // across)
        got = lax.all_to_all(total, AXES, 0, 0, tiled=True)
    projected = jnp.sum(got.astype(f32), axis=0) * (1.0 / (nrows * count))
    return (image, projected)


def solution(mesh):
    rows, cols = mesh.devices.shape
    outer = 4 if rows % 4 == 0 else 1
    split = jax.sharding.Mesh(mesh.devices.reshape(outer, rows // outer, cols), AXES)
    return jax.shard_map(
        local,
        mesh=split,
        in_specs=(
            P(AXES, None),
            P(AXES, None, None, None),
            P(AXES, None),
            P(AXES),
            P(AXES),
        ),
        out_specs=(P(AXES, None), P(AXES[:2], "col")),
        check_vma=False,
    )
```

```python
import functools

import jax
import jax.numpy as jnp
from jax import lax
from jax.experimental import pallas as pl
from jax.experimental.pallas import tpu as pltpu
from jax.sharding import PartitionSpec as P

REACH = 2
AXES = ("outer", "inner", "col")
ROWS_DOT = (((0,), (0,)), ((), ()))


def strip_of(cols_ref, live_ref, jac_ref, acc_ref, first, pair):
    _, slots, bsize, _ = jac_ref.shape
    tile = 2 * bsize
    half = lax.broadcasted_iota(jnp.int32, (1, tile), 1) // bsize
    row = lax.broadcasted_iota(jnp.int32, (bsize, tile), 0)
    lane = lax.broadcasted_iota(jnp.int32, (bsize, tile), 1)
    weight = acc_ref[pair : pair + 1, :]
    halves = []
    for side in range(2):
        g = 2 * pair + side
        tiles = [None, jnp.where(lane == row + side * bsize, weight, 0.0), None]
        for s in range(slots):
            place = cols_ref[s, g] - (first + 2 * pair) + REACH
            place = jnp.where(s < live_ref[g], place, -1)
            block = jac_ref[g, s]
            wide = jnp.concatenate([block, block], axis=1).astype(jnp.float32)
            for t in range(3):
                here = jnp.where(half + 2 * t == place, 1.0, 0.0)
                term = wide * here
                tiles[t] = term if tiles[t] is None else tiles[t] + term
        halves.append(jnp.concatenate(tiles, axis=1))
    strip = jnp.concatenate(halves, axis=0)
    high = strip.astype(jnp.bfloat16)
    low = (strip - high.astype(jnp.float32)).astype(jnp.bfloat16)
    return jnp.concatenate([high, low], axis=0)


def gathered_rows(cols_ref, live_ref, jac_ref, basis_ref, first, g):
    nblk, slots, bsize, _ = jac_ref.shape
    lane = lax.broadcasted_iota(jnp.int32, (1, slots * bsize), 1)
    keep = jnp.where(lane < live_ref[g] * bsize, 1.0, 0.0).astype(jnp.bfloat16)
    blocks = jnp.concatenate([jac_ref[g, s] for s in range(slots)], axis=1) * keep
    rows = []
    for s in range(slots):
        at = jnp.clip(cols_ref[s, g] - first, 0, nblk - 1) * bsize
        rows.append(basis_ref[pl.ds(pl.multiple_of(at, bsize), bsize), :])
    rows = jnp.concatenate(rows, axis=0)
    return jnp.dot(blocks, rows, preferred_element_type=jnp.float32)


def apply_strip(strip, rows):
    both = jnp.dot(strip, rows, preferred_element_type=jnp.float32)
    half = strip.shape[0] // 2
    return both[:half] + both[half:]


def far_kernel(basis_hbm, far_ref, sems):
    tile = far_ref.shape[0]
    last = basis_hbm.shape[0] - tile
    odd = lax.rem(lax.axis_index(AXES), 2)
    count = sems.shape[0]
    size = tile // count
    copies = []
    for i in range(count):
        source = pl.ds(pl.multiple_of(odd * last + i * size, size), size)
        target = far_ref.at[pl.ds(i * size, size)]
        copies.append(pltpu.make_async_copy(basis_hbm.at[source], target, sems.at[i]))
        copies[i].start()
    for copy in copies:
        copy.wait()


def hand_on_kernel(rows_ref, out_ref):
    out_ref[...] = rows_ref[...]


def near_kernel(basis_ref, near_ref):
    tile = near_ref.shape[0]
    last = basis_ref.shape[0] - tile
    odd = lax.rem(lax.axis_index(AXES), 2)
    where = pl.ds(pl.multiple_of((1 - odd) * last, tile), tile)
    near_ref[...] = basis_ref[where, :]


def inner_kernel(
    cols_ref, live_ref, jac_ref, basis_ref, acc_ref,
    image_ref, edge_ref, arm_ref, part_ref, staged, sems,
):
    nblk, _, bsize, _ = jac_ref.shape
    nrows = basis_ref.shape[0]
    tile = 2 * bsize
    pairs = nblk // 2
    first = lax.axis_index(AXES) * nblk

    def project(start, stop):
        total = lax.dot_general(
            basis_ref[start:stop, :], staged[start:stop, :], ROWS_DOT,
            preferred_element_type=jnp.float32,
        )
        parts, _, wide = part_ref.shape
        return [total[:, i * wide : (i + 1) * wide] for i in range(parts)]

    def store(start, stop, at):
        where = pl.ds(start, stop - start)
        copy = pltpu.make_async_copy(staged.at[where], image_ref.at[where], sems.at[at])
        copy.start()
        return copy

    row = lax.broadcasted_iota(jnp.int32, (tile, tile), 0)
    lane = lax.broadcasted_iota(jnp.int32, (tile, tile), 1)
    middle = (pairs // 2) * tile
    stored = tile
    copies = []
    for pair in range(1, pairs - 1):
        start = pair * tile
        stop = start + tile
        weight = jnp.where(lane == row, acc_ref[pair : pair + 1, :], 0.0)
        weight = jnp.sum(weight, axis=1, keepdims=True)
        coupled = [
            gathered_rows(cols_ref, live_ref, jac_ref, basis_ref, first, 2 * pair + side)
            for side in range(2)
        ]
        own = basis_ref[start:stop, :].astype(jnp.float32)
        total = jnp.concatenate(coupled, axis=0) + weight * own
        staged[start:stop, :] = total.astype(jnp.bfloat16)
        if pair % 3 == 0 or pair == pairs - 2:
            copies.append(store(stored, stop, len(copies)))
            stored = stop
        if stop == middle:
            for i, half in enumerate(project(tile, middle)):
                part_ref[i] = half
    for side, pair in enumerate((0, pairs - 1)):
        strip = strip_of(cols_ref, live_ref, jac_ref, acc_ref, first, pair)
        if side == 0:
            edge_ref[0] = apply_strip(strip[:, tile:], basis_ref[: 2 * tile, :])
            arm_ref[0] = strip[:, :tile]
        else:
            edge_ref[1] = apply_strip(strip[:, : 2 * tile], basis_ref[nrows - 2 * tile :, :])
            arm_ref[1] = strip[:, 2 * tile :]
    for i, half in enumerate(project(middle, nrows - tile)):
        part_ref[i] += half
    for copy in copies:
        copy.wait()


def side_of(odd, near):
    return 1 - odd if near else odd


def edge_tile(basis_ref, side, tile):
    last = basis_ref.shape[0] - tile
    return basis_ref[pl.ds(pl.multiple_of(side * last, tile), tile), :]


def edge_image(halo_ref, edge_ref, arm_ref, side, rows_ref):
    rows = edge_ref[side] + apply_strip(arm_ref[side], halo_ref[...])
    rows = rows.astype(jnp.bfloat16)
    parts, _, wide = rows_ref.shape
    for i in range(parts):
        rows_ref[i] = rows[:, i * wide : (i + 1) * wide]


def add_edge(part_ref, tile_rows, rows_ref, half):
    update = lax.dot_general(
        tile_rows, rows_ref[half], ROWS_DOT, preferred_element_type=jnp.float32
    )
    return part_ref[half] + update


def put_blocks(ref, value, orders, core):
    high = value.shape[0] // len(orders[0])
    blocks = [value[i * high : (i + 1) * high, :] for i in range(len(orders[0]))]
    for to, (first, second) in enumerate(zip(orders[0], orders[-1])):
        block = blocks[first]
        if first != second:
            block = jnp.where(core == 1, blocks[second], block)
        ref[to * high : (to + 1) * high, :] = block.astype(ref.dtype)


def leaving_half(parts):
    return 1 - lax.axis_index("col") if parts == 2 else 0


def near_edge_kernel(near_ref, edge_ref, arm_ref, basis_ref, part_ref, rows_ref, sum_ref):
    tile = near_ref.shape[0]
    side = side_of(lax.rem(lax.axis_index(AXES), 2), True)
    edge_image(near_ref, edge_ref, arm_ref, side, rows_ref)
    tile_rows = edge_tile(basis_ref, side, tile)
    for half in range(rows_ref.shape[0]):
        sum_ref[half] = add_edge(part_ref, tile_rows, rows_ref, half)


def far_edge_kernel(
    orders, far_ref, edge_ref, arm_ref, basis_ref, part_ref, rows_ref, send_ref,
):
    tile = far_ref.shape[0]
    side = side_of(lax.rem(lax.axis_index(AXES), 2), False)
    edge_image(far_ref, edge_ref, arm_ref, side, rows_ref)
    leaving = leaving_half(rows_ref.shape[0])
    send = add_edge(part_ref, edge_tile(basis_ref, side, tile), rows_ref, leaving)
    put_blocks(send_ref, send, orders, leaving)


def keep_kernel(orders, basis_ref, near_ref, far_ref, part_ref, _, image_ref, *rest):
    *keep_refs, sems = rest
    nrows = image_ref.shape[0]
    parts, tile, wide = far_ref.shape
    odd = lax.rem(lax.axis_index(AXES), 2)
    copies = []
    for at, rows_ref in enumerate((far_ref, near_ref)):
        start = pl.multiple_of(side_of(odd, at == 1) * (nrows - tile), tile)
        for i in range(parts):
            target = image_ref.at[pl.ds(start, tile), pl.ds(i * wide, wide)]
            copy = pltpu.make_async_copy(rows_ref.at[i], target, sems.at[at * parts + i])
            copy.start()
            copies.append(copy)
    for keep_ref in keep_refs:
        own = 1 - leaving_half(parts)
        tile_rows = edge_tile(basis_ref, side_of(odd, False), tile)
        put_blocks(keep_ref, add_edge(part_ref, tile_rows, far_ref, own), orders, own)
    for copy in copies:
        copy.wait()


def whole(memory_space=pltpu.VMEM):
    return pl.BlockSpec(memory_space=memory_space)


def local(basis, jac_blocks, block_cols, live_slots, accumulation):
    nrows, width = basis.shape
    nblk, slots, bsize, _ = jac_blocks.shape
    tile = 2 * bsize
    outer, inner, across = (lax.axis_size(axis) for axis in AXES)
    down = outer * inner
    count = down * across
    f32, bf16 = jnp.float32, jnp.bfloat16
    edge_shape = jax.ShapeDtypeStruct((tile, width), bf16)
    far_rows = pl.pallas_call(
        far_kernel,
        out_shape=edge_shape,
        in_specs=[whole(pltpu.HBM)],
        out_specs=whole(),
        scratch_shapes=[pltpu.SemaphoreType.DMA((4,))],
        compiler_params=pltpu.CompilerParams(vmem_limit_bytes=4 * 2**20),
        cost_estimate=pl.CostEstimate(flops=0, bytes_accessed=0, transcendentals=0),
        name="far_rows",
    )(pltpu.with_memory_space_constraint(basis, pltpu.HBM))
    far_send = pl.pallas_call(
        hand_on_kernel,
        out_shape=edge_shape,
        in_specs=[whole()],
        out_specs=whole(),
        compiler_params=pltpu.CompilerParams(vmem_limit_bytes=4 * 2**20),
        cost_estimate=pl.CostEstimate(
            flops=2 * nrows * width * width * slots, bytes_accessed=0, transcendentals=0
        ),
        name="hand_on",
    )(far_rows)
    near_send = pl.pallas_call(
        near_kernel,
        out_shape=edge_shape,
        in_specs=[whole()],
        out_specs=whole(),
        compiler_params=pltpu.CompilerParams(vmem_limit_bytes=4 * 2**20),
        name="near_rows",
    )(basis)
    swaps = [(i, i + 1) for i in range(1, count - 1, 2)]
    far = lax.ppermute(far_send, AXES, swaps + [(j, i) for i, j in swaps])
    swaps = [(i, i + 1) for i in range(0, count, 2)]
    near = lax.ppermute(near_send, AXES, swaps + [(j, i) for i, j in swaps])

    halved = across == 2
    parts = 2 if halved else 1
    wide = width // parts
    orders = [[0]]
    if halved:
        orders = [list(range(down))] * 2
        if (width // down) % 16 == 0:
            lines = [[o * inner + i for o in reversed(range(outer))] for i in range(inner)]
            orders = [sum(lines, []), sum(lines[:1] + lines[:0:-1], [])]
    image, edge, arm, part = pl.pallas_call(
        inner_kernel,
        out_shape=(
            jax.ShapeDtypeStruct((nrows, width), bf16),
            jax.ShapeDtypeStruct((2, tile, width), f32),
            jax.ShapeDtypeStruct((2, 2 * tile, tile), bf16),
            jax.ShapeDtypeStruct((parts, width, wide), f32),
        ),
        in_specs=[whole(pltpu.SMEM), whole(pltpu.SMEM), whole(), whole(), whole()],
        out_specs=(whole(pltpu.HBM), whole(), whole(), whole()),
        scratch_shapes=[
            pltpu.VMEM((nrows, width), bf16),
            pltpu.SemaphoreType.DMA((nblk // 6 + 1,)),
        ],
        compiler_params=pltpu.CompilerParams(vmem_limit_bytes=32 * 2**20),
        cost_estimate=pl.CostEstimate(
            flops=2 * nrows * width * (width + 12 * bsize),
            bytes_accessed=8 * 2**20,
            transcendentals=0,
        ),
        name="inner",
    )(
        block_cols.T,
        live_slots,
        jac_blocks,
        basis,
        accumulation.reshape(nblk // 2, tile),
    )

    limit = pltpu.CompilerParams(vmem_limit_bytes=32 * 2**20)
    rows_shape = jax.ShapeDtypeStruct((parts, tile, wide), bf16)
    near_rows, part = pl.pallas_call(
        near_edge_kernel,
        out_shape=(rows_shape, jax.ShapeDtypeStruct((parts, width, wide), f32)),
        in_specs=[whole()] * 5,
        out_specs=(whole(), whole()),
        compiler_params=limit,
        cost_estimate=pl.CostEstimate(
            flops=2 * tile * width * width, bytes_accessed=2**21, transcendentals=0
        ),
        name="near_edge",
    )(near, edge, arm, basis, part)
    far_rows, send = pl.pallas_call(
        functools.partial(far_edge_kernel, orders),
        out_shape=(rows_shape, jax.ShapeDtypeStruct((width, wide), bf16)),
        in_specs=[whole()] * 5,
        out_specs=(whole(), whole()),
        compiler_params=limit,
        name="far_edge",
    )(far, edge, arm, basis, part)
    image, *keep = pl.pallas_call(
        functools.partial(keep_kernel, orders),
        out_shape=(
            jax.ShapeDtypeStruct((nrows, width), bf16),
            *([jax.ShapeDtypeStruct((width, wide), f32)] if halved else []),
        ),
        in_specs=[whole(), whole(), whole(), whole(), whole(pl.ANY)],
        out_specs=(whole(pl.ANY), *([whole()] if halved else [])),
        scratch_shapes=[pltpu.SemaphoreType.DMA((2 * parts,))],
        input_output_aliases={4: 0},
        compiler_params=pltpu.CompilerParams(vmem_limit_bytes=32 * 2**20),
        cost_estimate=pl.CostEstimate(
            flops=4 * tile * width * width, bytes_accessed=2**21, transcendentals=0
        ),
        name="kept_half",
    )(basis, near_rows, far_rows, part, image)
    if halved:
        got = lax.ppermute(send, "col", [(0, 1), (1, 0)])
        total = (keep[0] + got.astype(f32)).astype(bf16)
        total = total.reshape(down, width // down, wide)
        groups = [[m * across + c for m in orders[c]] for c in range(across)]
        got = lax.all_to_all(total, AXES, 0, 0, axis_index_groups=groups, tiled=True)
    else:
        total = send.reshape(down, width // down, across, width // across)
        total = total.transpose(0, 2, 1, 3)
        total = total.reshape(count, width // down, width // across)
        got = lax.all_to_all(total, AXES, 0, 0, tiled=True)
    projected = jnp.sum(got.astype(f32), axis=0) * (1.0 / (nrows * count))
    return (image, projected)


def solution(mesh):
    rows, cols = mesh.devices.shape
    outer = 4 if rows % 4 == 0 else 1
    split = jax.sharding.Mesh(mesh.devices.reshape(outer, rows // outer, cols), AXES)
    return jax.shard_map(
        local,
        mesh=split,
        in_specs=(
            P(AXES, None),
            P(AXES, None, None, None),
            P(AXES, None),
            P(AXES),
            P(AXES),
        ),
        out_specs=(P(AXES, None), P(AXES[:2], "col")),
        check_vma=False,
    )
```

```python
import functools

import jax
import jax.numpy as jnp
from jax import lax
from jax.experimental import pallas as pl
from jax.experimental.pallas import tpu as pltpu
from jax.sharding import PartitionSpec as P

REACH = 2
AXES = ("outer", "inner", "col")
ROWS_DOT = (((0,), (0,)), ((), ()))


def strip_of(cols_ref, live_ref, jac_ref, acc_ref, first, pair):
    _, slots, bsize, _ = jac_ref.shape
    tile = 2 * bsize
    half = lax.broadcasted_iota(jnp.int32, (1, tile), 1) // bsize
    row = lax.broadcasted_iota(jnp.int32, (bsize, tile), 0)
    lane = lax.broadcasted_iota(jnp.int32, (bsize, tile), 1)
    weight = acc_ref[pair : pair + 1, :]
    halves = []
    for side in range(2):
        g = 2 * pair + side
        tiles = [None, jnp.where(lane == row + side * bsize, weight, 0.0), None]
        for s in range(slots):
            place = cols_ref[s, g] - (first + 2 * pair) + REACH
            place = jnp.where(s < live_ref[g], place, -1)
            block = jac_ref[g, s]
            wide = jnp.concatenate([block, block], axis=1).astype(jnp.float32)
            for t in range(3):
                here = jnp.where(half + 2 * t == place, 1.0, 0.0)
                term = wide * here
                tiles[t] = term if tiles[t] is None else tiles[t] + term
        halves.append(jnp.concatenate(tiles, axis=1))
    strip = jnp.concatenate(halves, axis=0)
    high = strip.astype(jnp.bfloat16)
    low = (strip - high.astype(jnp.float32)).astype(jnp.bfloat16)
    return jnp.concatenate([high, low], axis=0)


def gathered_rows(cols_ref, live_ref, jac_ref, basis_ref, first, g):
    nblk, slots, bsize, _ = jac_ref.shape
    lane = lax.broadcasted_iota(jnp.int32, (1, slots * bsize), 1)
    keep = jnp.where(lane < live_ref[g] * bsize, 1.0, 0.0).astype(jnp.bfloat16)
    blocks = jnp.concatenate([jac_ref[g, s] for s in range(slots)], axis=1) * keep
    rows = []
    for s in range(slots):
        at = jnp.clip(cols_ref[s, g] - first, 0, nblk - 1) * bsize
        rows.append(basis_ref[pl.ds(pl.multiple_of(at, bsize), bsize), :])
    rows = jnp.concatenate(rows, axis=0)
    return jnp.dot(blocks, rows, preferred_element_type=jnp.float32)


def apply_strip(strip, rows):
    both = jnp.dot(strip, rows, preferred_element_type=jnp.float32)
    half = strip.shape[0] // 2
    return both[:half] + both[half:]


def far_kernel(basis_hbm, far_ref, sems):
    tile = far_ref.shape[0]
    last = basis_hbm.shape[0] - tile
    odd = lax.rem(lax.axis_index(AXES), 2)
    count = sems.shape[0]
    size = tile // count
    copies = []
    for i in range(count):
        source = pl.ds(pl.multiple_of(odd * last + i * size, size), size)
        target = far_ref.at[pl.ds(i * size, size)]
        copies.append(pltpu.make_async_copy(basis_hbm.at[source], target, sems.at[i]))
        copies[i].start()
    for copy in copies:
        copy.wait()


def hand_on_kernel(rows_ref, out_ref):
    out_ref[...] = rows_ref[...]


def near_kernel(basis_ref, near_ref):
    tile = near_ref.shape[0]
    last = basis_ref.shape[0] - tile
    odd = lax.rem(lax.axis_index(AXES), 2)
    where = pl.ds(pl.multiple_of((1 - odd) * last, tile), tile)
    near_ref[...] = basis_ref[where, :]


def inner_kernel(
    cols_ref, live_ref, jac_ref, basis_ref, acc_ref,
    image_ref, edge_ref, arm_ref, part_ref, staged, sems,
):
    nblk, _, bsize, _ = jac_ref.shape
    nrows = basis_ref.shape[0]
    tile = 2 * bsize
    pairs = nblk // 2
    first = lax.axis_index(AXES) * nblk

    def project(start, stop):
        total = lax.dot_general(
            basis_ref[start:stop, :], staged[start:stop, :], ROWS_DOT,
            preferred_element_type=jnp.float32,
        )
        parts, _, wide = part_ref.shape
        return [total[:, i * wide : (i + 1) * wide] for i in range(parts)]

    def store(start, stop, at):
        where = pl.ds(start, stop - start)
        copy = pltpu.make_async_copy(staged.at[where], image_ref.at[where], sems.at[at])
        copy.start()
        return copy

    row = lax.broadcasted_iota(jnp.int32, (tile, tile), 0)
    lane = lax.broadcasted_iota(jnp.int32, (tile, tile), 1)
    middle = (pairs // 2) * tile
    stored = tile
    copies = []
    for pair in range(1, pairs - 1):
        start = pair * tile
        stop = start + tile
        weight = jnp.where(lane == row, acc_ref[pair : pair + 1, :], 0.0)
        weight = jnp.sum(weight, axis=1, keepdims=True)
        coupled = [
            gathered_rows(cols_ref, live_ref, jac_ref, basis_ref, first, 2 * pair + side)
            for side in range(2)
        ]
        own = basis_ref[start:stop, :].astype(jnp.float32)
        total = jnp.concatenate(coupled, axis=0) + weight * own
        staged[start:stop, :] = total.astype(jnp.bfloat16)
        if pair % 3 == 0 or pair == pairs - 2:
            copies.append(store(stored, stop, len(copies)))
            stored = stop
        if stop == middle:
            for i, half in enumerate(project(tile, middle)):
                part_ref[i] = half
    for side, pair in enumerate((0, pairs - 1)):
        strip = strip_of(cols_ref, live_ref, jac_ref, acc_ref, first, pair)
        if side == 0:
            edge_ref[0] = apply_strip(strip[:, tile:], basis_ref[: 2 * tile, :])
            arm_ref[0] = strip[:, :tile]
        else:
            edge_ref[1] = apply_strip(strip[:, : 2 * tile], basis_ref[nrows - 2 * tile :, :])
            arm_ref[1] = strip[:, 2 * tile :]
    for i, half in enumerate(project(middle, nrows - tile)):
        part_ref[i] += half
    for copy in copies:
        copy.wait()


def end_tiles(basis_ref, tile):
    nrows = basis_ref.shape[0]
    return jnp.concatenate([basis_ref[:tile, :], basis_ref[nrows - tile :, :]], axis=0)


def add_edges(part_ref, tiles, rows_ref, half):
    update = lax.dot_general(
        tiles, rows_ref[half], ROWS_DOT, preferred_element_type=jnp.float32
    )
    return part_ref[half] + update


def put_blocks(ref, value, orders, core):
    high = value.shape[0] // len(orders[0])
    blocks = [value[i * high : (i + 1) * high, :] for i in range(len(orders[0]))]
    for to, (first, second) in enumerate(zip(orders[0], orders[-1])):
        block = blocks[first]
        if first != second:
            block = jnp.where(core == 1, blocks[second], block)
        ref[to * high : (to + 1) * high, :] = block.astype(ref.dtype)


def leaving_half(parts):
    return 1 - lax.axis_index("col") if parts == 2 else 0


def edge_kernel(
    orders, far_ref, near_ref, edge_ref, arm_ref, basis_ref, part_ref, rows_ref, send_ref,
):
    tile = far_ref.shape[0]
    parts, _, wide = rows_ref.shape
    odd = lax.rem(lax.axis_index(AXES), 2) == 1
    near, far = near_ref[...], far_ref[...]
    halos = (jnp.where(odd, near, far), jnp.where(odd, far, near))
    for side in range(2):
        rows = edge_ref[side] + apply_strip(arm_ref[side], halos[side])
        rows = rows.astype(jnp.bfloat16)
        for i in range(parts):
            rows_ref[i, side * tile : (side + 1) * tile, :] = rows[:, i * wide : (i + 1) * wide]
    leaving = leaving_half(parts)
    send = add_edges(part_ref, end_tiles(basis_ref, tile), rows_ref, leaving)
    put_blocks(send_ref, send, orders, leaving)


def keep_kernel(orders, basis_ref, rows_ref, part_ref, _, image_ref, *rest):
    *keep_refs, sems = rest
    nrows = image_ref.shape[0]
    parts, rows, wide = rows_ref.shape
    tile = rows // 2
    copies = []
    for side, start in enumerate((0, nrows - tile)):
        for i in range(parts):
            source = rows_ref.at[i, pl.ds(side * tile, tile)]
            target = image_ref.at[pl.ds(start, tile), pl.ds(i * wide, wide)]
            copy = pltpu.make_async_copy(source, target, sems.at[side * parts + i])
            copy.start()
            copies.append(copy)
    for keep_ref in keep_refs:
        own = 1 - leaving_half(parts)
        keep = add_edges(part_ref, end_tiles(basis_ref, tile), rows_ref, own)
        put_blocks(keep_ref, keep, orders, own)
    for copy in copies:
        copy.wait()


def whole(memory_space=pltpu.VMEM):
    return pl.BlockSpec(memory_space=memory_space)


def local(basis, jac_blocks, block_cols, live_slots, accumulation):
    nrows, width = basis.shape
    nblk, slots, bsize, _ = jac_blocks.shape
    tile = 2 * bsize
    outer, inner, across = (lax.axis_size(axis) for axis in AXES)
    down = outer * inner
    count = down * across
    f32, bf16 = jnp.float32, jnp.bfloat16
    edge_shape = jax.ShapeDtypeStruct((tile, width), bf16)
    far_rows = pl.pallas_call(
        far_kernel,
        out_shape=edge_shape,
        in_specs=[whole(pltpu.HBM)],
        out_specs=whole(),
        scratch_shapes=[pltpu.SemaphoreType.DMA((4,))],
        compiler_params=pltpu.CompilerParams(vmem_limit_bytes=4 * 2**20),
        cost_estimate=pl.CostEstimate(flops=0, bytes_accessed=0, transcendentals=0),
        name="far_rows",
    )(pltpu.with_memory_space_constraint(basis, pltpu.HBM))
    far_send = pl.pallas_call(
        hand_on_kernel,
        out_shape=edge_shape,
        in_specs=[whole()],
        out_specs=whole(),
        compiler_params=pltpu.CompilerParams(vmem_limit_bytes=4 * 2**20),
        cost_estimate=pl.CostEstimate(
            flops=2 * nrows * width * width * slots, bytes_accessed=0, transcendentals=0
        ),
        name="hand_on",
    )(far_rows)
    near_send = pl.pallas_call(
        near_kernel,
        out_shape=edge_shape,
        in_specs=[whole()],
        out_specs=whole(),
        compiler_params=pltpu.CompilerParams(vmem_limit_bytes=4 * 2**20),
        name="near_rows",
    )(basis)
    swaps = [(i, i + 1) for i in range(1, count - 1, 2)]
    far = lax.ppermute(far_send, AXES, swaps + [(j, i) for i, j in swaps])
    swaps = [(i, i + 1) for i in range(0, count, 2)]
    near = lax.ppermute(near_send, AXES, swaps + [(j, i) for i, j in swaps])

    halved = across == 2
    parts = 2 if halved else 1
    wide = width // parts
    orders = [[0]]
    if halved:
        orders = [list(range(down))] * 2
        if (width // down) % 16 == 0:
            lines = [[o * inner + i for o in reversed(range(outer))] for i in range(inner)]
            orders = [sum(lines[1:] + lines[:1], []), sum(lines[1::-1] + lines[:1:-1], [])]
    image, edge, arm, part = pl.pallas_call(
        inner_kernel,
        out_shape=(
            jax.ShapeDtypeStruct((nrows, width), bf16),
            jax.ShapeDtypeStruct((2, tile, width), f32),
            jax.ShapeDtypeStruct((2, 2 * tile, tile), bf16),
            jax.ShapeDtypeStruct((parts, width, wide), f32),
        ),
        in_specs=[whole(pltpu.SMEM), whole(pltpu.SMEM), whole(), whole(), whole()],
        out_specs=(whole(pltpu.HBM), whole(), whole(), whole()),
        scratch_shapes=[
            pltpu.VMEM((nrows, width), bf16),
            pltpu.SemaphoreType.DMA((nblk // 6 + 1,)),
        ],
        compiler_params=pltpu.CompilerParams(vmem_limit_bytes=32 * 2**20),
        cost_estimate=pl.CostEstimate(
            flops=2 * nrows * width * (width + 12 * bsize),
            bytes_accessed=8 * 2**20,
            transcendentals=0,
        ),
        name="inner",
    )(
        block_cols.T,
        live_slots,
        jac_blocks,
        basis,
        accumulation.reshape(nblk // 2, tile),
    )

    rows, send = pl.pallas_call(
        functools.partial(edge_kernel, orders),
        out_shape=(
            jax.ShapeDtypeStruct((parts, 2 * tile, wide), bf16),
            jax.ShapeDtypeStruct((width, wide), bf16),
        ),
        in_specs=[whole()] * 6,
        out_specs=(whole(), whole()),
        compiler_params=pltpu.CompilerParams(vmem_limit_bytes=32 * 2**20),
        name="edges",
    )(far, near, edge, arm, basis, part)
    image, *keep = pl.pallas_call(
        functools.partial(keep_kernel, orders),
        out_shape=(
            jax.ShapeDtypeStruct((nrows, width), bf16),
            *([jax.ShapeDtypeStruct((width, wide), f32)] if halved else []),
        ),
        in_specs=[whole(), whole(), whole(), whole(pl.ANY)],
        out_specs=(whole(pl.ANY), *([whole()] if halved else [])),
        scratch_shapes=[pltpu.SemaphoreType.DMA((2 * parts,))],
        input_output_aliases={3: 0},
        compiler_params=pltpu.CompilerParams(vmem_limit_bytes=32 * 2**20),
        cost_estimate=pl.CostEstimate(
            flops=4 * tile * width * width, bytes_accessed=2**21, transcendentals=0
        ),
        name="kept_half",
    )(basis, rows, part, image)
    if halved:
        got = lax.ppermute(send, "col", [(0, 1), (1, 0)])
        total = (keep[0] + got.astype(f32)).astype(bf16)
        total = total.reshape(down, width // down, wide)
        groups = [[m * across + c for m in orders[c]] for c in range(across)]
        got = lax.all_to_all(total, AXES, 0, 0, axis_index_groups=groups, tiled=True)
    else:
        total = send.reshape(down, width // down, across, width // across)
        total = total.transpose(0, 2, 1, 3)
        total = total.reshape(count, width // down, width // across)
        got = lax.all_to_all(total, AXES, 0, 0, tiled=True)
    projected = jnp.sum(got.astype(f32), axis=0) * (1.0 / (nrows * count))
    return (image, projected)


def solution(mesh):
    rows, cols = mesh.devices.shape
    outer = 4 if rows % 4 == 0 else 1
    split = jax.sharding.Mesh(mesh.devices.reshape(outer, rows // outer, cols), AXES)
    return jax.shard_map(
        local,
        mesh=split,
        in_specs=(
            P(AXES, None),
            P(AXES, None, None, None),
            P(AXES, None),
            P(AXES),
            P(AXES),
        ),
        out_specs=(P(AXES, None), P(AXES[:2], "col")),
        check_vma=False,
    )
```

```python
import functools

import jax
import jax.numpy as jnp
from jax import lax
from jax.experimental import pallas as pl
from jax.experimental.pallas import tpu as pltpu
from jax.sharding import PartitionSpec as P

REACH = 2
AXES = ("outer", "inner", "col")
ROWS_DOT = (((0,), (0,)), ((), ()))


def strip_of(cols_ref, live_ref, jac_ref, acc_ref, first, pair):
    _, slots, bsize, _ = jac_ref.shape
    tile = 2 * bsize
    half = lax.broadcasted_iota(jnp.int32, (1, tile), 1) // bsize
    row = lax.broadcasted_iota(jnp.int32, (bsize, tile), 0)
    lane = lax.broadcasted_iota(jnp.int32, (bsize, tile), 1)
    weight = acc_ref[pair : pair + 1, :]
    halves = []
    for side in range(2):
        g = 2 * pair + side
        tiles = [None, jnp.where(lane == row + side * bsize, weight, 0.0), None]
        for s in range(slots):
            place = cols_ref[s, g] - (first + 2 * pair) + REACH
            place = jnp.where(s < live_ref[g], place, -1)
            block = jac_ref[g, s]
            wide = jnp.concatenate([block, block], axis=1).astype(jnp.float32)
            for t in range(3):
                here = jnp.where(half + 2 * t == place, 1.0, 0.0)
                term = wide * here
                tiles[t] = term if tiles[t] is None else tiles[t] + term
        halves.append(jnp.concatenate(tiles, axis=1))
    strip = jnp.concatenate(halves, axis=0)
    high = strip.astype(jnp.bfloat16)
    low = (strip - high.astype(jnp.float32)).astype(jnp.bfloat16)
    return jnp.concatenate([high, low], axis=0)


def gathered_rows(cols_ref, live_ref, jac_ref, basis_ref, first, g):
    nblk, slots, bsize, _ = jac_ref.shape
    lane = lax.broadcasted_iota(jnp.int32, (1, slots * bsize), 1)
    keep = jnp.where(lane < live_ref[g] * bsize, 1.0, 0.0).astype(jnp.bfloat16)
    blocks = jnp.concatenate([jac_ref[g, s] for s in range(slots)], axis=1) * keep
    rows = []
    for s in range(slots):
        at = jnp.clip(cols_ref[s, g] - first, 0, nblk - 1) * bsize
        rows.append(basis_ref[pl.ds(pl.multiple_of(at, bsize), bsize), :])
    rows = jnp.concatenate(rows, axis=0)
    return jnp.dot(blocks, rows, preferred_element_type=jnp.float32)


def apply_strip(strip, rows):
    both = jnp.dot(strip, rows, preferred_element_type=jnp.float32)
    half = strip.shape[0] // 2
    return both[:half] + both[half:]


def far_kernel(basis_hbm, far_ref, sems):
    tile = far_ref.shape[0]
    last = basis_hbm.shape[0] - tile
    odd = lax.rem(lax.axis_index(AXES), 2)
    count = sems.shape[0]
    size = tile // count
    copies = []
    for i in range(count):
        source = pl.ds(pl.multiple_of(odd * last + i * size, size), size)
        target = far_ref.at[pl.ds(i * size, size)]
        copies.append(pltpu.make_async_copy(basis_hbm.at[source], target, sems.at[i]))
        copies[i].start()
    for copy in copies:
        copy.wait()


def hand_on_kernel(rows_ref, out_ref):
    out_ref[...] = rows_ref[...]


def near_kernel(basis_ref, near_ref):
    tile = near_ref.shape[0]
    last = basis_ref.shape[0] - tile
    odd = lax.rem(lax.axis_index(AXES), 2)
    where = pl.ds(pl.multiple_of((1 - odd) * last, tile), tile)
    near_ref[...] = basis_ref[where, :]


def inner_kernel(
    cols_ref, live_ref, jac_ref, basis_ref, acc_ref,
    image_ref, edge_ref, arm_ref, part_ref, staged, sems,
):
    nblk, _, bsize, _ = jac_ref.shape
    nrows = basis_ref.shape[0]
    tile = 2 * bsize
    pairs = nblk // 2
    first = lax.axis_index(AXES) * nblk

    def project(start, stop):
        total = lax.dot_general(
            basis_ref[start:stop, :], staged[start:stop, :], ROWS_DOT,
            preferred_element_type=jnp.float32,
        )
        parts, _, wide = part_ref.shape
        return [total[:, i * wide : (i + 1) * wide] for i in range(parts)]

    def store(start, stop, at):
        where = pl.ds(start, stop - start)
        copy = pltpu.make_async_copy(staged.at[where], image_ref.at[where], sems.at[at])
        copy.start()
        return copy

    row = lax.broadcasted_iota(jnp.int32, (tile, tile), 0)
    lane = lax.broadcasted_iota(jnp.int32, (tile, tile), 1)
    middle = (pairs // 2) * tile
    stored = tile
    copies = []
    for pair in range(1, pairs - 1):
        start = pair * tile
        stop = start + tile
        weight = jnp.where(lane == row, acc_ref[pair : pair + 1, :], 0.0)
        weight = jnp.sum(weight, axis=1, keepdims=True)
        coupled = [
            gathered_rows(cols_ref, live_ref, jac_ref, basis_ref, first, 2 * pair + side)
            for side in range(2)
        ]
        own = basis_ref[start:stop, :].astype(jnp.float32)
        total = jnp.concatenate(coupled, axis=0) + weight * own
        staged[start:stop, :] = total.astype(jnp.bfloat16)
        if pair % 3 == 0 or pair == pairs - 2:
            copies.append(store(stored, stop, len(copies)))
            stored = stop
        if stop == middle:
            for i, half in enumerate(project(tile, middle)):
                part_ref[i] = half
    for side, pair in enumerate((0, pairs - 1)):
        strip = strip_of(cols_ref, live_ref, jac_ref, acc_ref, first, pair)
        if side == 0:
            edge_ref[0] = apply_strip(strip[:, tile:], basis_ref[: 2 * tile, :])
            arm_ref[0] = strip[:, :tile]
        else:
            edge_ref[1] = apply_strip(strip[:, : 2 * tile], basis_ref[nrows - 2 * tile :, :])
            arm_ref[1] = strip[:, 2 * tile :]
    for i, half in enumerate(project(middle, nrows - tile)):
        part_ref[i] += half
    for copy in copies:
        copy.wait()


def end_tiles(basis_ref, tile):
    nrows = basis_ref.shape[0]
    return jnp.concatenate([basis_ref[:tile, :], basis_ref[nrows - tile :, :]], axis=0)


def add_edges(part_ref, tiles, rows_ref, half):
    update = lax.dot_general(
        tiles, rows_ref[half], ROWS_DOT, preferred_element_type=jnp.float32
    )
    return part_ref[half] + update


def put_blocks(ref, value, orders, core):
    high = value.shape[0] // len(orders[0])
    blocks = [value[i * high : (i + 1) * high, :] for i in range(len(orders[0]))]
    for to, (first, second) in enumerate(zip(orders[0], orders[-1])):
        block = blocks[first]
        if first != second:
            block = jnp.where(core == 1, blocks[second], block)
        ref[to * high : (to + 1) * high, :] = block.astype(ref.dtype)


def leaving_half(parts):
    return 1 - lax.axis_index("col") if parts == 2 else 0


def edge_kernel(
    orders, far_ref, near_ref, edge_ref, arm_ref, basis_ref, part_ref, rows_ref, send_ref,
):
    tile = far_ref.shape[0]
    parts, _, wide = rows_ref.shape
    odd = lax.rem(lax.axis_index(AXES), 2) == 1
    near, far = near_ref[...], far_ref[...]
    halos = (jnp.where(odd, near, far), jnp.where(odd, far, near))
    for side in range(2):
        rows = edge_ref[side] + apply_strip(arm_ref[side], halos[side])
        rows = rows.astype(jnp.bfloat16)
        for i in range(parts):
            rows_ref[i, side * tile : (side + 1) * tile, :] = rows[:, i * wide : (i + 1) * wide]
    leaving = leaving_half(parts)
    send = add_edges(part_ref, end_tiles(basis_ref, tile), rows_ref, leaving)
    put_blocks(send_ref, send, orders, leaving)


def keep_kernel(orders, basis_ref, rows_ref, part_ref, _, image_ref, *rest):
    *keep_refs, sems = rest
    nrows = image_ref.shape[0]
    parts, rows, wide = rows_ref.shape
    tile = rows // 2
    copies = []
    for side, start in enumerate((0, nrows - tile)):
        for i in range(parts):
            source = rows_ref.at[i, pl.ds(side * tile, tile)]
            target = image_ref.at[pl.ds(start, tile), pl.ds(i * wide, wide)]
            copy = pltpu.make_async_copy(source, target, sems.at[side * parts + i])
            copy.start()
            copies.append(copy)
    for keep_ref in keep_refs:
        own = 1 - leaving_half(parts)
        keep = add_edges(part_ref, end_tiles(basis_ref, tile), rows_ref, own)
        put_blocks(keep_ref, keep, orders, own)
    for copy in copies:
        copy.wait()


def whole(memory_space=pltpu.VMEM):
    return pl.BlockSpec(memory_space=memory_space)


def local(basis, jac_blocks, block_cols, live_slots, accumulation):
    nrows, width = basis.shape
    nblk, slots, bsize, _ = jac_blocks.shape
    tile = 2 * bsize
    outer, inner, across = (lax.axis_size(axis) for axis in AXES)
    down = outer * inner
    count = down * across
    f32, bf16 = jnp.float32, jnp.bfloat16
    edge_shape = jax.ShapeDtypeStruct((tile, width), bf16)
    far_rows = pl.pallas_call(
        far_kernel,
        out_shape=edge_shape,
        in_specs=[whole(pltpu.HBM)],
        out_specs=whole(),
        scratch_shapes=[pltpu.SemaphoreType.DMA((4,))],
        compiler_params=pltpu.CompilerParams(vmem_limit_bytes=4 * 2**20),
        cost_estimate=pl.CostEstimate(flops=0, bytes_accessed=0, transcendentals=0),
        name="far_rows",
    )(pltpu.with_memory_space_constraint(basis, pltpu.HBM))
    far_send = pl.pallas_call(
        hand_on_kernel,
        out_shape=edge_shape,
        in_specs=[whole()],
        out_specs=whole(),
        compiler_params=pltpu.CompilerParams(vmem_limit_bytes=4 * 2**20),
        cost_estimate=pl.CostEstimate(
            flops=2 * nrows * width * width * slots, bytes_accessed=0, transcendentals=0
        ),
        name="hand_on",
    )(far_rows)
    near_send = pl.pallas_call(
        near_kernel,
        out_shape=edge_shape,
        in_specs=[whole()],
        out_specs=whole(),
        compiler_params=pltpu.CompilerParams(vmem_limit_bytes=4 * 2**20),
        name="near_rows",
    )(basis)
    swaps = [(i, i + 1) for i in range(1, count - 1, 2)]
    far = lax.ppermute(far_send, AXES, swaps + [(j, i) for i, j in swaps])
    swaps = [(i, i + 1) for i in range(0, count, 2)]
    near = lax.ppermute(near_send, AXES, swaps + [(j, i) for i, j in swaps])

    halved = across == 2
    parts = 2 if halved else 1
    wide = width // parts
    orders = [[0]]
    if halved:
        orders = [list(range(down))] * 2
        if (width // down) % 16 == 0:
            lines = [[o * inner + i for o in reversed(range(outer))] for i in range(inner)]
            orders = [sum(lines[:1] + lines[:0:-1], []), sum(lines, [])]
    image, edge, arm, part = pl.pallas_call(
        inner_kernel,
        out_shape=(
            jax.ShapeDtypeStruct((nrows, width), bf16),
            jax.ShapeDtypeStruct((2, tile, width), f32),
            jax.ShapeDtypeStruct((2, 2 * tile, tile), bf16),
            jax.ShapeDtypeStruct((parts, width, wide), f32),
        ),
        in_specs=[whole(pltpu.SMEM), whole(pltpu.SMEM), whole(), whole(), whole()],
        out_specs=(whole(pltpu.HBM), whole(), whole(), whole()),
        scratch_shapes=[
            pltpu.VMEM((nrows, width), bf16),
            pltpu.SemaphoreType.DMA((nblk // 6 + 1,)),
        ],
        compiler_params=pltpu.CompilerParams(vmem_limit_bytes=32 * 2**20),
        cost_estimate=pl.CostEstimate(
            flops=2 * nrows * width * (width + 12 * bsize),
            bytes_accessed=8 * 2**20,
            transcendentals=0,
        ),
        name="inner",
    )(
        block_cols.T,
        live_slots,
        jac_blocks,
        basis,
        accumulation.reshape(nblk // 2, tile),
    )

    rows, send = pl.pallas_call(
        functools.partial(edge_kernel, orders),
        out_shape=(
            jax.ShapeDtypeStruct((parts, 2 * tile, wide), bf16),
            jax.ShapeDtypeStruct((width, wide), bf16),
        ),
        in_specs=[whole()] * 6,
        out_specs=(whole(), whole()),
        compiler_params=pltpu.CompilerParams(vmem_limit_bytes=32 * 2**20),
        name="edges",
    )(far, near, edge, arm, basis, part)
    image, *keep = pl.pallas_call(
        functools.partial(keep_kernel, orders),
        out_shape=(
            jax.ShapeDtypeStruct((nrows, width), bf16),
            *([jax.ShapeDtypeStruct((width, wide), f32)] if halved else []),
        ),
        in_specs=[whole(), whole(), whole(), whole(pl.ANY)],
        out_specs=(whole(pl.ANY), *([whole()] if halved else [])),
        scratch_shapes=[pltpu.SemaphoreType.DMA((2 * parts,))],
        input_output_aliases={3: 0},
        compiler_params=pltpu.CompilerParams(vmem_limit_bytes=32 * 2**20),
        cost_estimate=pl.CostEstimate(
            flops=4 * tile * width * width, bytes_accessed=2**21, transcendentals=0
        ),
        name="kept_half",
    )(basis, rows, part, image)
    if halved:
        got = lax.ppermute(send, "col", [(0, 1), (1, 0)])
        total = (keep[0] + got.astype(f32)).astype(bf16)
        total = total.reshape(down, width // down, wide)
        groups = [[m * across + c for m in orders[c]] for c in range(across)]
        got = lax.all_to_all(total, AXES, 0, 0, axis_index_groups=groups, tiled=True)
    else:
        total = send.reshape(down, width // down, across, width // across)
        total = total.transpose(0, 2, 1, 3)
        total = total.reshape(count, width // down, width // across)
        got = lax.all_to_all(total, AXES, 0, 0, tiled=True)
    projected = jnp.sum(got.astype(f32), axis=0) * (1.0 / (nrows * count))
    return (image, projected)


def solution(mesh):
    rows, cols = mesh.devices.shape
    outer = 4 if rows % 4 == 0 else 1
    split = jax.sharding.Mesh(mesh.devices.reshape(outer, rows // outer, cols), AXES)
    return jax.shard_map(
        local,
        mesh=split,
        in_specs=(
            P(AXES, None),
            P(AXES, None, None, None),
            P(AXES, None),
            P(AXES),
            P(AXES),
        ),
        out_specs=(P(AXES, None), P(AXES[:2], "col")),
        check_vma=False,
    )
```

```python
import functools

import jax
import jax.numpy as jnp
from jax import lax
from jax.experimental import pallas as pl
from jax.experimental.pallas import tpu as pltpu
from jax.sharding import PartitionSpec as P

REACH = 2
AXES = ("outer", "inner", "col")
ROWS_DOT = (((0,), (0,)), ((), ()))


def strip_of(cols_ref, live_ref, jac_ref, acc_ref, first, pair):
    _, slots, bsize, _ = jac_ref.shape
    tile = 2 * bsize
    half = lax.broadcasted_iota(jnp.int32, (1, tile), 1) // bsize
    row = lax.broadcasted_iota(jnp.int32, (bsize, tile), 0)
    lane = lax.broadcasted_iota(jnp.int32, (bsize, tile), 1)
    weight = acc_ref[pair : pair + 1, :]
    halves = []
    for side in range(2):
        g = 2 * pair + side
        tiles = [None, jnp.where(lane == row + side * bsize, weight, 0.0), None]
        for s in range(slots):
            place = cols_ref[s, g] - (first + 2 * pair) + REACH
            place = jnp.where(s < live_ref[g], place, -1)
            block = jac_ref[g, s]
            wide = jnp.concatenate([block, block], axis=1).astype(jnp.float32)
            for t in range(3):
                here = jnp.where(half + 2 * t == place, 1.0, 0.0)
                term = wide * here
                tiles[t] = term if tiles[t] is None else tiles[t] + term
        halves.append(jnp.concatenate(tiles, axis=1))
    strip = jnp.concatenate(halves, axis=0)
    high = strip.astype(jnp.bfloat16)
    low = (strip - high.astype(jnp.float32)).astype(jnp.bfloat16)
    return jnp.concatenate([high, low], axis=0)


def gathered_rows(cols_ref, live_ref, jac_ref, basis_ref, first, g):
    nblk, slots, bsize, _ = jac_ref.shape
    lane = lax.broadcasted_iota(jnp.int32, (1, slots * bsize), 1)
    keep = jnp.where(lane < live_ref[g] * bsize, 1.0, 0.0).astype(jnp.bfloat16)
    blocks = jnp.concatenate([jac_ref[g, s] for s in range(slots)], axis=1) * keep
    rows = []
    for s in range(slots):
        at = jnp.clip(cols_ref[s, g] - first, 0, nblk - 1) * bsize
        rows.append(basis_ref[pl.ds(pl.multiple_of(at, bsize), bsize), :])
    rows = jnp.concatenate(rows, axis=0)
    return jnp.dot(blocks, rows, preferred_element_type=jnp.float32)


def apply_strip(strip, rows):
    both = jnp.dot(strip, rows, preferred_element_type=jnp.float32)
    half = strip.shape[0] // 2
    return both[:half] + both[half:]


def far_kernel(basis_hbm, far_ref, sems):
    tile = far_ref.shape[0]
    last = basis_hbm.shape[0] - tile
    odd = lax.rem(lax.axis_index(AXES), 2)
    count = sems.shape[0]
    size = tile // count
    copies = []
    for i in range(count):
        source = pl.ds(pl.multiple_of(odd * last + i * size, size), size)
        target = far_ref.at[pl.ds(i * size, size)]
        copies.append(pltpu.make_async_copy(basis_hbm.at[source], target, sems.at[i]))
        copies[i].start()
    for copy in copies:
        copy.wait()


def hand_on_kernel(rows_ref, out_ref):
    out_ref[...] = rows_ref[...]


def near_kernel(basis_ref, near_ref):
    tile = near_ref.shape[0]
    last = basis_ref.shape[0] - tile
    odd = lax.rem(lax.axis_index(AXES), 2)
    where = pl.ds(pl.multiple_of((1 - odd) * last, tile), tile)
    near_ref[...] = basis_ref[where, :]


def inner_kernel(
    cols_ref, live_ref, jac_ref, basis_ref, acc_ref,
    image_ref, edge_ref, arm_ref, part_ref, staged, sems,
):
    nblk, _, bsize, _ = jac_ref.shape
    nrows = basis_ref.shape[0]
    tile = 2 * bsize
    pairs = nblk // 2
    first = lax.axis_index(AXES) * nblk

    def project(start, stop):
        total = lax.dot_general(
            basis_ref[start:stop, :], staged[start:stop, :], ROWS_DOT,
            preferred_element_type=jnp.float32,
        )
        parts, _, wide = part_ref.shape
        return [total[:, i * wide : (i + 1) * wide] for i in range(parts)]

    def store(start, stop, at):
        where = pl.ds(start, stop - start)
        copy = pltpu.make_async_copy(staged.at[where], image_ref.at[where], sems.at[at])
        copy.start()
        return copy

    row = lax.broadcasted_iota(jnp.int32, (tile, tile), 0)
    lane = lax.broadcasted_iota(jnp.int32, (tile, tile), 1)
    middle = (pairs // 2) * tile
    stored = tile
    copies = []
    for pair in range(1, pairs - 1):
        start = pair * tile
        stop = start + tile
        weight = jnp.where(lane == row, acc_ref[pair : pair + 1, :], 0.0)
        weight = jnp.sum(weight, axis=1, keepdims=True)
        coupled = [
            gathered_rows(cols_ref, live_ref, jac_ref, basis_ref, first, 2 * pair + side)
            for side in range(2)
        ]
        own = basis_ref[start:stop, :].astype(jnp.float32)
        total = jnp.concatenate(coupled, axis=0) + weight * own
        staged[start:stop, :] = total.astype(jnp.bfloat16)
        if pair % 3 == 0 or pair == pairs - 2:
            copies.append(store(stored, stop, len(copies)))
            stored = stop
        if stop == middle:
            for i, half in enumerate(project(tile, middle)):
                part_ref[i] = half
    for side, pair in enumerate((0, pairs - 1)):
        strip = strip_of(cols_ref, live_ref, jac_ref, acc_ref, first, pair)
        if side == 0:
            edge_ref[0] = apply_strip(strip[:, tile:], basis_ref[: 2 * tile, :])
            arm_ref[0] = strip[:, :tile]
        else:
            edge_ref[1] = apply_strip(strip[:, : 2 * tile], basis_ref[nrows - 2 * tile :, :])
            arm_ref[1] = strip[:, 2 * tile :]
    for i, half in enumerate(project(middle, nrows - tile)):
        part_ref[i] += half
    for copy in copies:
        copy.wait()


def end_tiles(basis_ref, tile):
    nrows = basis_ref.shape[0]
    return jnp.concatenate([basis_ref[:tile, :], basis_ref[nrows - tile :, :]], axis=0)


def add_edges(part_ref, tiles, rows_ref, half):
    update = lax.dot_general(
        tiles, rows_ref[half], ROWS_DOT, preferred_element_type=jnp.float32
    )
    return part_ref[half] + update


def put_blocks(ref, value, orders, core):
    high = value.shape[0] // len(orders[0])
    blocks = [value[i * high : (i + 1) * high, :] for i in range(len(orders[0]))]
    for to, (first, second) in enumerate(zip(orders[0], orders[-1])):
        block = blocks[first]
        if first != second:
            block = jnp.where(core == 1, blocks[second], block)
        ref[to * high : (to + 1) * high, :] = block.astype(ref.dtype)


def leaving_half(parts):
    return 1 - lax.axis_index("col") if parts == 2 else 0


def edge_kernel(
    orders, far_ref, near_ref, edge_ref, arm_ref, basis_ref, part_ref, rows_ref, send_ref,
):
    tile = far_ref.shape[0]
    parts, _, wide = rows_ref.shape
    odd = lax.rem(lax.axis_index(AXES), 2) == 1
    near, far = near_ref[...], far_ref[...]
    halos = (jnp.where(odd, near, far), jnp.where(odd, far, near))
    for side in range(2):
        rows = edge_ref[side] + apply_strip(arm_ref[side], halos[side])
        rows = rows.astype(jnp.bfloat16)
        for i in range(parts):
            rows_ref[i, side * tile : (side + 1) * tile, :] = rows[:, i * wide : (i + 1) * wide]
    leaving = leaving_half(parts)
    send = add_edges(part_ref, end_tiles(basis_ref, tile), rows_ref, leaving)
    put_blocks(send_ref, send, orders, leaving)


def keep_kernel(orders, basis_ref, rows_ref, part_ref, _, image_ref, *rest):
    *keep_refs, sems = rest
    nrows = image_ref.shape[0]
    parts, rows, wide = rows_ref.shape
    tile = rows // 2
    copies = []
    for side, start in enumerate((0, nrows - tile)):
        for i in range(parts):
            source = rows_ref.at[i, pl.ds(side * tile, tile)]
            target = image_ref.at[pl.ds(start, tile), pl.ds(i * wide, wide)]
            copy = pltpu.make_async_copy(source, target, sems.at[side * parts + i])
            copy.start()
            copies.append(copy)
    for keep_ref in keep_refs:
        own = 1 - leaving_half(parts)
        keep = add_edges(part_ref, end_tiles(basis_ref, tile), rows_ref, own)
        put_blocks(keep_ref, keep, orders, own)
    for copy in copies:
        copy.wait()


def whole(memory_space=pltpu.VMEM):
    return pl.BlockSpec(memory_space=memory_space)


def local(basis, jac_blocks, block_cols, live_slots, accumulation):
    nrows, width = basis.shape
    nblk, slots, bsize, _ = jac_blocks.shape
    tile = 2 * bsize
    outer, inner, across = (lax.axis_size(axis) for axis in AXES)
    down = outer * inner
    count = down * across
    f32, bf16 = jnp.float32, jnp.bfloat16
    edge_shape = jax.ShapeDtypeStruct((tile, width), bf16)
    far_rows = pl.pallas_call(
        far_kernel,
        out_shape=edge_shape,
        in_specs=[whole(pltpu.HBM)],
        out_specs=whole(),
        scratch_shapes=[pltpu.SemaphoreType.DMA((4,))],
        compiler_params=pltpu.CompilerParams(vmem_limit_bytes=4 * 2**20),
        cost_estimate=pl.CostEstimate(flops=0, bytes_accessed=0, transcendentals=0),
        name="far_rows",
    )(pltpu.with_memory_space_constraint(basis, pltpu.HBM))
    far_send = pl.pallas_call(
        hand_on_kernel,
        out_shape=edge_shape,
        in_specs=[whole()],
        out_specs=whole(),
        compiler_params=pltpu.CompilerParams(vmem_limit_bytes=4 * 2**20),
        cost_estimate=pl.CostEstimate(
            flops=2 * nrows * width * width * slots, bytes_accessed=0, transcendentals=0
        ),
        name="hand_on",
    )(far_rows)
    near_send = pl.pallas_call(
        near_kernel,
        out_shape=edge_shape,
        in_specs=[whole()],
        out_specs=whole(),
        compiler_params=pltpu.CompilerParams(vmem_limit_bytes=4 * 2**20),
        name="near_rows",
    )(basis)
    swaps = [(i, i + 1) for i in range(1, count - 1, 2)]
    far = lax.ppermute(far_send, AXES, swaps + [(j, i) for i, j in swaps])
    swaps = [(i, i + 1) for i in range(0, count, 2)]
    near = lax.ppermute(near_send, AXES, swaps + [(j, i) for i, j in swaps])

    halved = across == 2
    parts = 2 if halved else 1
    wide = width // parts
    orders = [[0]]
    if halved:
        orders = [list(range(down))] * 2
        if (width // down) % 16 == 0:
            lines = [[o * inner + i for o in reversed(range(outer))] for i in range(inner)]
            orders = [sum(lines, []), sum(lines[:1] + lines[:0:-1], [])]
    image, edge, arm, part = pl.pallas_call(
        inner_kernel,
        out_shape=(
            jax.ShapeDtypeStruct((nrows, width), bf16),
            jax.ShapeDtypeStruct((2, tile, width), f32),
            jax.ShapeDtypeStruct((2, 2 * tile, tile), bf16),
            jax.ShapeDtypeStruct((parts, width, wide), f32),
        ),
        in_specs=[whole(pltpu.SMEM), whole(pltpu.SMEM), whole(), whole(), whole()],
        out_specs=(whole(pltpu.HBM), whole(), whole(), whole()),
        scratch_shapes=[
            pltpu.VMEM((nrows, width), bf16),
            pltpu.SemaphoreType.DMA((nblk // 6 + 1,)),
        ],
        compiler_params=pltpu.CompilerParams(vmem_limit_bytes=32 * 2**20),
        cost_estimate=pl.CostEstimate(
            flops=2 * nrows * width * (width + 12 * bsize),
            bytes_accessed=8 * 2**20,
            transcendentals=0,
        ),
        name="inner",
    )(
        block_cols.T,
        live_slots,
        jac_blocks,
        basis,
        accumulation.reshape(nblk // 2, tile),
    )

    rows, send = pl.pallas_call(
        functools.partial(edge_kernel, orders),
        out_shape=(
            jax.ShapeDtypeStruct((parts, 2 * tile, wide), bf16),
            jax.ShapeDtypeStruct((width, wide), bf16),
        ),
        in_specs=[whole()] * 6,
        out_specs=(whole(), whole()),
        compiler_params=pltpu.CompilerParams(vmem_limit_bytes=32 * 2**20),
        name="edges",
    )(far, near, edge, arm, basis, part)
    image, *keep = pl.pallas_call(
        functools.partial(keep_kernel, orders),
        out_shape=(
            jax.ShapeDtypeStruct((nrows, width), bf16),
            *([jax.ShapeDtypeStruct((width, wide), f32)] if halved else []),
        ),
        in_specs=[whole(), whole(), whole(), whole(pl.ANY)],
        out_specs=(whole(pl.ANY), *([whole()] if halved else [])),
        scratch_shapes=[pltpu.SemaphoreType.DMA((2 * parts,))],
        input_output_aliases={3: 0},
        compiler_params=pltpu.CompilerParams(vmem_limit_bytes=32 * 2**20),
        cost_estimate=pl.CostEstimate(
            flops=4 * tile * width * width, bytes_accessed=2**21, transcendentals=0
        ),
        name="kept_half",
    )(basis, rows, part, image)
    scale = 1.0 / (nrows * count)
    if halved:
        got = lax.ppermute(send, "col", [(0, 1), (1, 0)])
        total = ((keep[0] + got.astype(f32)) * scale).astype(bf16)
        total = total.reshape(down, width // down, wide)
        groups = [[m * across + c for m in orders[c]] for c in range(across)]
        got = lax.all_to_all(total, AXES, 0, 0, axis_index_groups=groups, tiled=True)
    else:
        total = (send.astype(f32) * scale).astype(bf16).reshape(down, width // down, across, width // across)
        total = total.transpose(0, 2, 1, 3)
        total = total.reshape(count, width // down, width // across)
        got = lax.all_to_all(total, AXES, 0, 0, tiled=True)
    projected = jnp.sum(got.astype(f32), axis=0)
    return (image, projected)


def solution(mesh):
    rows, cols = mesh.devices.shape
    outer = 4 if rows % 4 == 0 else 1
    split = jax.sharding.Mesh(mesh.devices.reshape(outer, rows // outer, cols), AXES)
    return jax.shard_map(
        local,
        mesh=split,
        in_specs=(
            P(AXES, None),
            P(AXES, None, None, None),
            P(AXES, None),
            P(AXES),
            P(AXES),
        ),
        out_specs=(P(AXES, None), P(AXES[:2], "col")),
        check_vma=False,
    )
```

```python
import functools

import jax
import jax.numpy as jnp
from jax import lax
from jax.experimental import pallas as pl
from jax.experimental.pallas import tpu as pltpu
from jax.sharding import PartitionSpec as P

REACH = 2
AXES = ("outer", "inner", "col")
ROWS_DOT = (((0,), (0,)), ((), ()))


def strip_of(cols_ref, live_ref, jac_ref, acc_ref, first, pair):
    _, slots, bsize, _ = jac_ref.shape
    tile = 2 * bsize
    half = lax.broadcasted_iota(jnp.int32, (1, tile), 1) // bsize
    row = lax.broadcasted_iota(jnp.int32, (bsize, tile), 0)
    lane = lax.broadcasted_iota(jnp.int32, (bsize, tile), 1)
    weight = acc_ref[pair : pair + 1, :]
    halves = []
    for side in range(2):
        g = 2 * pair + side
        tiles = [None, jnp.where(lane == row + side * bsize, weight, 0.0), None]
        for s in range(slots):
            place = cols_ref[s, g] - (first + 2 * pair) + REACH
            place = jnp.where(s < live_ref[g], place, -1)
            block = jac_ref[g, s]
            wide = jnp.concatenate([block, block], axis=1).astype(jnp.float32)
            for t in range(3):
                here = jnp.where(half + 2 * t == place, 1.0, 0.0)
                term = wide * here
                tiles[t] = term if tiles[t] is None else tiles[t] + term
        halves.append(jnp.concatenate(tiles, axis=1))
    strip = jnp.concatenate(halves, axis=0)
    high = strip.astype(jnp.bfloat16)
    low = (strip - high.astype(jnp.float32)).astype(jnp.bfloat16)
    return jnp.concatenate([high, low], axis=0)


def gathered_rows(cols_ref, live_ref, jac_ref, basis_ref, first, g):
    nblk, slots, bsize, _ = jac_ref.shape
    lane = lax.broadcasted_iota(jnp.int32, (1, slots * bsize), 1)
    keep = jnp.where(lane < live_ref[g] * bsize, 1.0, 0.0).astype(jnp.bfloat16)
    blocks = jnp.concatenate([jac_ref[g, s] for s in range(slots)], axis=1) * keep
    rows = []
    for s in range(slots):
        at = jnp.clip(cols_ref[s, g] - first, 0, nblk - 1) * bsize
        rows.append(basis_ref[pl.ds(pl.multiple_of(at, bsize), bsize), :])
    rows = jnp.concatenate(rows, axis=0)
    return jnp.dot(blocks, rows, preferred_element_type=jnp.float32)


def apply_strip(strip, rows):
    both = jnp.dot(strip, rows, preferred_element_type=jnp.float32)
    half = strip.shape[0] // 2
    return both[:half] + both[half:]


def far_kernel(basis_hbm, far_ref, sems):
    tile = far_ref.shape[0]
    last = basis_hbm.shape[0] - tile
    odd = lax.rem(lax.axis_index(AXES), 2)
    count = sems.shape[0]
    size = tile // count
    copies = []
    for i in range(count):
        source = pl.ds(pl.multiple_of(odd * last + i * size, size), size)
        target = far_ref.at[pl.ds(i * size, size)]
        copies.append(pltpu.make_async_copy(basis_hbm.at[source], target, sems.at[i]))
        copies[i].start()
    for copy in copies:
        copy.wait()


def hand_on_kernel(rows_ref, out_ref):
    out_ref[...] = rows_ref[...]


def near_kernel(basis_ref, near_ref):
    tile = near_ref.shape[0]
    last = basis_ref.shape[0] - tile
    odd = lax.rem(lax.axis_index(AXES), 2)
    where = pl.ds(pl.multiple_of((1 - odd) * last, tile), tile)
    near_ref[...] = basis_ref[where, :]


def inner_kernel(
    cols_ref, live_ref, jac_ref, basis_ref, acc_ref,
    image_ref, edge_ref, arm_ref, part_ref, staged, sems,
):
    nblk, _, bsize, _ = jac_ref.shape
    nrows = basis_ref.shape[0]
    tile = 2 * bsize
    pairs = nblk // 2
    first = lax.axis_index(AXES) * nblk

    def project(start, stop):
        total = lax.dot_general(
            basis_ref[start:stop, :], staged[start:stop, :], ROWS_DOT,
            preferred_element_type=jnp.float32,
        )
        parts, _, wide = part_ref.shape
        return [total[:, i * wide : (i + 1) * wide] for i in range(parts)]

    def store(start, stop, at):
        where = pl.ds(start, stop - start)
        copy = pltpu.make_async_copy(staged.at[where], image_ref.at[where], sems.at[at])
        copy.start()
        return copy

    row = lax.broadcasted_iota(jnp.int32, (tile, tile), 0)
    lane = lax.broadcasted_iota(jnp.int32, (tile, tile), 1)
    middle = (pairs // 2) * tile
    stored = tile
    copies = []
    for pair in range(1, pairs - 1):
        start = pair * tile
        stop = start + tile
        weight = jnp.where(lane == row, acc_ref[pair : pair + 1, :], 0.0)
        weight = jnp.sum(weight, axis=1, keepdims=True)
        coupled = [
            gathered_rows(cols_ref, live_ref, jac_ref, basis_ref, first, 2 * pair + side)
            for side in range(2)
        ]
        own = basis_ref[start:stop, :].astype(jnp.float32)
        total = jnp.concatenate(coupled, axis=0) + weight * own
        staged[start:stop, :] = total.astype(jnp.bfloat16)
        if pair % 3 == 0 or pair == pairs - 2:
            copies.append(store(stored, stop, len(copies)))
            stored = stop
        if stop == middle:
            for i, half in enumerate(project(tile, middle)):
                part_ref[i] = half
    for side, pair in enumerate((0, pairs - 1)):
        strip = strip_of(cols_ref, live_ref, jac_ref, acc_ref, first, pair)
        if side == 0:
            edge_ref[0] = apply_strip(strip[:, tile:], basis_ref[: 2 * tile, :])
            arm_ref[0] = strip[:, :tile]
        else:
            edge_ref[1] = apply_strip(strip[:, : 2 * tile], basis_ref[nrows - 2 * tile :, :])
            arm_ref[1] = strip[:, 2 * tile :]
    for i, half in enumerate(project(middle, nrows - tile)):
        part_ref[i] += half
    for copy in copies:
        copy.wait()


def end_tiles(basis_ref, tile):
    nrows = basis_ref.shape[0]
    return jnp.concatenate([basis_ref[:tile, :], basis_ref[nrows - tile :, :]], axis=0)


def add_edges(part_ref, tiles, rows_ref, half):
    update = lax.dot_general(
        tiles, rows_ref[half], ROWS_DOT, preferred_element_type=jnp.float32
    )
    return part_ref[half] + update


def put_blocks(ref, value, orders, core):
    high = value.shape[0] // len(orders[0])
    blocks = [value[i * high : (i + 1) * high, :] for i in range(len(orders[0]))]
    for to, (first, second) in enumerate(zip(orders[0], orders[-1])):
        block = blocks[first]
        if first != second:
            block = jnp.where(core == 1, blocks[second], block)
        ref[to * high : (to + 1) * high, :] = block.astype(ref.dtype)


def leaving_half(parts):
    return 1 - lax.axis_index("col") if parts == 2 else 0


def edge_kernel(
    orders, far_ref, near_ref, edge_ref, arm_ref, basis_ref, part_ref, rows_ref, send_ref,
):
    tile = far_ref.shape[0]
    parts, _, wide = rows_ref.shape
    odd = lax.rem(lax.axis_index(AXES), 2) == 1
    near, far = near_ref[...], far_ref[...]
    halos = (jnp.where(odd, near, far), jnp.where(odd, far, near))
    for side in range(2):
        rows = edge_ref[side] + apply_strip(arm_ref[side], halos[side])
        rows = rows.astype(jnp.bfloat16)
        for i in range(parts):
            rows_ref[i, side * tile : (side + 1) * tile, :] = rows[:, i * wide : (i + 1) * wide]
    leaving = leaving_half(parts)
    send = add_edges(part_ref, end_tiles(basis_ref, tile), rows_ref, leaving)
    put_blocks(send_ref, send, orders, leaving)


def keep_kernel(orders, basis_ref, rows_ref, part_ref, _, image_ref, *rest):
    *keep_refs, sems = rest
    nrows = image_ref.shape[0]
    parts, rows, wide = rows_ref.shape
    tile = rows // 2
    copies = []
    for side, start in enumerate((0, nrows - tile)):
        for i in range(parts):
            source = rows_ref.at[i, pl.ds(side * tile, tile)]
            target = image_ref.at[pl.ds(start, tile), pl.ds(i * wide, wide)]
            copy = pltpu.make_async_copy(source, target, sems.at[side * parts + i])
            copy.start()
            copies.append(copy)
    for keep_ref in keep_refs:
        own = 1 - leaving_half(parts)
        keep = add_edges(part_ref, end_tiles(basis_ref, tile), rows_ref, own)
        put_blocks(keep_ref, keep, orders, own)
    for copy in copies:
        copy.wait()


def whole(memory_space=pltpu.VMEM):
    return pl.BlockSpec(memory_space=memory_space)


def local(basis, jac_blocks, block_cols, live_slots, accumulation):
    nrows, width = basis.shape
    nblk, slots, bsize, _ = jac_blocks.shape
    tile = 2 * bsize
    outer, inner, across = (lax.axis_size(axis) for axis in AXES)
    down = outer * inner
    count = down * across
    f32, bf16 = jnp.float32, jnp.bfloat16
    edge_shape = jax.ShapeDtypeStruct((tile, width), bf16)
    far_rows = pl.pallas_call(
        far_kernel,
        out_shape=edge_shape,
        in_specs=[whole(pltpu.HBM)],
        out_specs=whole(),
        scratch_shapes=[pltpu.SemaphoreType.DMA((4,))],
        compiler_params=pltpu.CompilerParams(vmem_limit_bytes=4 * 2**20),
        cost_estimate=pl.CostEstimate(flops=0, bytes_accessed=0, transcendentals=0),
        name="far_rows",
    )(pltpu.with_memory_space_constraint(basis, pltpu.HBM))
    far_send = pl.pallas_call(
        hand_on_kernel,
        out_shape=edge_shape,
        in_specs=[whole()],
        out_specs=whole(),
        compiler_params=pltpu.CompilerParams(vmem_limit_bytes=4 * 2**20),
        cost_estimate=pl.CostEstimate(
            flops=2 * nrows * width * width * slots, bytes_accessed=0, transcendentals=0
        ),
        name="hand_on",
    )(far_rows)
    near_send = pl.pallas_call(
        near_kernel,
        out_shape=edge_shape,
        in_specs=[whole()],
        out_specs=whole(),
        compiler_params=pltpu.CompilerParams(vmem_limit_bytes=4 * 2**20),
        name="near_rows",
    )(basis)
    swaps = [(i, i + 1) for i in range(1, count - 1, 2)]
    far = lax.ppermute(far_send, AXES, swaps + [(j, i) for i, j in swaps])
    swaps = [(i, i + 1) for i in range(0, count, 2)]
    near = lax.ppermute(near_send, AXES, swaps + [(j, i) for i, j in swaps])

    halved = across == 2
    parts = 2 if halved else 1
    wide = width // parts
    orders = [[0]]
    if halved:
        orders = [list(range(down))] * 2
        if (width // down) % 16 == 0:
            lines = [[o * inner + i for o in reversed(range(outer))] for i in range(inner)]
            orders = [sum(lines, [])] * 2
    image, edge, arm, part = pl.pallas_call(
        inner_kernel,
        out_shape=(
            jax.ShapeDtypeStruct((nrows, width), bf16),
            jax.ShapeDtypeStruct((2, tile, width), f32),
            jax.ShapeDtypeStruct((2, 2 * tile, tile), bf16),
            jax.ShapeDtypeStruct((parts, width, wide), f32),
        ),
        in_specs=[whole(pltpu.SMEM), whole(pltpu.SMEM), whole(), whole(), whole()],
        out_specs=(whole(pltpu.HBM), whole(), whole(), whole()),
        scratch_shapes=[
            pltpu.VMEM((nrows, width), bf16),
            pltpu.SemaphoreType.DMA((nblk // 6 + 1,)),
        ],
        compiler_params=pltpu.CompilerParams(vmem_limit_bytes=32 * 2**20),
        cost_estimate=pl.CostEstimate(
            flops=2 * nrows * width * (width + 12 * bsize),
            bytes_accessed=8 * 2**20,
            transcendentals=0,
        ),
        name="inner",
    )(
        block_cols.T,
        live_slots,
        jac_blocks,
        basis,
        accumulation.reshape(nblk // 2, tile),
    )

    rows, send = pl.pallas_call(
        functools.partial(edge_kernel, orders),
        out_shape=(
            jax.ShapeDtypeStruct((parts, 2 * tile, wide), bf16),
            jax.ShapeDtypeStruct((width, wide), bf16),
        ),
        in_specs=[whole()] * 6,
        out_specs=(whole(), whole()),
        compiler_params=pltpu.CompilerParams(vmem_limit_bytes=32 * 2**20),
        name="edges",
    )(far, near, edge, arm, basis, part)
    image, *keep = pl.pallas_call(
        functools.partial(keep_kernel, orders),
        out_shape=(
            jax.ShapeDtypeStruct((nrows, width), bf16),
            *([jax.ShapeDtypeStruct((width, wide), f32)] if halved else []),
        ),
        in_specs=[whole(), whole(), whole(), whole(pl.ANY)],
        out_specs=(whole(pl.ANY), *([whole()] if halved else [])),
        scratch_shapes=[pltpu.SemaphoreType.DMA((2 * parts,))],
        input_output_aliases={3: 0},
        compiler_params=pltpu.CompilerParams(vmem_limit_bytes=32 * 2**20),
        cost_estimate=pl.CostEstimate(
            flops=4 * tile * width * width, bytes_accessed=2**21, transcendentals=0
        ),
        name="kept_half",
    )(basis, rows, part, image)
    scale = 1.0 / (nrows * count)
    if halved:
        got = lax.ppermute(send, "col", [(0, 1), (1, 0)])
        total = ((keep[0] + got.astype(f32)) * scale).astype(bf16)
        total = total.reshape(down, width // down, wide)
        groups = [[m * across + c for m in orders[c]] for c in range(across)]
        got = lax.all_to_all(total, AXES, 0, 0, axis_index_groups=groups, tiled=True)
    else:
        total = (send.astype(f32) * scale).astype(bf16).reshape(down, width // down, across, width // across)
        total = total.transpose(0, 2, 1, 3)
        total = total.reshape(count, width // down, width // across)
        got = lax.all_to_all(total, AXES, 0, 0, tiled=True)
    projected = jnp.sum(got.astype(f32), axis=0)
    return (image, projected)


def solution(mesh):
    rows, cols = mesh.devices.shape
    outer = 4 if rows % 4 == 0 else 1
    split = jax.sharding.Mesh(mesh.devices.reshape(outer, rows // outer, cols), AXES)
    return jax.shard_map(
        local,
        mesh=split,
        in_specs=(
            P(AXES, None),
            P(AXES, None, None, None),
            P(AXES, None),
            P(AXES),
            P(AXES),
        ),
        out_specs=(P(AXES, None), P(AXES[:2], "col")),
        check_vma=False,
    )
```
